32 devices in a mesh: tm: 16 (over z, y, core), lat: 2 (over x).
Axes of the slice: x: 2, y: 2, z: 4, core: 2. Of those that a mesh axis runs over, the one named last changes fastest.
Arguments:
- fields: bfloat16 [32, 720, 1440], P('tm', 'lat'), may hold values from -6 to 6
- legendre: bfloat16 [720, 8192], P('lat'), may hold values from -0.21875 to 0.21875
- order_table: int32 [3, 16384], replicated, may hold values from 0 to 720, as said below
- window_start: int32 [1], replicated, may hold values from 0 to 8192
- ridge: float32 [1], replicated, may hold values from 0.3 to 1
Outputs:
- factored: float32 [8192, 8192], P('tm', 'lat')
The draws below stay inside these ranges and needn't reach their ends.
Inputs may be any that keep to these rules, and one draw needn't show every extreme that they name: `order_table`: row 0 holds each entry's degree, row 1 its order, which is at most the degree and below 720, row 2 is 0 for a cosine and 1 for a sine part, and is 1 only where the order is positive.
All inputs are finite; a program needn't handle non-finite values.
Results may differ from the reference program's by a relative error of at most 0.0048.
Values may be sent and summed in bfloat16 or wider, within the bound.
No kernel may reach another device: no remote copies, remote signals or barrier semaphores. Data moves between devices by JAX's collectives and lax.ppermute only.
A program may use at most 64 MiB of HBM per device.

```python
import math
import jax
import jax.numpy as jnp
from jax import lax

T_DEV = 2
NLAT = 720
NLON = 1440
MORD = 720
LMAX = 720
K = 8192
PANEL = 512
NT = 32
TAB = 16384
N_TM = 16


def draw_order_table(key, part):
    key_order, key_degree, key_sine, key_spot = jax.random.split(jax.random.fold_in(key, 11), 4)
    position = jnp.arange(TAB, dtype=jnp.int32)
    spot_index = jax.random.randint(key_spot, (), 0, TAB)
    order_row = jax.random.randint(key_order, (TAB,), 0, MORD)
    order_row = jnp.where(position == spot_index, 0, order_row)
    extra = jax.random.randint(key_degree, (TAB,), 0, 1 << 20) % (LMAX + 1 - order_row)
    degree_row = jnp.where(position == spot_index, LMAX, order_row + extra)
    sine_row = jax.random.randint(key_sine, (TAB,), 0, 2) * (order_row > 0).astype(jnp.int32)
    return jnp.stack([degree_row, order_row, sine_row]).astype(jnp.int32)


def shard_levels(rng, extent, cuts, smallest, largest):
    loudness, own = 1.0, jax.random.fold_in(rng, 6)
    for dim, shards_of in cuts:
        steps = jnp.exp(jax.random.uniform(jax.random.fold_in(own, dim), (shards_of,), jnp.float32, smallest / len(cuts), largest / len(cuts)))
        loudness = loudness * jnp.repeat(steps, extent[dim] // shards_of).reshape([-1 if axis == dim else 1 for axis in range(len(extent))])
    return loudness


def scatter_about(stream_key, dims, deviation, most, shards=(), kind=jnp.bfloat16):
    values = jax.random.normal(stream_key, dims, jnp.float32) * deviation
    if len(shards) > 0:
        values = shard_levels(stream_key, dims, shards, -0.22, 0.18) * values
    return jnp.clip(values, min=-most, max=most).astype(kind)


def setup_inputs(seed: int = 0) -> dict:
    keys = jax.random.split(jax.random.key(seed), 6)
    fields = scatter_about(keys[0], (NT, NLAT, NLON), 1.0, 6.0, ((0, 16), (1, 2)))
    legendre = scatter_about(keys[1], (NLAT, K), NLAT ** -0.5, 0.21875, ((0, 2),))
    order_table = draw_order_table(jax.random.fold_in(keys[5], 71), 0)
    window_start = jax.random.randint(keys[3], (1,), 0, TAB - K + 1).astype(jnp.int32)
    ridge = jnp.clip(jnp.exp(jax.random.uniform(keys[4], (1,), jnp.float32, math.log(0.3), math.log(1.0))), 0.3, 1.0)
    return {"fields": fields, "legendre": legendre, "order_table": order_table, "window_start": window_start, "ridge": ridge}


def make_basis(nlon):
    half = nlon // 2
    longitude = jnp.arange(nlon, dtype=jnp.int32)[:, None]
    column = jnp.arange(nlon, dtype=jnp.int32)[None, :]
    freq = column % half
    phase = (freq * longitude % nlon).astype(jnp.float32) * (2.0 * math.pi / nlon)
    return jnp.where(column < half, jnp.cos(phase), jnp.sin(phase)).astype(jnp.bfloat16)

def legendre_contract(spectra, legendre, column):
    kcoef = legendre.shape[1]
    width = kcoef // 8

    def one_part(number):
        start = (number * width).astype(jnp.int32)
        chosen_cols = lax.dynamic_slice_in_dim(column, start, width, 0)
        weights = lax.dynamic_slice_in_dim(legendre, start, width, 1).astype(jnp.float32)
        chosen = jnp.take(spectra, chosen_cols, axis=2)
        return jnp.einsum('tlk,lk->tk', chosen, weights)
    parts_out = lax.map(one_part, jnp.arange(8, dtype=jnp.int32))
    return jnp.transpose(parts_out, (1, 0, 2)).reshape(spectra.shape[0], kcoef)

def gram_dot(left, right):
    return lax.dot_general(left.astype(jnp.float32), right.astype(jnp.float32), (((0,), (0,)), ((), ())), preferred_element_type=jnp.float32)

def reference(fields, legendre, order_table, window_start, ridge):
    window = lax.dynamic_slice_in_dim(order_table, window_start[0].astype(jnp.int32), K, 1)
    degree = window[0]
    column = (window[1] + MORD * window[2]).astype(jnp.int32)
    dft_basis = make_basis(NLON)
    scale = 1.0 / math.sqrt(NLON)

    def one_block(time_block):
        flat = time_block.reshape(T_DEV * NLAT, NLON)
        spectra = (jnp.dot(flat.astype(jnp.float32), dft_basis.astype(jnp.float32), preferred_element_type=jnp.float32) * scale).reshape(T_DEV, NLAT, NLON)
        return legendre_contract(spectra, legendre, column)
    blocks = fields.reshape(N_TM, T_DEV, NLAT, NLON)
    coeffs = lax.map(one_block, blocks).reshape(NT, K).astype(jnp.bfloat16)
    ridge_diag = ridge[0] * (1.0 + (degree * (degree + 1)).astype(jnp.float32) / float(LMAX * (LMAX + 1)))
    gram = gram_dot(coeffs, coeffs) * (1.0 / NT) + jnp.diag(ridge_diag)
    factor = jnp.linalg.cholesky(gram[:PANEL, :PANEL])
    panel = jax.scipy.linalg.solve_triangular(factor, gram[:, :PANEL].T, lower=True).T
    lower_rows = panel[PANEL:]
    schur = gram[PANEL:, PANEL:] - jnp.dot(lower_rows, lower_rows.T, precision=lax.Precision.HIGHEST)
    upper_part = jnp.concatenate([panel[:PANEL], lower_rows.T], axis=1)
    lower_part = jnp.concatenate([lower_rows, schur], axis=1)
    return jnp.concatenate([upper_part, lower_part], axis=0)
```

```python
import functools
import math

import jax
import jax.numpy as jnp
import ml_dtypes
import numpy as np
from jax import lax
from jax.experimental import pallas as pl
from jax.experimental.pallas import tpu as pltpu
from jax.sharding import PartitionSpec as P

LMAX = 720
PANEL = 512
CBLK = 256
KBLK = 512
LANE = 128
VMEM_LIMIT = 56 * 1024 * 1024
F32 = jnp.float32
BF16 = jnp.bfloat16


def basis_blocks(nlon):
    half = nlon // 2
    longitude = np.arange(nlon, dtype=np.int64)[:, None]
    column = np.arange(nlon, dtype=np.int64)[None, :]
    freq = column % half
    phase = (freq * longitude % nlon).astype(np.float32) * np.float32(2.0 * math.pi / nlon)
    table = np.where(column < half, np.cos(phase), np.sin(phase)).astype(ml_dtypes.bfloat16)
    blocks = -(-nlon // CBLK)
    padded = np.zeros((nlon, blocks * CBLK), ml_dtypes.bfloat16)
    padded[:, :nlon] = table
    return np.ascontiguousarray(padded.reshape(nlon, blocks, CBLK).transpose(1, 0, 2))


def one_hot(column, start, rows):
    ids = lax.broadcasted_iota(jnp.int32, (rows, column.shape[1]), 0)
    return jnp.where(ids == column - start, 1.0, 0.0).astype(BF16)


def latitude_sums(chosen, weights, times):
    lats = weights.shape[0]
    sums = [
        jnp.sum(chosen[t * lats : (t + 1) * lats] * weights, axis=0, keepdims=True)
        for t in range(times)
    ]
    return jnp.concatenate(sums, axis=0)


def spectra_kernel(scale, fields_ref, basis_ref, column_ref, weights_ref, spectra_ref, part_ref, chosen_ref):
    step = pl.program_id(0)
    times = fields_ref.shape[0]
    block = jnp.concatenate(
        [jnp.dot(fields_ref[t], basis_ref[0], preferred_element_type=F32) for t in range(times)], axis=0
    )
    block = (block * scale).astype(BF16)
    spectra_ref[...] = block
    hot = one_hot(column_ref[...], step * CBLK, CBLK)
    term = jnp.dot(block, hot, preferred_element_type=F32)

    @pl.when(step == 0)
    def _():
        chosen_ref[...] = term

    @pl.when(step > 0)
    def _():
        chosen_ref[...] += term

    @pl.when(step == pl.num_programs(0) - 1)
    def _():
        part_ref[...] = latitude_sums(chosen_ref[...], weights_ref[...].astype(F32), times)


def spectra_and_panel(fields, basis, column, legendre):
    times, lats, nlon = fields.shape
    blocks = basis.shape[0]
    rows = times * lats
    return pl.pallas_call(
        functools.partial(spectra_kernel, 1.0 / math.sqrt(nlon)),
        grid=(blocks,),
        in_specs=[
            pl.BlockSpec((times, lats, nlon), lambda i: (0, 0, 0)),
            pl.BlockSpec((1, nlon, CBLK), lambda i: (i, 0, 0)),
            pl.BlockSpec((1, PANEL), lambda i: (0, 0)),
            pl.BlockSpec((lats, PANEL), lambda i: (0, 0)),
        ],
        out_specs=[
            pl.BlockSpec((rows, CBLK), lambda i: (0, i)),
            pl.BlockSpec((times, PANEL), lambda i: (0, 0)),
        ],
        out_shape=[
            jax.ShapeDtypeStruct((rows, blocks * CBLK), BF16),
            jax.ShapeDtypeStruct((times, PANEL), F32),
        ],
        scratch_shapes=[pltpu.VMEM((rows, PANEL), F32)],
        compiler_params=pltpu.CompilerParams(vmem_limit_bytes=VMEM_LIMIT),
        cost_estimate=pl.CostEstimate(
            flops=2 * rows * blocks * CBLK * (nlon + PANEL), bytes_accessed=8 << 20, transcendentals=0
        ),
        name="spectra_and_panel",
    )(fields, basis, column, legendre)


def contract_kernel(times, spectra_ref, column_ref, weights_ref, part_ref):
    hot = one_hot(column_ref[...], 0, spectra_ref.shape[1])
    chosen = jnp.dot(spectra_ref[...], hot, preferred_element_type=F32)
    part_ref[...] = latitude_sums(chosen, weights_ref[...].astype(F32), times)


def contract_rest(spectra, column, legendre, times):
    rows, cols = spectra.shape
    lats, kcoef = legendre.shape
    first = PANEL // KBLK
    steps = kcoef // KBLK - first
    return pl.pallas_call(
        functools.partial(contract_kernel, times),
        grid=(steps,),
        in_specs=[
            pl.BlockSpec((rows, cols), lambda i: (0, 0)),
            pl.BlockSpec((1, KBLK), lambda i: (0, i + first)),
            pl.BlockSpec((lats, KBLK), lambda i: (0, i + first)),
        ],
        out_specs=pl.BlockSpec((times, KBLK), lambda i: (0, i)),
        out_shape=jax.ShapeDtypeStruct((times, steps * KBLK), F32),
        compiler_params=pltpu.CompilerParams(vmem_limit_bytes=VMEM_LIMIT),
        cost_estimate=pl.CostEstimate(
            flops=2 * rows * cols * steps * KBLK, bytes_accessed=8 << 20, transcendentals=0
        ),
        name="contract_rest",
    )(spectra, column, legendre)


def split(value, pieces):
    out = []
    for _ in range(pieces):
        piece = value.astype(BF16)
        out.append(piece)
        value = value - piece.astype(F32)
    return out


def panel_kernel(coef_ref, lam_ref, w_ref, diag_ref, inverse_ref, q_ref, g_ref, y_ref, x_ref, z_ref):
    nt = coef_ref.shape[0]
    lanes = PANEL + LANE
    coef = coef_ref[...]
    lam = lam_ref[...]
    scaled = coef / lam
    starts, total = [], 0
    for r in range(nt):
        low = r // 8 * 8
        z_ref[total : total + nt - low, :] = coef[low:, :] * scaled[r : r + 1, :]
        starts.append(total)
        total += nt - low
    ids = lax.broadcasted_iota(jnp.int32, (PANEL, lanes), 0)
    upto = lax.broadcasted_iota(jnp.int32, (PANEL, lanes), 1)
    tri = jnp.where(ids < upto, 1.0, 0.0).astype(BF16)
    prefix = 0.0
    for piece in split(z_ref[...], 3)[::-1]:
        prefix = prefix + jnp.dot(piece, tri, preferred_element_type=F32)
    q_ref[...] = prefix
    y_ref[:, :PANEL] = coef
    eye = lax.broadcasted_iota(jnp.int32, (nt, LANE), 0) == lax.broadcasted_iota(jnp.int32, (nt, LANE), 1)
    y_ref[:, PANEL:] = jnp.where(eye, 1.0, 0.0)
    inverses = []
    for r in range(nt):
        low = r // 8 * 8
        place = low + lax.broadcasted_iota(jnp.int32, (nt - low, lanes), 0)
        row = q_ref[starts[r] : starts[r] + nt - low, :] + jnp.where(place == r, float(nt), 0.0)
        for p in range(r):
            base = starts[p] + low - p // 8 * 8
            factor = g_ref[starts[p] + r - p // 8 * 8 : starts[p] + r - p // 8 * 8 + 1, :]
            row = row - factor * q_ref[base : base + nt - low, :]
        q_ref[starts[r] : starts[r] + nt - low, :] = row
        inv = 1.0 / row[r - low : r - low + 1, :]
        inverses.append(inv)
        ratio = jnp.where(place > r, row * inv, 0.0)
        g_ref[starts[r] : starts[r] + nt - low, :] = ratio
        y_ref[low:, :] = y_ref[low:, :] - ratio * y_ref[r : r + 1, :]
    x_ref[...] = jnp.zeros_like(x_ref)
    for r in range(nt - 1, -1, -1):
        low = r // 8 * 8
        ratio = g_ref[starts[r] : starts[r] + nt - low, :]
        tail = jnp.sum(ratio * x_ref[low:, :], axis=0, keepdims=True)
        x_ref[r : r + 1, :] = y_ref[r : r + 1, :] * inverses[r] - tail
    solved = x_ref[:, :PANEL]
    pivot = jnp.sqrt(lam + jnp.sum(coef * solved, axis=0, keepdims=True))
    w_ref[...] = solved / pivot
    diag_ref[...] = lam / pivot
    inverse_ref[...] = x_ref[:, PANEL:]


def panel_small(coef, lam):
    nt = coef.shape[0]
    rows = sum(nt - r // 8 * 8 for r in range(nt))
    lanes = PANEL + LANE
    return pl.pallas_call(
        panel_kernel,
        out_shape=[
            jax.ShapeDtypeStruct((nt, PANEL), F32),
            jax.ShapeDtypeStruct((1, PANEL), F32),
            jax.ShapeDtypeStruct((nt, LANE), F32),
        ],
        scratch_shapes=[
            pltpu.VMEM((rows, lanes), F32),
            pltpu.VMEM((rows, lanes), F32),
            pltpu.VMEM((nt, lanes), F32),
            pltpu.VMEM((nt, lanes), F32),
            pltpu.VMEM((rows, PANEL), F32),
        ],
        compiler_params=pltpu.CompilerParams(vmem_limit_bytes=VMEM_LIMIT),
        cost_estimate=pl.CostEstimate(flops=4 << 30, bytes_accessed=1 << 18, transcendentals=0),
        name="panel_small",
    )(coef, lam)


def panel_large(coef, lam):
    nt = coef.shape[0]
    gram = jnp.dot(coef.T, coef, precision=lax.Precision.HIGHEST) / nt + jnp.diag(lam[0])
    factor = jnp.linalg.cholesky(gram)
    solved = jax.scipy.linalg.solve_triangular(factor, coef.T, lower=True)
    w = solved.T / nt
    rest = jnp.eye(nt, dtype=F32) / nt - jnp.dot(w, w.T, precision=lax.Precision.HIGHEST)
    pivot = jnp.diagonal(factor)[None, :]
    pad = -(-nt // LANE) * LANE - nt
    return w, pivot - jnp.sum(coef * w, axis=0, keepdims=True), jnp.pad(rest, ((0, 0), (0, pad)))


def stack_pieces(value):
    high, low = split(value, 2)
    return jnp.concatenate([high.astype(F32), low.astype(F32)], axis=0).astype(BF16)


def twice(value):
    return jnp.concatenate([value, value], axis=0).astype(BF16)


def contract_times(left, right):
    return lax.dot_general(left, right, (((0,), (0,)), ((), ())), preferred_element_type=F32)


def tile_kernel(place_ref, rows_ref, cols_ref, w_ref, wrows_ref, diag_ref, lam_ref, inverse_ref, out_ref):
    height, width = out_ref.shape
    nt = rows_ref.shape[0]
    row_start = place_ref[0]
    col_start = place_ref[1] + pl.program_id(0) * width
    row_ids = row_start + lax.broadcasted_iota(jnp.int32, (height, width), 0)
    col_ids = col_start + lax.broadcasted_iota(jnp.int32, (height, width), 1)
    in_panel_rows = row_start < PANEL
    in_panel_cols = col_start < PANEL

    @pl.when(in_panel_cols)
    def _():
        value = contract_times(twice(rows_ref[...]), stack_pieces(w_ref[...]))
        value = jnp.where(row_ids >= col_ids, value, 0.0)
        out_ref[...] = value + jnp.where(row_ids == col_ids, diag_ref[...], 0.0)

    @pl.when(jnp.logical_not(in_panel_cols) & in_panel_rows)
    def _():
        out_ref[...] = contract_times(stack_pieces(wrows_ref[...]), twice(cols_ref[...]))

    @pl.when(jnp.logical_not(in_panel_cols) & jnp.logical_not(in_panel_rows))
    def _():
        cols = cols_ref[...]
        turned = contract_times(stack_pieces(inverse_ref[:, :nt]), twice(cols))
        value = contract_times(twice(rows_ref[...]), stack_pieces(turned))
        out_ref[...] = value + jnp.where(row_ids == col_ids, lam_ref[...], 0.0)


def out_tile(place, rows, cols, w, wrows, diag, lam_cols, inverse):
    nt, height = rows.shape
    width = cols.shape[1]
    block = min(PANEL, width)
    whole = lambda i: (0, 0)
    part = lambda i: (0, i)
    return pl.pallas_call(
        tile_kernel,
        grid=(width // block,),
        in_specs=[
            pl.BlockSpec(memory_space=pltpu.SMEM),
            pl.BlockSpec((nt, height), whole),
            pl.BlockSpec((nt, block), part),
            pl.BlockSpec((nt, PANEL), whole),
            pl.BlockSpec((nt, height), whole),
            pl.BlockSpec((1, PANEL), whole),
            pl.BlockSpec((1, block), part),
            pl.BlockSpec(inverse.shape, whole),
        ],
        out_specs=pl.BlockSpec((height, block), part),
        out_shape=jax.ShapeDtypeStruct((height, width), F32),
        compiler_params=pltpu.CompilerParams(vmem_limit_bytes=VMEM_LIMIT),
        cost_estimate=pl.CostEstimate(
            flops=4 * nt * height * width, bytes_accessed=4 * height * width, transcendentals=0
        ),
        name="out_tile",
    )(place, rows, cols, w, wrows, diag, lam_cols, inverse)


def on_device(basis, fields, legendre, order_table, window_start, ridge):
    times, lats, nlon = fields.shape
    kcoef = legendre.shape[1]
    tm_count, lat_count = lax.axis_size("tm"), lax.axis_size("lat")
    nt = times * tm_count
    rows_width, cols_width = kcoef // tm_count, kcoef // lat_count
    tm_index, lat_index = lax.axis_index("tm"), lax.axis_index("lat")
    window = lax.dynamic_slice_in_dim(order_table, window_start[0], kcoef, 1)
    degree = window[0:1]
    column = window[1:2] + nlon // 2 * window[2:3]
    lam = ridge[0] * (1.0 + (degree * (degree + 1)).astype(F32) / float(LMAX * (LMAX + 1)))
    spare = -lats % 8
    if spare:
        fields = jnp.pad(fields, ((0, 0), (0, spare), (0, 0)))
        legendre = jnp.pad(legendre, ((0, spare), (0, 0)))

    spectra, panel_part = spectra_and_panel(fields, basis, column, legendre)
    everyone = ("tm", "lat")
    sent = jnp.broadcast_to(panel_part[None], (tm_count * lat_count, times, PANEL))
    arrived = lax.all_to_all(sent, everyone, 0, 0).reshape(tm_count, lat_count, times, PANEL)
    panel_coef = jnp.sum(arrived, axis=1).astype(BF16).astype(F32).reshape(nt, PANEL)

    rest_part = contract_rest(spectra, column, legendre, times)
    part = jnp.concatenate([panel_part, rest_part], axis=1)
    coef = lax.psum(part, "lat").astype(BF16)
    cols_own = lax.dynamic_slice_in_dim(coef, lat_index * cols_width, cols_width, 1)
    wanted = jnp.concatenate(
        [
            jnp.broadcast_to(cols_own[None], (tm_count, times, cols_width)),
            coef.reshape(times, tm_count, rows_width).transpose(1, 0, 2),
        ],
        axis=2,
    )
    got = lax.all_to_all(wanted, "tm", 0, 0).reshape(nt, cols_width + rows_width)
    cols, rows = got[:, :cols_width].astype(F32), got[:, cols_width:].astype(F32)

    lam_panel = lam[:, :PANEL]
    w, diag, inverse = (panel_small if nt <= 32 else panel_large)(panel_coef, lam_panel)
    row_start, col_start = tm_index * rows_width, lat_index * cols_width
    wrows = lax.dynamic_slice_in_dim(w, jnp.minimum(row_start, PANEL - rows_width), rows_width, 1)
    lam_cols = lax.dynamic_slice_in_dim(lam, col_start, cols_width, 1)
    place = jnp.stack([row_start, col_start]).astype(jnp.int32)
    return out_tile(place, rows, cols, w, wrows, diag, lam_cols, inverse)


def solution(mesh):
    def run(fields, legendre, order_table, window_start, ridge):
        basis = jnp.asarray(basis_blocks(fields.shape[2]))
        placed = (P(), P("tm", "lat", None), P("lat", None), P(), P(), P())
        body = jax.shard_map(on_device, mesh=mesh, in_specs=placed, out_specs=P("tm", "lat"), check_vma=False)
        return body(basis, fields, legendre, order_table, window_start, ridge)

    return run
```

```python
import functools
import math

import jax
import jax.numpy as jnp
import ml_dtypes
import numpy as np
from jax import lax
from jax.experimental import pallas as pl
from jax.experimental.pallas import tpu as pltpu
from jax.sharding import PartitionSpec as P

LMAX = 720
PANEL = 512
LANE = 128
SUB = 8
GATHER = 256
STEP = 1024
TRANSFORMS = 3
VMEM_LIMIT = 56 * 1024 * 1024
F32 = jnp.float32
BF16 = jnp.bfloat16


def basis_table(nlon):
    half = nlon // 2
    column = np.arange(nlon, dtype=np.int64)[:, None]
    longitude = np.arange(nlon, dtype=np.int64)[None, :]
    phase = (column % half * longitude % nlon).astype(np.float32) * np.float32(2.0 * math.pi / nlon)
    return np.where(column < half, np.cos(phase), np.sin(phase)).astype(ml_dtypes.bfloat16)


def pick_rows(column_ref, start, table_ref, picked_ref):
    for j in range(GATHER):
        group = pl.multiple_of(column_ref[start + j], SUB)
        picked_ref[SUB * j : SUB * (j + 1), :] = table_ref[pl.ds(group, SUB), :]


def latitude_sums(picked_ref, weights, times):
    lats = weights.shape[0]
    pieces = -(-lats // LANE)
    sums = []
    for t in range(times):
        rows = [picked_ref[pl.ds(pieces * t + s, GATHER, stride=SUB), :] for s in range(pieces)]
        value = jnp.concatenate(rows, axis=1).astype(BF16)[:, :lats]
        every = jnp.dot(value, weights, preferred_element_type=F32)
        own = []
        for low in range(0, GATHER, LANE):
            square = every[low : low + LANE, low : low + LANE]
            shape = (LANE, LANE)
            eye = lax.broadcasted_iota(jnp.int32, shape, 0) == lax.broadcasted_iota(jnp.int32, shape, 1)
            own.append(jnp.sum(jnp.where(eye, square, 0.0), axis=0, keepdims=True))
        sums.append(jnp.concatenate(own, axis=1))
    return jnp.concatenate(sums, axis=0)


def contract_block(place, width, step, first, last, column_ref, table_ref, weights_ref, sums_ref, even_ref, odd_ref):
    times = sums_ref.shape[0]
    picked = [even_ref, odd_ref]

    @pl.when(step == first)
    def _():
        pick_rows(column_ref, place(0), table_ref, even_ref)

    for part in range(width // GATHER):
        low = part * GATHER
        if low + GATHER < width:
            after = place(step - first) + low + GATHER
        else:
            after = place(jnp.minimum(step + 1, last) - first)
        pick_rows(column_ref, after, table_ref, picked[(part + 1) % 2])
        at = pl.multiple_of((step - first) * width + low, GATHER)
        sums_ref[:, pl.ds(at, GATHER)] = latitude_sums(
            picked[part % 2], weights_ref[:, low : low + GATHER], times
        )


class Plan:
    def __init__(self, kcoef, tm_count, lat_count, times, skip, take, with_panel):
        self.tm_count, self.lat_count, self.times = tm_count, lat_count, times
        self.skip, self.take = skip, take
        self.part_width, self.rows_width = kcoef // lat_count, kcoef // tm_count
        self.width = min(STEP, take)
        self.per_part = take // self.width
        self.steps = self.per_part * lat_count
        self.col_tiles, self.row_tiles = take // LANE, self.rows_width // LANE
        self.panel_tiles = PANEL // LANE if with_panel else 0
        self.first_panel = self.col_tiles + self.row_tiles
        self.across = -(-(self.first_panel + self.panel_tiles) // SUB)
        self.slab = (times * SUB, self.across * LANE)
        self.shape = (tm_count * lat_count,) + self.slab
        self.sums_shape = (self.across, tm_count * self.slab[0], LANE)

    def place(self, i):
        return i // self.per_part * self.part_width + self.skip + i % self.per_part * self.width

    def block(self, i):
        return i // self.per_part * (self.part_width // self.width) + self.skip // self.width + i % self.per_part

    def rows_place(self, owner):
        part, low = divmod(owner * self.rows_width, self.part_width)
        low -= self.skip
        return part * self.take + low if 0 <= low < self.take else None

    def holds_rows(self, tm_index):
        low = tm_index * self.rows_width % self.part_width - self.skip
        return (low >= 0) & (low < self.take)

    def spot(self, tile, time):
        low = tile % self.across * LANE
        return time * SUB + tile // self.across, slice(low, low + LANE)

    def pack(self, sums_ref, slab_ref, sent_ref):
        def fill(tile, source, count):
            for n in range(count):
                for t in range(self.times):
                    row, lanes = self.spot(tile + n, t)
                    low = source + n * LANE
                    slab_ref[row : row + 1, lanes] = sums_ref[t : t + 1, low : low + LANE]

        slab_ref[...] = jnp.zeros_like(slab_ref)
        fill(self.first_panel, 0, self.panel_tiles)
        for part in range(self.lat_count):
            fill(0, part * self.take, self.col_tiles)
            for owner in range(self.tm_count):
                source = self.rows_place(owner)
                if source is not None:
                    fill(self.col_tiles, source, self.row_tiles)
                sent_ref[owner * self.lat_count + part] = slab_ref[...].astype(BF16)

    def gather_sums(self, got_ref, slabs_ref):
        rows = self.slab[0]
        for sender in range(self.tm_count):
            first = sender * self.lat_count
            total = got_ref[first].astype(F32)
            for part in range(1, self.lat_count):
                total = total + got_ref[first + part].astype(F32)
            for n in range(self.across):
                slabs_ref[n, sender * rows : (sender + 1) * rows, :] = total[:, n * LANE : (n + 1) * LANE]

    def tile(self, slabs_ref, tile):
        pieces = []
        for t in range(self.times):
            row = t * SUB + tile // self.across
            pieces.append(slabs_ref[tile % self.across, pl.ds(row, self.tm_count, stride=self.slab[0]), :])
        return jnp.concatenate(pieces, axis=0).astype(BF16).astype(F32)

    def unpack(self, got):
        split_shape = (self.tm_count, self.lat_count, self.times, SUB * self.across * LANE)
        total = got.astype(F32).reshape(split_shape).sum(axis=1).astype(BF16).astype(F32)
        return total.transpose(1, 0, 2).reshape(self.times * self.tm_count, -1)


def spectra_kernel(plan, scale, transforms, column_ref, fields_ref, basis_ref, weights_ref, sent_ref, kept_ref,
                   lines_ref, table_ref, even_ref, odd_ref, sums_ref, slab_ref, kept_sem):
    step = pl.program_id(0)
    last = pl.num_programs(0) - 1
    times, lats, _ = fields_ref.shape
    pieces = -(-lats // LANE)
    rows = basis_ref.shape[0]
    keep = pltpu.make_async_copy(table_ref, kept_ref, kept_sem)

    @pl.when(step == 0)
    def _():
        for t in range(times):
            lines_ref[pieces * LANE * t : pieces * LANE * t + lats, :] = fields_ref[t]

    @pl.when(step < transforms)
    def _():
        spectra = scale * lax.dot_general(
            basis_ref[...], lines_ref[...], (((1,), (1,)), ((), ())), preferred_element_type=F32
        )
        for s in range(times * pieces):
            table_ref[pl.ds(step * rows * SUB + s, rows, stride=SUB), :] = spectra[:, LANE * s : LANE * (s + 1)]

    @pl.when(step == transforms - 1)
    def _():
        keep.start()

    @pl.when(step >= transforms)
    def _():
        contract_block(plan.place, plan.width, step, transforms, last, column_ref, table_ref, weights_ref,
                       sums_ref, even_ref, odd_ref)

    @pl.when(step == last)
    def _():
        plan.pack(sums_ref, slab_ref, sent_ref)
        keep.wait()


def contract_kernel(plan, column_ref, table_ref, weights_ref, sent_ref, even_ref, odd_ref, sums_ref, slab_ref):
    step = pl.program_id(0)
    last = pl.num_programs(0) - 1
    contract_block(plan.place, plan.width, step, 0, last, column_ref, table_ref, weights_ref, sums_ref,
                   even_ref, odd_ref)

    @pl.when(step == last)
    def _():
        plan.pack(sums_ref, slab_ref, sent_ref)


def contract_scratch(plan):
    return [
        pltpu.VMEM((GATHER * SUB, LANE), F32),
        pltpu.VMEM((GATHER * SUB, LANE), F32),
        pltpu.VMEM((plan.times, plan.steps * plan.width), F32),
        pltpu.VMEM(plan.slab, F32),
    ]


def spectra_and_contract(plan, fields, basis, column, legendre):
    times, lats, nlon = fields.shape
    pieces = -(-lats // LANE)
    rows = nlon // TRANSFORMS
    later = lambda i: jnp.maximum(i - TRANSFORMS, 0)
    return pl.pallas_call(
        functools.partial(spectra_kernel, plan, 1.0 / math.sqrt(nlon), TRANSFORMS),
        grid_spec=pltpu.PrefetchScalarGridSpec(
            num_scalar_prefetch=1,
            grid=(TRANSFORMS + plan.steps,),
            in_specs=[
                pl.BlockSpec((times, lats, nlon), lambda i, c: (0, 0, 0)),
                pl.BlockSpec((rows, nlon), lambda i, c: (jnp.minimum(i, TRANSFORMS - 1), 0)),
                pl.BlockSpec((lats, plan.width), lambda i, c: (0, plan.block(later(i)))),
            ],
            out_specs=[
                pl.BlockSpec(plan.shape, lambda i, c: (0, 0, 0)),
                pl.BlockSpec(memory_space=pl.ANY),
            ],
            scratch_shapes=[
                pltpu.VMEM((times * pieces * LANE, nlon), BF16),
                pltpu.VMEM((nlon * SUB, LANE), F32),
                *contract_scratch(plan),
                pltpu.SemaphoreType.DMA(()),
            ],
        ),
        out_shape=[
            jax.ShapeDtypeStruct(plan.shape, BF16),
            jax.ShapeDtypeStruct((nlon * SUB, LANE), F32),
        ],
        compiler_params=pltpu.CompilerParams(vmem_limit_bytes=VMEM_LIMIT),
        cost_estimate=pl.CostEstimate(flops=12 << 30, bytes_accessed=8 << 20, transcendentals=0),
        name="spectra_and_contract",
    )(column, fields, basis, legendre)


def contract_rest(plan, table, column, legendre):
    lats = legendre.shape[0]
    return pl.pallas_call(
        functools.partial(contract_kernel, plan),
        grid_spec=pltpu.PrefetchScalarGridSpec(
            num_scalar_prefetch=1,
            grid=(plan.steps,),
            in_specs=[
                pl.BlockSpec(table.shape, lambda i, c: (0, 0)),
                pl.BlockSpec((lats, plan.width), lambda i, c: (0, plan.block(i))),
            ],
            out_specs=pl.BlockSpec(plan.shape, lambda i, c: (0, 0, 0)),
            scratch_shapes=contract_scratch(plan),
        ),
        out_shape=jax.ShapeDtypeStruct(plan.shape, BF16),
        compiler_params=pltpu.CompilerParams(vmem_limit_bytes=VMEM_LIMIT),
        cost_estimate=pl.CostEstimate(flops=8 << 30, bytes_accessed=8 << 20, transcendentals=0),
        name="contract_rest",
    )(column, table, legendre)


def split(value, pieces):
    out = []
    for _ in range(pieces):
        piece = value.astype(BF16)
        out.append(piece)
        value = value - piece.astype(F32)
    return out


def panel_kernel(plan, got_ref, lam_ref, w_ref, diag_ref, inverse_ref, slabs_ref, q_ref, g_ref, y_ref, x_ref, z_ref):
    nt = w_ref.shape[0]
    lanes = PANEL + LANE
    plan.gather_sums(got_ref, slabs_ref)
    coef = jnp.concatenate(
        [plan.tile(slabs_ref, plan.first_panel + n) for n in range(plan.panel_tiles)], axis=1
    )
    lam = lam_ref[...]
    scaled = coef / lam
    starts, total = [], 0
    for r in range(nt):
        low = r // 8 * 8
        z_ref[total : total + nt - low, :] = coef[low:, :] * scaled[r : r + 1, :]
        starts.append(total)
        total += nt - low
    ids = lax.broadcasted_iota(jnp.int32, (PANEL, lanes), 0)
    upto = lax.broadcasted_iota(jnp.int32, (PANEL, lanes), 1)
    tri = jnp.where(ids < upto, 1.0, 0.0).astype(BF16)
    prefix = 0.0
    for piece in split(z_ref[...], 3)[::-1]:
        prefix = prefix + jnp.dot(piece, tri, preferred_element_type=F32)
    q_ref[...] = prefix
    y_ref[:, :PANEL] = coef
    eye = lax.broadcasted_iota(jnp.int32, (nt, LANE), 0) == lax.broadcasted_iota(jnp.int32, (nt, LANE), 1)
    y_ref[:, PANEL:] = jnp.where(eye, 1.0, 0.0)
    inverses = []
    for r in range(nt):
        low = r // 8 * 8
        place = low + lax.broadcasted_iota(jnp.int32, (nt - low, lanes), 0)
        row = q_ref[starts[r] : starts[r] + nt - low, :] + jnp.where(place == r, float(nt), 0.0)
        for p in range(r):
            base = starts[p] + low - p // 8 * 8
            factor = g_ref[starts[p] + r - p // 8 * 8 : starts[p] + r - p // 8 * 8 + 1, :]
            row = row - factor * q_ref[base : base + nt - low, :]
        q_ref[starts[r] : starts[r] + nt - low, :] = row
        inv = 1.0 / row[r - low : r - low + 1, :]
        inverses.append(inv)
        ratio = jnp.where(place > r, row * inv, 0.0)
        g_ref[starts[r] : starts[r] + nt - low, :] = ratio
        y_ref[low:, :] = y_ref[low:, :] - ratio * y_ref[r : r + 1, :]
    x_ref[...] = jnp.zeros_like(x_ref)
    for r in range(nt - 1, -1, -1):
        low = r // 8 * 8
        ratio = g_ref[starts[r] : starts[r] + nt - low, :]
        tail = jnp.sum(ratio * x_ref[low:, :], axis=0, keepdims=True)
        x_ref[r : r + 1, :] = y_ref[r : r + 1, :] * inverses[r] - tail
    solved = x_ref[:, :PANEL]
    pivot = jnp.sqrt(lam + jnp.sum(coef * solved, axis=0, keepdims=True))
    w_ref[...] = solved / pivot
    diag_ref[...] = lam / pivot
    inverse_ref[...] = x_ref[:, PANEL:]


def panel_small(plan, got, lam):
    nt = plan.times * plan.tm_count
    rows = sum(nt - r // 8 * 8 for r in range(nt))
    lanes = PANEL + LANE
    return pl.pallas_call(
        functools.partial(panel_kernel, plan),
        grid=(1,),
        in_specs=[
            pl.BlockSpec(plan.shape, lambda i: (0, 0, 0)),
            pl.BlockSpec((1, PANEL), lambda i: (0, 0)),
        ],
        out_specs=[
            pl.BlockSpec((nt, PANEL), lambda i: (0, 0)),
            pl.BlockSpec((1, PANEL), lambda i: (0, 0)),
            pl.BlockSpec((nt, LANE), lambda i: (0, 0)),
        ],
        out_shape=[
            jax.ShapeDtypeStruct((nt, PANEL), F32),
            jax.ShapeDtypeStruct((1, PANEL), F32),
            jax.ShapeDtypeStruct((nt, LANE), F32),
        ],
        scratch_shapes=[
            pltpu.VMEM(plan.sums_shape, F32),
            pltpu.VMEM((rows, lanes), F32),
            pltpu.VMEM((rows, lanes), F32),
            pltpu.VMEM((nt, lanes), F32),
            pltpu.VMEM((nt, lanes), F32),
            pltpu.VMEM((rows, PANEL), F32),
        ],
        compiler_params=pltpu.CompilerParams(vmem_limit_bytes=VMEM_LIMIT),
        cost_estimate=pl.CostEstimate(flops=4 << 30, bytes_accessed=1 << 18, transcendentals=0),
        name="panel_small",
    )(got, lam)


def panel_large(plan, got, lam):
    low = plan.first_panel * LANE
    coef, lam = plan.unpack(got)[:, low : low + PANEL], lam[:, :PANEL]
    nt = coef.shape[0]
    gram = jnp.dot(coef.T, coef, precision=lax.Precision.HIGHEST) / nt + jnp.diag(lam[0])
    factor = jnp.linalg.cholesky(gram)
    solved = jax.scipy.linalg.solve_triangular(factor, coef.T, lower=True)
    w = solved.T / nt
    rest = jnp.eye(nt, dtype=F32) / nt - jnp.dot(w, w.T, precision=lax.Precision.HIGHEST)
    pivot = jnp.diagonal(factor)[None, :]
    pad = -(-nt // LANE) * LANE - nt
    return w, pivot - jnp.sum(coef * w, axis=0, keepdims=True), jnp.pad(rest, ((0, 0), (0, pad)))


def stack_pieces(value):
    high, low = split(value, 2)
    return jnp.concatenate([high.astype(F32), low.astype(F32)], axis=0).astype(BF16)


def twice(value):
    return jnp.concatenate([value, value], axis=0).astype(BF16)


def contract_times(left, right):
    return lax.dot_general(left, right, (((0,), (0,)), ((), ())), preferred_element_type=F32)


def times_first(value):
    return value.astype(F32).T.astype(BF16)


def tile_kernel(early, late, first_ref, second_ref, w_ref, diag_ref, lam_ref, inverse_ref, out_ref,
                first_slabs, second_slabs, rows_ref, cols_ref, left_ref, left_panel_ref):
    height, width = out_ref.shape
    nt = rows_ref.shape[0]
    step = pl.program_id(0)
    tm_index = lax.axis_index("tm")
    row_start = tm_index * height
    col_start = lax.axis_index("lat") * cols_ref.shape[1] + step * width
    in_panel_rows = row_start < PANEL
    in_panel_cols = col_start < PANEL
    on_diagonal = (row_start < col_start + width) & (col_start < row_start + height)

    @pl.when(step == 0)
    def _():
        early.gather_sums(first_ref, first_slabs)
        late.gather_sums(second_ref, second_slabs)
        for n in range(early.col_tiles):
            cols_ref[:, n * LANE : (n + 1) * LANE] = early.tile(first_slabs, n)
        for n in range(late.col_tiles):
            low = early.take + n * LANE
            cols_ref[:, low : low + LANE] = late.tile(second_slabs, n)
        in_early = early.holds_rows(tm_index)
        for n in range(early.row_tiles):
            value = jnp.where(
                in_early,
                early.tile(first_slabs, early.col_tiles + n),
                late.tile(second_slabs, late.col_tiles + n),
            )
            rows_ref[:, n * LANE : (n + 1) * LANE] = value
        left_ref[...] = times_first(twice(rows_ref[...]))

    @pl.when((step == 0) & in_panel_rows)
    def _():
        low = pl.multiple_of(jnp.minimum(row_start, PANEL - height), LANE)
        left_panel_ref[...] = times_first(stack_pieces(w_ref[:, pl.ds(low, height)]))

    def ids():
        rows = row_start + lax.broadcasted_iota(jnp.int32, (height, width), 0)
        return rows, col_start + lax.broadcasted_iota(jnp.int32, (height, width), 1)

    def product(left, right):
        return jnp.dot(left, right, preferred_element_type=F32)

    own = pl.ds(pl.multiple_of(step * width, LANE), width)

    @pl.when(in_panel_cols & in_panel_rows)
    def _():
        row_ids, col_ids = ids()
        value = product(left_ref[...], stack_pieces(w_ref[...]))
        value = jnp.where(row_ids >= col_ids, value, 0.0)
        out_ref[...] = value + jnp.where(row_ids == col_ids, diag_ref[...], 0.0)

    @pl.when(in_panel_cols & jnp.logical_not(in_panel_rows))
    def _():
        out_ref[...] = product(left_ref[...], stack_pieces(w_ref[...]))

    @pl.when(jnp.logical_not(in_panel_cols) & in_panel_rows)
    def _():
        out_ref[...] = product(left_panel_ref[...], twice(cols_ref[:, own]))

    @pl.when(jnp.logical_not(in_panel_cols) & jnp.logical_not(in_panel_rows))
    def _():
        turned = contract_times(stack_pieces(inverse_ref[:, :nt]), twice(cols_ref[:, own]))
        value = product(left_ref[...], stack_pieces(turned))

        @pl.when(on_diagonal)
        def _():
            row_ids, col_ids = ids()
            lam = lam_ref[:, pl.ds(pl.multiple_of(col_start, LANE), width)]
            out_ref[...] = value + jnp.where(row_ids == col_ids, lam, 0.0)

        @pl.when(jnp.logical_not(on_diagonal))
        def _():
            out_ref[...] = value


def out_tile(early, late, first, second, w, diag, lam, inverse):
    nt, height, width = early.times * early.tm_count, early.rows_width, early.part_width
    whole = lambda i: (0, 0)
    return pl.pallas_call(
        functools.partial(tile_kernel, early, late),
        grid=(width // PANEL,),
        in_specs=[
            pl.BlockSpec(early.shape, lambda i: (0, 0, 0)),
            pl.BlockSpec(late.shape, lambda i: (0, 0, 0)),
            pl.BlockSpec((nt, PANEL), whole),
            pl.BlockSpec((1, PANEL), whole),
            pl.BlockSpec(lam.shape, whole),
            pl.BlockSpec(inverse.shape, whole),
        ],
        out_specs=pl.BlockSpec((height, PANEL), lambda i: (0, i)),
        out_shape=jax.ShapeDtypeStruct((height, width), F32),
        scratch_shapes=[
            pltpu.VMEM(early.sums_shape, F32),
            pltpu.VMEM(late.sums_shape, F32),
            pltpu.VMEM((nt, height), F32),
            pltpu.VMEM((nt, width), F32),
            pltpu.VMEM((height, 2 * nt), BF16),
            pltpu.VMEM((height, 2 * nt), BF16),
        ],
        compiler_params=pltpu.CompilerParams(vmem_limit_bytes=VMEM_LIMIT),
        cost_estimate=pl.CostEstimate(
            flops=4 * nt * height * width, bytes_accessed=4 * height * width, transcendentals=0
        ),
        name="out_tile",
    )(first, second, w, diag, lam, inverse)


def on_device(basis, fields, legendre, order_table, window_start, ridge):
    times, _, nlon = fields.shape
    kcoef = legendre.shape[1]
    tm_count, lat_count = lax.axis_size("tm"), lax.axis_size("lat")
    window = lax.dynamic_slice_in_dim(order_table, window_start[0], kcoef, 1)
    degree = window[0:1]
    column = SUB * (window[1] + nlon // 2 * window[2])
    lam = ridge[0] * (1.0 + (degree * (degree + 1)).astype(F32) / float(LMAX * (LMAX + 1)))
    part_width = kcoef // lat_count
    cut = max(PANEL, part_width // 2)
    early = Plan(kcoef, tm_count, lat_count, times, 0, cut, True)
    late = Plan(kcoef, tm_count, lat_count, times, cut, part_width - cut, False)

    def exchange(sent):
        return lax.all_to_all(sent, ("tm", "lat"), 0, 0, tiled=True)

    sent, table = spectra_and_contract(early, fields, basis, column, legendre)
    first = exchange(sent)
    second = exchange(contract_rest(late, table, column, legendre))
    small = times * tm_count <= LANE // 4
    w, diag, inverse = (panel_small if small else panel_large)(early, first, lam)
    return out_tile(early, late, first, second, w, diag, lam, inverse)


def solution(mesh):
    def run(fields, legendre, order_table, window_start, ridge):
        basis = jnp.asarray(basis_table(fields.shape[2]))
        placed = (P(), P("tm", "lat", None), P("lat", None), P(), P(), P())
        body = jax.shard_map(on_device, mesh=mesh, in_specs=placed, out_specs=P("tm", "lat"), check_vma=False)
        return body(basis, fields, legendre, order_table, window_start, ridge)

    return run
```

```python
import functools
import math

import jax
import jax.numpy as jnp
import ml_dtypes
import numpy as np
from jax import lax
from jax.experimental import pallas as pl
from jax.experimental.pallas import tpu as pltpu
from jax.sharding import PartitionSpec as P

LMAX = 720
PANEL = 512
LANE = 128
SUB = 8
GATHER = 256
GROUP = 4
TRANSFORMS = 3
WIDE = 256
SPECTRA_VMEM = 36 * 1024 * 1024
SMALL_VMEM = 20 * 1024 * 1024
F32 = jnp.float32
BF16 = jnp.bfloat16


def basis_table(nlon):
    half = nlon // 2
    column = np.arange(nlon, dtype=np.int64)[:, None]
    longitude = np.arange(nlon, dtype=np.int64)[None, :]
    phase = (column % half * longitude % nlon).astype(np.float32) * np.float32(2.0 * math.pi / nlon)
    return np.where(column < half, np.cos(phase), np.sin(phase)).astype(ml_dtypes.bfloat16)


def pick_rows(column_ref, start, table_ref, picked_ref):
    for j in range(GATHER):
        group = pl.multiple_of(column_ref[start + j], SUB)
        picked_ref[SUB * j : SUB * (j + 1), :] = table_ref[pl.ds(group, SUB), :]


def latitude_sums(picked_ref, weights, times):
    lats = weights.shape[0]
    pieces = -(-lats // LANE)
    picked = [picked_ref[pl.ds(s, GATHER, stride=SUB), :] for s in range(times * pieces)]
    value = jnp.concatenate(
        [jnp.concatenate(picked[pieces * t : pieces * (t + 1)], axis=1) for t in range(times)], axis=0
    )
    spare = jnp.zeros((pieces * LANE - lats, GATHER), BF16)
    every = jnp.dot(value.astype(BF16), jnp.concatenate([weights, spare], axis=0), preferred_element_type=F32)
    shape = (LANE, LANE)
    eye = lax.broadcasted_iota(jnp.int32, shape, 0) == lax.broadcasted_iota(jnp.int32, shape, 1)
    sums = []
    for t in range(times):
        own = []
        for low in range(0, GATHER, LANE):
            square = every[t * GATHER + low : t * GATHER + low + LANE, low : low + LANE]
            own.append(jnp.sum(jnp.where(eye, square, 0.0), axis=0, keepdims=True))
        sums.append(jnp.concatenate(own, axis=1))
    return jnp.concatenate(sums, axis=0)


def contract(plan, column_ref, table_ref, weights_ref, sums_ref, even_ref, odd_ref, weights_copy):
    picked = [even_ref, odd_ref]

    def place(part):
        return jnp.minimum(part, plan.parts - 1) * GATHER

    pick_rows(column_ref, 0, table_ref, even_ref)

    @pl.loop(0, plan.parts // GROUP)
    def _(group):
        weights_copy(group).wait()
        for n in range(GROUP):
            part = group * GROUP + n
            pick_rows(column_ref, place(part + 1), table_ref, picked[(n + 1) % 2])
            at = pl.ds(pl.multiple_of(part * GATHER, GATHER), GATHER)
            sums_ref[:, at] = latitude_sums(picked[n % 2], weights_ref[:, at], plan.times)


class Plan:
    def __init__(self, kcoef, tm_count, lat_count, times):
        self.tm_count, self.lat_count, self.times = tm_count, lat_count, times
        self.kcoef, self.part_width, self.rows_width = kcoef, kcoef // lat_count, kcoef // tm_count
        self.parts = kcoef // GATHER
        self.half = self.part_width // 2
        self.col_tiles, self.row_tiles, self.panel_tiles = self.half // LANE, self.rows_width // LANE, PANEL // LANE
        self.first_panel = self.col_tiles + self.row_tiles
        self.across = -(-(self.first_panel + self.panel_tiles) // SUB)
        self.slab = (times * SUB, self.across * LANE)
        self.shape = (tm_count * lat_count,) + self.slab
        self.sums_shape = (self.across, tm_count * self.slab[0], LANE)

    def weights_copies(self, legendre_ref, weights_ref, sems):
        width = GROUP * GATHER

        def copy(group):
            own = pl.ds(pl.multiple_of(group * width, width), width)
            return pltpu.make_async_copy(legendre_ref.at[:, own], weights_ref.at[:, own], sems.at[group])

        @pl.loop(0, self.parts // GROUP)
        def _(group):
            copy(group).start()

        return copy

    def spot(self, tile, time):
        low = tile % self.across * LANE
        return time * SUB + tile // self.across, slice(low, low + LANE)

    def pack(self, sums_ref, slab_ref, sent_ref):
        def fill(tile, source, count):
            for n in range(count):
                for t in range(self.times):
                    row, lanes = self.spot(tile + n, t)
                    low = source + n * LANE
                    slab_ref[row : row + 1, lanes] = sums_ref[t : t + 1, low : low + LANE]

        slab_ref[...] = jnp.zeros_like(slab_ref)
        fill(self.first_panel, 0, self.panel_tiles)
        for part in range(self.lat_count):
            for core in range(2):
                fill(0, part * self.part_width + core * self.half, self.col_tiles)
                for owner in range(core, self.tm_count, 2):
                    fill(self.col_tiles, owner * self.rows_width, self.row_tiles)
                    sent_ref[owner * self.lat_count + part] = slab_ref[...].astype(BF16)

    def gather_sums(self, got_ref, slabs_ref):
        rows = self.slab[0]
        for sender in range(self.tm_count):
            first = sender * self.lat_count
            total = got_ref[first].astype(F32)
            for part in range(1, self.lat_count):
                total = total + got_ref[first + part].astype(F32)
            for n in range(self.across):
                slabs_ref[n, sender * rows : (sender + 1) * rows, :] = total[:, n * LANE : (n + 1) * LANE]

    def tile(self, slabs_ref, tile):
        pieces = []
        for t in range(self.times):
            row = t * SUB + tile // self.across
            pieces.append(slabs_ref[tile % self.across, pl.ds(row, self.tm_count, stride=self.slab[0]), :])
        return jnp.concatenate(pieces, axis=0).astype(BF16).astype(F32)

    def unpack(self, got):
        split_shape = (self.tm_count, self.lat_count, self.times, SUB * self.across * LANE)
        total = got.astype(F32).reshape(split_shape).sum(axis=1).astype(BF16).astype(F32)
        return total.transpose(1, 0, 2).reshape(self.times * self.tm_count, -1)


def spectra_kernel(plan, scale, column_ref, fields_ref, basis_ref, legendre_ref, sent_ref,
                   table_ref, fields_buf, basis_buf, weights_ref, lines_ref, even_ref, odd_ref, sums_ref, slab_ref,
                   fields_sem, basis_sem, weights_sem):
    times, lats, nlon = fields_ref.shape
    pieces = -(-lats // LANE)
    rows = nlon // TRANSFORMS
    fields_copy = pltpu.make_async_copy(fields_ref, fields_buf, fields_sem)
    fields_copy.start()
    basis_copies = []
    for step in range(TRANSFORMS):
        part = pl.ds(step * rows, rows)
        copy = pltpu.make_async_copy(basis_ref.at[part, :], basis_buf.at[part, :], basis_sem.at[step])
        copy.start()
        basis_copies.append(copy)
    weights_copy = plan.weights_copies(legendre_ref, weights_ref, weights_sem)
    lines_ref[...] = jnp.zeros_like(lines_ref)
    fields_copy.wait()
    for t in range(times):
        lines_ref[pieces * LANE * t : pieces * LANE * t + lats, :] = fields_buf[t]
    for step in range(TRANSFORMS):
        basis_copies[step].wait()
        spectra = scale * lax.dot_general(
            basis_buf[step * rows : (step + 1) * rows, :], lines_ref[...], (((1,), (1,)), ((), ())),
            preferred_element_type=F32,
        )
        for s in range(times * pieces):
            table_ref[pl.ds(step * rows * SUB + s, rows, stride=SUB), :] = spectra[:, LANE * s : LANE * (s + 1)]
    contract(plan, column_ref, table_ref, weights_ref, sums_ref, even_ref, odd_ref, weights_copy)
    plan.pack(sums_ref, slab_ref, sent_ref)


def in_hbm(value):
    return pltpu.with_memory_space_constraint(value, pltpu.HBM)


def spot_in(space):
    return pl.BlockSpec(memory_space=space)


def spectra_and_contract(plan, fields, basis, column, legendre):
    times, lats, nlon = fields.shape
    pieces = -(-lats // LANE)
    return pl.pallas_call(
        functools.partial(spectra_kernel, plan, 1.0 / math.sqrt(nlon)),
        in_specs=[spot_in(pltpu.SMEM), spot_in(pltpu.HBM), spot_in(pltpu.HBM), spot_in(pltpu.HBM)],
        out_specs=spot_in(pltpu.VMEM),
        out_shape=jax.ShapeDtypeStruct(plan.shape, BF16),
        scratch_shapes=[
            pltpu.VMEM((nlon * SUB, LANE), F32),
            pltpu.VMEM(fields.shape, BF16),
            pltpu.VMEM(basis.shape, BF16),
            pltpu.VMEM((lats, plan.kcoef), BF16),
            pltpu.VMEM((times * pieces * LANE, nlon), BF16),
            pltpu.VMEM((GATHER * SUB, LANE), F32),
            pltpu.VMEM((GATHER * SUB, LANE), F32),
            pltpu.VMEM((times, plan.kcoef), F32),
            pltpu.VMEM(plan.slab, F32),
            pltpu.SemaphoreType.DMA(()),
            pltpu.SemaphoreType.DMA((TRANSFORMS,)),
            pltpu.SemaphoreType.DMA((plan.parts // GROUP,)),
        ],
        compiler_params=pltpu.CompilerParams(vmem_limit_bytes=SPECTRA_VMEM),
        cost_estimate=pl.CostEstimate(flops=12 << 30, bytes_accessed=8 << 20, transcendentals=0),
        name="spectra_and_contract",
    )(column, in_hbm(fields), in_hbm(basis), in_hbm(legendre))


def split(value, pieces):
    out = []
    for _ in range(pieces):
        piece = value.astype(BF16)
        out.append(piece)
        value = value - piece.astype(F32)
    return out


def panel_kernel(plan, got_ref, lam_ref, w_ref, diag_ref, inverse_ref, slabs_ref, q_ref, g_ref, y_ref, x_ref, z_ref):
    nt = w_ref.shape[0]
    lanes = PANEL + LANE
    plan.gather_sums(got_ref, slabs_ref)
    coef = jnp.concatenate(
        [plan.tile(slabs_ref, plan.first_panel + n) for n in range(plan.panel_tiles)], axis=1
    )
    lam = lam_ref[...]
    scaled = coef / lam
    starts, total = [], 0
    for r in range(nt):
        low = r // 8 * 8
        z_ref[total : total + nt - low, :] = coef[low:, :] * scaled[r : r + 1, :]
        starts.append(total)
        total += nt - low
    ids = lax.broadcasted_iota(jnp.int32, (PANEL, lanes), 0)
    upto = lax.broadcasted_iota(jnp.int32, (PANEL, lanes), 1)
    tri = jnp.where(ids < upto, 1.0, 0.0).astype(BF16)
    prefix = 0.0
    for piece in split(z_ref[...], 3)[::-1]:
        prefix = prefix + jnp.dot(piece, tri, preferred_element_type=F32)
    q_ref[...] = prefix
    y_ref[:, :PANEL] = coef
    eye = lax.broadcasted_iota(jnp.int32, (nt, LANE), 0) == lax.broadcasted_iota(jnp.int32, (nt, LANE), 1)
    y_ref[:, PANEL:] = jnp.where(eye, 1.0, 0.0)
    inverses = []
    for r in range(nt):
        low = r // 8 * 8
        place = low + lax.broadcasted_iota(jnp.int32, (nt - low, lanes), 0)
        row = q_ref[starts[r] : starts[r] + nt - low, :] + jnp.where(place == r, float(nt), 0.0)
        for p in range(r):
            base = starts[p] + low - p // 8 * 8
            factor = g_ref[starts[p] + r - p // 8 * 8 : starts[p] + r - p // 8 * 8 + 1, :]
            row = row - factor * q_ref[base : base + nt - low, :]
        q_ref[starts[r] : starts[r] + nt - low, :] = row
        inv = 1.0 / row[r - low : r - low + 1, :]
        inverses.append(inv)
        ratio = jnp.where(place > r, row * inv, 0.0)
        g_ref[starts[r] : starts[r] + nt - low, :] = ratio
        y_ref[low:, :] = y_ref[low:, :] - ratio * y_ref[r : r + 1, :]
    x_ref[...] = jnp.zeros_like(x_ref)
    for r in range(nt - 1, -1, -1):
        low = r // 8 * 8
        ratio = g_ref[starts[r] : starts[r] + nt - low, :]
        tail = jnp.sum(ratio * x_ref[low:, :], axis=0, keepdims=True)
        x_ref[r : r + 1, :] = y_ref[r : r + 1, :] * inverses[r] - tail
    solved = x_ref[:, :PANEL]
    pivot = jnp.sqrt(lam + jnp.sum(coef * solved, axis=0, keepdims=True))
    w_ref[...] = solved / pivot
    diag_ref[...] = lam / pivot
    inverse_ref[...] = x_ref[:, PANEL:]


def panel_small(plan, got, lam):
    nt = plan.times * plan.tm_count
    rows = sum(nt - r // 8 * 8 for r in range(nt))
    lanes = PANEL + LANE
    return pl.pallas_call(
        functools.partial(panel_kernel, plan),
        grid=(1,),
        in_specs=[
            pl.BlockSpec(plan.shape, lambda i: (0, 0, 0)),
            pl.BlockSpec((1, PANEL), lambda i: (0, 0)),
        ],
        out_specs=[
            pl.BlockSpec((nt, PANEL), lambda i: (0, 0)),
            pl.BlockSpec((1, PANEL), lambda i: (0, 0)),
            pl.BlockSpec((nt, LANE), lambda i: (0, 0)),
        ],
        out_shape=[
            jax.ShapeDtypeStruct((nt, PANEL), F32),
            jax.ShapeDtypeStruct((1, PANEL), F32),
            jax.ShapeDtypeStruct((nt, LANE), F32),
        ],
        scratch_shapes=[
            pltpu.VMEM(plan.sums_shape, F32),
            pltpu.VMEM((rows, lanes), F32),
            pltpu.VMEM((rows, lanes), F32),
            pltpu.VMEM((nt, lanes), F32),
            pltpu.VMEM((nt, lanes), F32),
            pltpu.VMEM((rows, PANEL), F32),
        ],
        compiler_params=pltpu.CompilerParams(vmem_limit_bytes=SMALL_VMEM),
        cost_estimate=pl.CostEstimate(flops=4 << 30, bytes_accessed=1 << 18, transcendentals=0),
        name="panel_small",
    )(got, lam)


def panel_large(plan, got, lam):
    low = plan.first_panel * LANE
    coef, lam = plan.unpack(got)[:, low : low + PANEL], lam[:, :PANEL]
    nt = coef.shape[0]
    gram = jnp.dot(coef.T, coef, precision=lax.Precision.HIGHEST) / nt + jnp.diag(lam[0])
    factor = jnp.linalg.cholesky(gram)
    solved = jax.scipy.linalg.solve_triangular(factor, coef.T, lower=True)
    w = solved.T / nt
    rest = jnp.eye(nt, dtype=F32) / nt - jnp.dot(w, w.T, precision=lax.Precision.HIGHEST)
    pivot = jnp.diagonal(factor)[None, :]
    pad = -(-nt // LANE) * LANE - nt
    return w, pivot - jnp.sum(coef * w, axis=0, keepdims=True), jnp.pad(rest, ((0, 0), (0, pad)))


def stack_pieces(value):
    high, low = split(value, 2)
    return jnp.concatenate([high.astype(F32), low.astype(F32)], axis=0).astype(BF16)


def twice(value):
    return jnp.concatenate([value, value], axis=0).astype(BF16)


def contract_times(left, right):
    return lax.dot_general(left, right, (((0,), (0,)), ((), ())), preferred_element_type=F32)


def times_first(value):
    return value.astype(F32).T.astype(BF16)


def tile_kernel(plan, own_ref, other_ref, w_ref, diag_ref, lam_ref, inverse_ref, out_ref,
                own_slabs, other_slabs, rows_ref, cols_ref, left_ref, left_panel_ref, tiles_ref, out_sem):
    height = out_ref.shape[0]
    nt = rows_ref.shape[0]
    tm_index = lax.axis_index("tm")
    row_start = tm_index * height
    first_col = lax.axis_index("lat") * cols_ref.shape[1]
    in_panel_rows = row_start < PANEL

    for got_ref, slabs_ref, core in (
        (own_ref, own_slabs, lax.rem(tm_index, 2)),
        (other_ref, other_slabs, 1 - lax.rem(tm_index, 2)),
    ):
        plan.gather_sums(got_ref, slabs_ref)
        for n in range(plan.col_tiles):
            low = pl.multiple_of(core * plan.half + n * LANE, LANE)
            cols_ref[:, pl.ds(low, LANE)] = plan.tile(slabs_ref, n)
    for n in range(plan.row_tiles):
        rows_ref[:, n * LANE : (n + 1) * LANE] = plan.tile(own_slabs, plan.col_tiles + n)
    left_ref[...] = times_first(twice(rows_ref[...]))

    @pl.when(in_panel_rows)
    def _():
        low = pl.multiple_of(jnp.minimum(row_start, PANEL - height), LANE)
        left_panel_ref[...] = times_first(stack_pieces(w_ref[:, pl.ds(low, height)]))

    def product(left, right):
        return jnp.dot(left, right, preferred_element_type=F32)

    def copy(step):
        own = pl.ds(pl.multiple_of(step * WIDE, WIDE), WIDE)
        return pltpu.make_async_copy(tiles_ref.at[step], out_ref.at[:, own], out_sem.at[step])

    @pl.loop(0, cols_ref.shape[1] // WIDE)
    def _(step):
        col_start = first_col + step * WIDE
        in_panel_cols = col_start < PANEL
        on_diagonal = (row_start < col_start + WIDE) & (col_start < row_start + height)
        own = pl.ds(pl.multiple_of(step * WIDE, WIDE), WIDE)
        out = tiles_ref.at[step]

        def ids():
            rows = row_start + lax.broadcasted_iota(jnp.int32, (height, WIDE), 0)
            return rows, col_start + lax.broadcasted_iota(jnp.int32, (height, WIDE), 1)

        @pl.when(in_panel_cols)
        def _():
            out[...] = product(left_ref[...], stack_pieces(w_ref[:, own_panel(step)]))

        @pl.when(in_panel_cols & in_panel_rows)
        def _():
            row_ids, col_ids = ids()
            diag = jnp.where(row_ids == col_ids, diag_ref[:, own_panel(step)], 0.0)
            out[...] = jnp.where(row_ids >= col_ids, out[...], 0.0) + diag

        @pl.when(jnp.logical_not(in_panel_cols) & in_panel_rows)
        def _():
            out[...] = product(left_panel_ref[...], twice(cols_ref[:, own]))

        @pl.when(jnp.logical_not(in_panel_cols) & jnp.logical_not(in_panel_rows))
        def _():
            turned = contract_times(stack_pieces(inverse_ref[:, :nt]), twice(cols_ref[:, own]))
            out[...] = product(left_ref[...], stack_pieces(turned))

            @pl.when(on_diagonal)
            def _():
                row_ids, col_ids = ids()
                lam = lam_ref[:, pl.ds(pl.multiple_of(col_start, LANE), WIDE)]
                out[...] += jnp.where(row_ids == col_ids, lam, 0.0)

        copy(step).start()

    @pl.loop(0, cols_ref.shape[1] // WIDE)
    def _(step):
        copy(step).wait()


def own_panel(step):
    return pl.ds(pl.multiple_of(jnp.minimum(step * WIDE, PANEL - WIDE), WIDE), WIDE)


def out_tile(plan, own, other, w, diag, lam, inverse):
    nt, height, width = plan.times * plan.tm_count, plan.rows_width, plan.part_width
    return pl.pallas_call(
        functools.partial(tile_kernel, plan),
        in_specs=[spot_in(pltpu.VMEM)] * 6,
        out_specs=spot_in(pltpu.HBM),
        out_shape=jax.ShapeDtypeStruct((height, width), F32),
        scratch_shapes=[
            pltpu.VMEM(plan.sums_shape, F32),
            pltpu.VMEM(plan.sums_shape, F32),
            pltpu.VMEM((nt, height), F32),
            pltpu.VMEM((nt, width), F32),
            pltpu.VMEM((height, 2 * nt), BF16),
            pltpu.VMEM((height, 2 * nt), BF16),
            pltpu.VMEM((width // WIDE, height, WIDE), F32),
            pltpu.SemaphoreType.DMA((width // WIDE,)),
        ],
        compiler_params=pltpu.CompilerParams(vmem_limit_bytes=SMALL_VMEM),
        cost_estimate=pl.CostEstimate(
            flops=4 * nt * height * width, bytes_accessed=4 * height * width, transcendentals=0
        ),
        name="out_tile",
    )(own, other, w, diag, lam, inverse)


def on_device(basis, fields, legendre, order_table, window_start, ridge):
    times, _, nlon = fields.shape
    kcoef = legendre.shape[1]
    tm_count, lat_count = lax.axis_size("tm"), lax.axis_size("lat")
    window = lax.dynamic_slice_in_dim(order_table, window_start[0], kcoef, 1)
    degree = window[0:1]
    column = SUB * (window[1] + nlon // 2 * window[2])
    lam = ridge[0] * (1.0 + (degree * (degree + 1)).astype(F32) / float(LMAX * (LMAX + 1)))
    plan = Plan(kcoef, tm_count, lat_count, times)
    sent = spectra_and_contract(plan, fields, basis, column, legendre)
    own = lax.all_to_all(sent, ("tm", "lat"), 0, 0, tiled=True)
    other = lax.ppermute(own, "tm", [(i, i ^ 1) for i in range(tm_count)])
    small = times * tm_count <= LANE // 4
    w, diag, inverse = (panel_small if small else panel_large)(plan, own, lam)
    return out_tile(plan, own, other, w, diag, lam, inverse)


def solution(mesh):
    def run(fields, legendre, order_table, window_start, ridge):
        basis = jnp.asarray(basis_table(fields.shape[2]))
        placed = (P(), P("tm", "lat", None), P("lat", None), P(), P(), P())
        body = jax.shard_map(on_device, mesh=mesh, in_specs=placed, out_specs=P("tm", "lat"), check_vma=False)
        return body(basis, fields, legendre, order_table, window_start, ridge)

    return run
```

```python
import functools
import math

import jax
import jax.numpy as jnp
import ml_dtypes
import numpy as np
from jax import lax
from jax.experimental import pallas as pl
from jax.experimental.pallas import tpu as pltpu
from jax.sharding import PartitionSpec as P

LMAX = 720
PANEL = 512
LANE = 128
SUB = 8
GATHER = 256
GROUP = 4
TRANSFORMS = 3
WIDE = 512
SPECTRA_VMEM = 36 * 1024 * 1024
SMALL_VMEM = 20 * 1024 * 1024
F32 = jnp.float32
BF16 = jnp.bfloat16


def basis_table(nlon):
    half = nlon // 2
    column = np.arange(nlon, dtype=np.int64)[:, None]
    longitude = np.arange(nlon, dtype=np.int64)[None, :]
    phase = (column % half * longitude % nlon).astype(np.float32) * np.float32(2.0 * math.pi / nlon)
    return np.where(column < half, np.cos(phase), np.sin(phase)).astype(ml_dtypes.bfloat16)


def pick_rows(column_ref, start, table_ref, picked_ref):
    row = start // LANE
    for j in range(GATHER):
        group = pl.multiple_of(column_ref[row + j // LANE, j % LANE], SUB)
        picked_ref[SUB * j : SUB * (j + 1), :] = table_ref[pl.ds(group, SUB), :]


def latitude_sums(picked_ref, weights, times):
    lats = weights.shape[0]
    pieces = -(-lats // LANE)
    picked = [picked_ref[pl.ds(s, GATHER, stride=SUB), :] for s in range(times * pieces)]
    value = jnp.concatenate(
        [jnp.concatenate(picked[pieces * t : pieces * (t + 1)], axis=1) for t in range(times)], axis=0
    )
    spare = jnp.zeros((pieces * LANE - lats, GATHER), BF16)
    every = jnp.dot(value.astype(BF16), jnp.concatenate([weights, spare], axis=0), preferred_element_type=F32)
    shape = (LANE, LANE)
    eye = lax.broadcasted_iota(jnp.int32, shape, 0) == lax.broadcasted_iota(jnp.int32, shape, 1)
    sums = []
    for t in range(times):
        own = []
        for low in range(0, GATHER, LANE):
            square = every[t * GATHER + low : t * GATHER + low + LANE, low : low + LANE]
            own.append(jnp.sum(jnp.where(eye, square, 0.0), axis=0, keepdims=True))
        sums.append(jnp.concatenate(own, axis=1))
    return jnp.concatenate(sums, axis=0)


def contract(plan, column_ref, table_ref, weights_ref, sums_ref, even_ref, odd_ref, weights_copy):
    picked = [even_ref, odd_ref]

    def place(part):
        return jnp.minimum(part, plan.parts - 1) * GATHER

    pick_rows(column_ref, 0, table_ref, even_ref)

    @pl.loop(0, plan.parts // GROUP)
    def _(group):
        weights_copy(group).wait()
        for n in range(GROUP):
            part = group * GROUP + n
            pick_rows(column_ref, place(part + 1), table_ref, picked[(n + 1) % 2])
            at = pl.ds(pl.multiple_of(part * GATHER, GATHER), GATHER)
            sums_ref[:, at] = latitude_sums(picked[n % 2], weights_ref[:, at], plan.times)


class Plan:
    def __init__(self, kcoef, tm_count, lat_count, times):
        self.tm_count, self.lat_count, self.times = tm_count, lat_count, times
        self.kcoef, self.part_width, self.rows_width = kcoef, kcoef // lat_count, kcoef // tm_count
        self.parts = kcoef // GATHER
        self.half = self.part_width // 2
        self.col_tiles, self.row_tiles, self.panel_tiles = self.half // LANE, self.rows_width // LANE, PANEL // LANE
        self.first_panel = self.col_tiles + self.row_tiles
        self.across = -(-(self.first_panel + self.panel_tiles) // SUB)
        self.slab = (times * SUB, self.across * LANE)
        self.shape = (tm_count * lat_count,) + self.slab
        self.sums_shape = (self.across, tm_count * self.slab[0], LANE)

    def weights_copies(self, legendre_ref, weights_ref, sems):
        width = GROUP * GATHER

        def copy(group):
            own = pl.ds(pl.multiple_of(group * width, width), width)
            return pltpu.make_async_copy(legendre_ref.at[:, own], weights_ref.at[:, own], sems.at[group])

        @pl.loop(0, self.parts // GROUP)
        def _(group):
            copy(group).start()

        return copy

    def spot(self, tile, time):
        low = tile % self.across * LANE
        return time * SUB + tile // self.across, slice(low, low + LANE)

    def pack(self, sums_ref, slab_ref, sent_ref):
        def fill(tile, source, count):
            for n in range(count):
                for t in range(self.times):
                    row, lanes = self.spot(tile + n, t)
                    low = source + n * LANE
                    slab_ref[row : row + 1, lanes] = sums_ref[t : t + 1, low : low + LANE]

        slab_ref[...] = jnp.zeros_like(slab_ref)
        fill(self.first_panel, 0, self.panel_tiles)
        for part in range(self.lat_count):
            for core in range(2):
                fill(0, part * self.part_width + core * self.half, self.col_tiles)
                for owner in range(core, self.tm_count, 2):
                    fill(self.col_tiles, owner * self.rows_width, self.row_tiles)
                    sent_ref[owner * self.lat_count + part] = slab_ref[...].astype(BF16)

    def gather_sums(self, got_ref, slabs_ref):
        rows = self.slab[0]
        for sender in range(self.tm_count):
            first = sender * self.lat_count
            total = got_ref[first].astype(F32)
            for part in range(1, self.lat_count):
                total = total + got_ref[first + part].astype(F32)
            for n in range(self.across):
                slabs_ref[n, sender * rows : (sender + 1) * rows, :] = total[:, n * LANE : (n + 1) * LANE]

    def tile(self, slabs_ref, tile):
        pieces = []
        for t in range(self.times):
            row = t * SUB + tile // self.across
            pieces.append(slabs_ref[tile % self.across, pl.ds(row, self.tm_count, stride=self.slab[0]), :])
        return jnp.concatenate(pieces, axis=0).astype(BF16).astype(F32)

    def unpack(self, got):
        split_shape = (self.tm_count, self.lat_count, self.times, SUB * self.across * LANE)
        total = got.astype(F32).reshape(split_shape).sum(axis=1).astype(BF16).astype(F32)
        return total.transpose(1, 0, 2).reshape(self.times * self.tm_count, -1)


def window_of(value, start, length, lines_ref):
    for n in range(value.shape[1] // LANE):
        lines_ref[n : n + 1, :] = value[:, n * LANE : (n + 1) * LANE]
    over = lax.rem(start, LANE)
    lines_ref[...] = pltpu.roll(lines_ref[...], lax.rem(LANE - over, LANE), 1)
    first = lines_ref[pl.ds(start // LANE, length // LANE), :]
    second = lines_ref[pl.ds(start // LANE + 1, length // LANE), :]
    lane = lax.broadcasted_iota(jnp.int32, first.shape, 1)
    return jnp.where(lane < LANE - over, first, second)


def spectra_kernel(plan, scale, start_ref, ridge_ref, order_ref, fields_ref, basis_ref, legendre_ref, sent_ref,
                   lam_ref, order_buf, index_ref, window_ref, column_ref, table_ref, fields_buf, basis_buf, weights_ref, lines_ref, even_ref, odd_ref, sums_ref, slab_ref,
                   order_sem, column_sem, fields_sem, basis_sem, weights_sem):
    times, lats, nlon = fields_ref.shape
    pieces = -(-lats // LANE)
    rows = nlon // TRANSFORMS
    order_copy = pltpu.make_async_copy(order_ref, order_buf, order_sem)
    order_copy.start()
    fields_copy = pltpu.make_async_copy(fields_ref, fields_buf, fields_sem)
    fields_copy.start()
    basis_copies = []
    for step in range(TRANSFORMS):
        part = pl.ds(step * rows, rows)
        copy = pltpu.make_async_copy(basis_ref.at[part, :], basis_buf.at[part, :], basis_sem.at[step])
        copy.start()
        basis_copies.append(copy)
    for t in range(times):
        end = pieces * LANE * (t + 1)
        low = end - LANE
        lines_ref[low:end, :] = jnp.zeros((LANE, nlon), BF16)
    order_copy.wait()
    start = start_ref[0]
    column = SUB * (order_buf[1:2, :] + nlon // 2 * order_buf[2:3, :])
    window_ref[...] = window_of(column, start, plan.kcoef, index_ref)
    column_copy = pltpu.make_async_copy(window_ref, column_ref, column_sem)
    column_copy.start()
    degree = window_of(order_buf[0:1, :], start, plan.kcoef, index_ref)
    lam = ridge_ref[0] * (1.0 + (degree * (degree + 1)).astype(F32) / float(LMAX * (LMAX + 1)))
    for n in range(plan.kcoef // LANE):
        lam_ref[:, n * LANE : (n + 1) * LANE] = lam[n : n + 1, :]
    fields_copy.wait()
    for t in range(times):
        lines_ref[pieces * LANE * t : pieces * LANE * t + lats, :] = fields_buf[t]
    basis_copies[0].wait()
    weights_copy = plan.weights_copies(legendre_ref, weights_ref, weights_sem)
    for step in range(TRANSFORMS):
        if step > 0:
            basis_copies[step].wait()
        spectra = scale * lax.dot_general(
            basis_buf[step * rows : (step + 1) * rows, :], lines_ref[...], (((1,), (1,)), ((), ())),
            preferred_element_type=F32,
        )
        for s in range(times * pieces):
            table_ref[pl.ds(step * rows * SUB + s, rows, stride=SUB), :] = spectra[:, LANE * s : LANE * (s + 1)]
    column_copy.wait()
    contract(plan, column_ref, table_ref, weights_ref, sums_ref, even_ref, odd_ref, weights_copy)
    plan.pack(sums_ref, slab_ref, sent_ref)


def in_hbm(value):
    return pltpu.with_memory_space_constraint(value, pltpu.HBM)


def spot_in(space):
    return pl.BlockSpec(memory_space=space)


def spectra_and_contract(plan, start, ridge, order, fields, basis, legendre):
    times, lats, nlon = fields.shape
    entries = order.shape[1] // LANE
    pieces = -(-lats // LANE)
    return pl.pallas_call(
        functools.partial(spectra_kernel, plan, 1.0 / math.sqrt(nlon)),
        in_specs=[spot_in(pltpu.SMEM)] * 2 + [spot_in(pltpu.HBM)] * 4,
        out_specs=[spot_in(pltpu.VMEM)] * 2,
        out_shape=[jax.ShapeDtypeStruct(plan.shape, BF16), jax.ShapeDtypeStruct((1, plan.kcoef), F32)],
        scratch_shapes=[
            pltpu.VMEM(order.shape, jnp.int32),
            pltpu.VMEM((entries + SUB, LANE), jnp.int32),
            pltpu.VMEM((plan.kcoef // LANE, LANE), jnp.int32),
            pltpu.SMEM((plan.kcoef // LANE, LANE), jnp.int32),
            pltpu.VMEM((nlon * SUB, LANE), F32),
            pltpu.VMEM(fields.shape, BF16),
            pltpu.VMEM(basis.shape, BF16),
            pltpu.VMEM((lats, plan.kcoef), BF16),
            pltpu.VMEM((times * pieces * LANE, nlon), BF16),
            pltpu.VMEM((GATHER * SUB, LANE), F32),
            pltpu.VMEM((GATHER * SUB, LANE), F32),
            pltpu.VMEM((times, plan.kcoef), F32),
            pltpu.VMEM(plan.slab, F32),
            pltpu.SemaphoreType.DMA(()),
            pltpu.SemaphoreType.DMA(()),
            pltpu.SemaphoreType.DMA(()),
            pltpu.SemaphoreType.DMA((TRANSFORMS,)),
            pltpu.SemaphoreType.DMA((plan.parts // GROUP,)),
        ],
        compiler_params=pltpu.CompilerParams(vmem_limit_bytes=SPECTRA_VMEM),
        cost_estimate=pl.CostEstimate(flops=12 << 30, bytes_accessed=8 << 20, transcendentals=0),
        name="spectra_and_contract",
    )(start, ridge, in_hbm(order), in_hbm(fields), in_hbm(basis), in_hbm(legendre))


def split(value, pieces):
    out = []
    for _ in range(pieces):
        piece = value.astype(BF16)
        out.append(piece)
        value = value - piece.astype(F32)
    return out


def panel_kernel(plan, got_ref, lam_ref, w_ref, diag_ref, inverse_ref, slabs_ref, q_ref, g_ref, y_ref, x_ref, z_ref):
    nt = w_ref.shape[0]
    lanes = PANEL + LANE
    plan.gather_sums(got_ref, slabs_ref)
    coef = jnp.concatenate(
        [plan.tile(slabs_ref, plan.first_panel + n) for n in range(plan.panel_tiles)], axis=1
    )
    lam = lam_ref[...]
    scaled = coef / lam
    starts, total = [], 0
    for r in range(nt):
        low = r // 8 * 8
        z_ref[total : total + nt - low, :] = coef[low:, :] * scaled[r : r + 1, :]
        starts.append(total)
        total += nt - low
    ids = lax.broadcasted_iota(jnp.int32, (PANEL, lanes), 0)
    upto = lax.broadcasted_iota(jnp.int32, (PANEL, lanes), 1)
    tri = jnp.where(ids < upto, 1.0, 0.0).astype(BF16)
    prefix = 0.0
    for piece in split(z_ref[...], 3)[::-1]:
        prefix = prefix + jnp.dot(piece, tri, preferred_element_type=F32)
    q_ref[...] = prefix
    y_ref[:, :PANEL] = coef
    eye = lax.broadcasted_iota(jnp.int32, (nt, LANE), 0) == lax.broadcasted_iota(jnp.int32, (nt, LANE), 1)
    y_ref[:, PANEL:] = jnp.where(eye, 1.0, 0.0)
    inverses = []
    for r in range(nt):
        low = r // 8 * 8
        place = low + lax.broadcasted_iota(jnp.int32, (nt - low, lanes), 0)
        row = q_ref[starts[r] : starts[r] + nt - low, :] + jnp.where(place == r, float(nt), 0.0)
        for p in range(r):
            base = starts[p] + low - p // 8 * 8
            factor = g_ref[starts[p] + r - p // 8 * 8 : starts[p] + r - p // 8 * 8 + 1, :]
            row = row - factor * q_ref[base : base + nt - low, :]
        q_ref[starts[r] : starts[r] + nt - low, :] = row
        inv = 1.0 / row[r - low : r - low + 1, :]
        inverses.append(inv)
        ratio = jnp.where(place > r, row * inv, 0.0)
        g_ref[starts[r] : starts[r] + nt - low, :] = ratio
        y_ref[low:, :] = y_ref[low:, :] - ratio * y_ref[r : r + 1, :]
    x_ref[...] = jnp.zeros_like(x_ref)
    for r in range(nt - 1, -1, -1):
        low = r // 8 * 8
        ratio = g_ref[starts[r] : starts[r] + nt - low, :]
        tail = jnp.sum(ratio * x_ref[low:, :], axis=0, keepdims=True)
        x_ref[r : r + 1, :] = y_ref[r : r + 1, :] * inverses[r] - tail
    solved = x_ref[:, :PANEL]
    pivot = jnp.sqrt(lam + jnp.sum(coef * solved, axis=0, keepdims=True))
    w_ref[...] = solved / pivot
    diag_ref[...] = lam / pivot
    inverse_ref[...] = x_ref[:, PANEL:]


def panel_small(plan, got, lam):
    nt = plan.times * plan.tm_count
    rows = sum(nt - r // 8 * 8 for r in range(nt))
    lanes = PANEL + LANE
    return pl.pallas_call(
        functools.partial(panel_kernel, plan),
        grid=(1,),
        in_specs=[
            pl.BlockSpec(plan.shape, lambda i: (0, 0, 0)),
            pl.BlockSpec((1, PANEL), lambda i: (0, 0)),
        ],
        out_specs=[
            pl.BlockSpec((nt, PANEL), lambda i: (0, 0)),
            pl.BlockSpec((1, PANEL), lambda i: (0, 0)),
            pl.BlockSpec((nt, LANE), lambda i: (0, 0)),
        ],
        out_shape=[
            jax.ShapeDtypeStruct((nt, PANEL), F32),
            jax.ShapeDtypeStruct((1, PANEL), F32),
            jax.ShapeDtypeStruct((nt, LANE), F32),
        ],
        scratch_shapes=[
            pltpu.VMEM(plan.sums_shape, F32),
            pltpu.VMEM((rows, lanes), F32),
            pltpu.VMEM((rows, lanes), F32),
            pltpu.VMEM((nt, lanes), F32),
            pltpu.VMEM((nt, lanes), F32),
            pltpu.VMEM((rows, PANEL), F32),
        ],
        compiler_params=pltpu.CompilerParams(vmem_limit_bytes=SMALL_VMEM),
        cost_estimate=pl.CostEstimate(flops=4 << 30, bytes_accessed=1 << 18, transcendentals=0),
        name="panel_small",
    )(got, lam)


def panel_large(plan, got, lam):
    low = plan.first_panel * LANE
    coef, lam = plan.unpack(got)[:, low : low + PANEL], lam[:, :PANEL]
    nt = coef.shape[0]
    gram = jnp.dot(coef.T, coef, precision=lax.Precision.HIGHEST) / nt + jnp.diag(lam[0])
    factor = jnp.linalg.cholesky(gram)
    solved = jax.scipy.linalg.solve_triangular(factor, coef.T, lower=True)
    w = solved.T / nt
    rest = jnp.eye(nt, dtype=F32) / nt - jnp.dot(w, w.T, precision=lax.Precision.HIGHEST)
    pivot = jnp.diagonal(factor)[None, :]
    pad = -(-nt // LANE) * LANE - nt
    return w, pivot - jnp.sum(coef * w, axis=0, keepdims=True), jnp.pad(rest, ((0, 0), (0, pad)))


def stack_pieces(value):
    high, low = split(value, 2)
    return jnp.concatenate([high.astype(F32), low.astype(F32)], axis=0).astype(BF16)


def twice(value):
    return jnp.concatenate([value, value], axis=0).astype(BF16)


def contract_times(left, right):
    return lax.dot_general(left, right, (((0,), (0,)), ((), ())), preferred_element_type=F32)


def times_first(value):
    return value.astype(F32).T.astype(BF16)


def tile_kernel(plan, own_ref, other_ref, w_ref, diag_ref, lam_ref, inverse_ref, out_ref,
                own_slabs, other_slabs, rows_ref, cols_ref, left_ref, left_main_ref, right_ref, tiles_ref, out_sem):
    height = out_ref.shape[0]
    nt = rows_ref.shape[0]
    tm_index = lax.axis_index("tm")
    row_start = tm_index * height
    first_col = lax.axis_index("lat") * cols_ref.shape[1]
    in_panel_rows = row_start < PANEL

    for got_ref, slabs_ref, core in (
        (own_ref, own_slabs, lax.rem(tm_index, 2)),
        (other_ref, other_slabs, 1 - lax.rem(tm_index, 2)),
    ):
        plan.gather_sums(got_ref, slabs_ref)
        for n in range(plan.col_tiles):
            low = pl.multiple_of(core * plan.half + n * LANE, LANE)
            cols_ref[:, pl.ds(low, LANE)] = plan.tile(slabs_ref, n)
    for n in range(plan.row_tiles):
        rows_ref[:, n * LANE : (n + 1) * LANE] = plan.tile(own_slabs, plan.col_tiles + n)
    left_ref[...] = times_first(twice(rows_ref[...]))

    @pl.when(in_panel_rows)
    def _():
        low = pl.multiple_of(jnp.minimum(row_start, PANEL - height), LANE)
        left_main_ref[...] = times_first(stack_pieces(w_ref[:, pl.ds(low, height)]))
        right_ref[...] = twice(cols_ref[...])

    @pl.when(jnp.logical_not(in_panel_rows))
    def _():
        left_main_ref[...] = left_ref[...]
        turned = contract_times(stack_pieces(inverse_ref[:, :nt]), twice(cols_ref[...]))
        right_ref[...] = stack_pieces(turned)

    @pl.when(first_col < PANEL)
    def _():
        right_ref[:, :PANEL] = stack_pieces(w_ref[...])

    def copy(step):
        own = pl.ds(pl.multiple_of(step * WIDE, WIDE), WIDE)
        return pltpu.make_async_copy(tiles_ref.at[step], out_ref.at[:, own], out_sem.at[step])

    @pl.loop(0, cols_ref.shape[1] // WIDE)
    def _(step):
        col_start = first_col + step * WIDE
        in_panel_cols = col_start < PANEL
        on_diagonal = (row_start < col_start + WIDE) & (col_start < row_start + height)
        own = pl.ds(pl.multiple_of(step * WIDE, WIDE), WIDE)
        out = tiles_ref.at[step]

        def ids():
            rows = row_start + lax.broadcasted_iota(jnp.int32, (height, WIDE), 0)
            return rows, col_start + lax.broadcasted_iota(jnp.int32, (height, WIDE), 1)

        @pl.when(in_panel_cols)
        def _():
            out[...] = jnp.dot(left_ref[...], right_ref[:, own], preferred_element_type=F32)

        @pl.when(jnp.logical_not(in_panel_cols))
        def _():
            out[...] = jnp.dot(left_main_ref[...], right_ref[:, own], preferred_element_type=F32)

        @pl.when(in_panel_cols & in_panel_rows)
        def _():
            row_ids, col_ids = ids()
            diag = jnp.where(row_ids == col_ids, diag_ref[:, own_panel(step)], 0.0)
            out[...] = jnp.where(row_ids >= col_ids, out[...], 0.0) + diag

        @pl.when(on_diagonal & jnp.logical_not(in_panel_rows))
        def _():
            row_ids, col_ids = ids()
            lam = lam_ref[:, pl.ds(pl.multiple_of(col_start, LANE), WIDE)]
            out[...] += jnp.where(row_ids == col_ids, lam, 0.0)

        copy(step).start()

    @pl.loop(0, cols_ref.shape[1] // WIDE)
    def _(step):
        copy(step).wait()


def own_panel(step):
    return pl.ds(pl.multiple_of(jnp.minimum(step * WIDE, PANEL - WIDE), WIDE), WIDE)


def out_tile(plan, own, other, w, diag, lam, inverse):
    nt, height, width = plan.times * plan.tm_count, plan.rows_width, plan.part_width
    return pl.pallas_call(
        functools.partial(tile_kernel, plan),
        in_specs=[spot_in(pltpu.VMEM)] * 6,
        out_specs=spot_in(pltpu.HBM),
        out_shape=jax.ShapeDtypeStruct((height, width), F32),
        scratch_shapes=[
            pltpu.VMEM(plan.sums_shape, F32),
            pltpu.VMEM(plan.sums_shape, F32),
            pltpu.VMEM((nt, height), F32),
            pltpu.VMEM((nt, width), F32),
            pltpu.VMEM((height, 2 * nt), BF16),
            pltpu.VMEM((height, 2 * nt), BF16),
            pltpu.VMEM((2 * nt, width), BF16),
            pltpu.VMEM((width // WIDE, height, WIDE), F32),
            pltpu.SemaphoreType.DMA((width // WIDE,)),
        ],
        compiler_params=pltpu.CompilerParams(vmem_limit_bytes=SMALL_VMEM),
        cost_estimate=pl.CostEstimate(
            flops=4 * nt * height * width, bytes_accessed=4 * height * width, transcendentals=0
        ),
        name="out_tile",
    )(own, other, w, diag, lam, inverse)


def on_device(basis, fields, legendre, order_table, window_start, ridge):
    times = fields.shape[0]
    kcoef = legendre.shape[1]
    tm_count, lat_count = lax.axis_size("tm"), lax.axis_size("lat")
    plan = Plan(kcoef, tm_count, lat_count, times)
    sent, lam = spectra_and_contract(plan, window_start, ridge, order_table, fields, basis, legendre)
    own = lax.all_to_all(sent, ("tm", "lat"), 0, 0, tiled=True)
    other = lax.ppermute(own, "tm", [(i, i ^ 1) for i in range(tm_count)])
    small = times * tm_count <= LANE // 4
    w, diag, inverse = (panel_small if small else panel_large)(plan, own, lam)
    return out_tile(plan, own, other, w, diag, lam, inverse)


def solution(mesh):
    def run(fields, legendre, order_table, window_start, ridge):
        basis = jnp.asarray(basis_table(fields.shape[2]))
        placed = (P(), P("tm", "lat", None), P("lat", None), P(), P(), P())
        body = jax.shard_map(on_device, mesh=mesh, in_specs=placed, out_specs=P("tm", "lat"), check_vma=False)
        return body(basis, fields, legendre, order_table, window_start, ridge)

    return run
```

```python
import functools
import math

import jax
import jax.numpy as jnp
import ml_dtypes
import numpy as np
from jax import lax
from jax.experimental import pallas as pl
from jax.experimental.pallas import tpu as pltpu
from jax.sharding import PartitionSpec as P

LMAX = 720
PANEL = 512
LANE = 128
SUB = 8
GATHER = 256
GROUP = 4
WIDE = 512
SPECTRA_VMEM = 36 * 1024 * 1024
SMALL_VMEM = 20 * 1024 * 1024
F32 = jnp.float32
BF16 = jnp.bfloat16


def basis_table(nlon):
    half = nlon // 2
    column = np.arange(nlon, dtype=np.int64)[:, None]
    longitude = np.arange(nlon, dtype=np.int64)[None, :]
    phase = (column % half * longitude % nlon).astype(np.float32) * np.float32(2.0 * math.pi / nlon)
    return np.where(column < half, np.cos(phase), np.sin(phase)).astype(ml_dtypes.bfloat16)


def pick_rows(column_ref, start, table_ref, picked_ref):
    row = start // LANE
    for j in range(GATHER):
        group = pl.multiple_of(column_ref[row + j // LANE, j % LANE], SUB)
        picked_ref[SUB * j : SUB * (j + 1), :] = table_ref[pl.ds(group, SUB), :]


def latitude_sums(picked_ref, weights, times):
    lats = weights.shape[0]
    pieces = -(-lats // LANE)
    picked = [picked_ref[pl.ds(s, GATHER, stride=SUB), :] for s in range(times * pieces)]
    value = jnp.concatenate(
        [jnp.concatenate(picked[pieces * t : pieces * (t + 1)], axis=1) for t in range(times)], axis=0
    )
    spare = jnp.zeros((pieces * LANE - lats, GATHER), BF16)
    every = jnp.dot(value.astype(BF16), jnp.concatenate([weights, spare], axis=0), preferred_element_type=F32)
    shape = (LANE, LANE)
    eye = lax.broadcasted_iota(jnp.int32, shape, 0) == lax.broadcasted_iota(jnp.int32, shape, 1)
    sums = []
    for t in range(times):
        own = []
        for low in range(0, GATHER, LANE):
            square = every[t * GATHER + low : t * GATHER + low + LANE, low : low + LANE]
            own.append(jnp.sum(jnp.where(eye, square, 0.0), axis=0, keepdims=True))
        sums.append(jnp.concatenate(own, axis=1))
    return jnp.concatenate(sums, axis=0)


def contract(plan, column_ref, table_ref, weights_ref, sums_ref, even_ref, odd_ref, weights_copy):
    picked = [even_ref, odd_ref]

    def place(part):
        return jnp.minimum(part, plan.parts - 1) * GATHER

    pick_rows(column_ref, 0, table_ref, even_ref)

    @pl.loop(0, plan.parts // GROUP)
    def _(group):
        weights_copy(group).wait()
        for n in range(GROUP):
            part = group * GROUP + n
            pick_rows(column_ref, place(part + 1), table_ref, picked[(n + 1) % 2])
            at = pl.ds(pl.multiple_of(part * GATHER, GATHER), GATHER)
            sums_ref[:, at] = latitude_sums(picked[n % 2], weights_ref[:, at], plan.times)


class Plan:
    def __init__(self, kcoef, tm_count, lat_count, times):
        self.tm_count, self.lat_count, self.times = tm_count, lat_count, times
        self.kcoef, self.part_width, self.rows_width = kcoef, kcoef // lat_count, kcoef // tm_count
        self.parts = kcoef // GATHER
        self.half = self.part_width // 2
        self.col_tiles, self.row_tiles, self.panel_tiles = self.half // LANE, self.rows_width // LANE, PANEL // LANE
        self.first_panel = self.col_tiles + self.row_tiles
        self.across = -(-(self.first_panel + self.panel_tiles) // SUB)
        self.slab = (times * SUB, self.across * LANE)
        self.shape = (tm_count * lat_count,) + self.slab
        self.sums_shape = (self.across, tm_count * self.slab[0], LANE)

    def weights_copies(self, legendre_ref, weights_ref, sems):
        width = GROUP * GATHER

        def copy(group):
            own = pl.ds(pl.multiple_of(group * width, width), width)
            return pltpu.make_async_copy(legendre_ref.at[:, own], weights_ref.at[:, own], sems.at[group])

        @pl.loop(0, self.parts // GROUP)
        def _(group):
            copy(group).start()

        return copy

    def spot(self, tile, time):
        low = tile % self.across * LANE
        return time * SUB + tile // self.across, slice(low, low + LANE)

    def pack(self, sums_ref, slab_ref, sent_ref):
        def fill(tile, source, count):
            for n in range(count):
                for t in range(self.times):
                    row, lanes = self.spot(tile + n, t)
                    low = source + n * LANE
                    slab_ref[row : row + 1, lanes] = sums_ref[t : t + 1, low : low + LANE]

        slab_ref[...] = jnp.zeros_like(slab_ref)
        fill(self.first_panel, 0, self.panel_tiles)
        for part in range(self.lat_count):
            for core in range(2):
                fill(0, part * self.part_width + core * self.half, self.col_tiles)
                for owner in range(core, self.tm_count, 2):
                    fill(self.col_tiles, owner * self.rows_width, self.row_tiles)
                    sent_ref[owner * self.lat_count + part] = slab_ref[...].astype(BF16)

    def gather_sums(self, got_ref, slabs_ref):
        rows = self.slab[0]
        for sender in range(self.tm_count):
            first = sender * self.lat_count
            total = got_ref[first].astype(F32)
            for part in range(1, self.lat_count):
                total = total + got_ref[first + part].astype(F32)
            for n in range(self.across):
                slabs_ref[n, sender * rows : (sender + 1) * rows, :] = total[:, n * LANE : (n + 1) * LANE]

    def tile(self, slabs_ref, tile):
        pieces = []
        for t in range(self.times):
            row = t * SUB + tile // self.across
            pieces.append(slabs_ref[tile % self.across, pl.ds(row, self.tm_count, stride=self.slab[0]), :])
        return jnp.concatenate(pieces, axis=0).astype(BF16).astype(F32)

    def unpack(self, got):
        split_shape = (self.tm_count, self.lat_count, self.times, SUB * self.across * LANE)
        total = got.astype(F32).reshape(split_shape).sum(axis=1).astype(BF16).astype(F32)
        return total.transpose(1, 0, 2).reshape(self.times * self.tm_count, -1)


def window_of(value, start, length, lines_ref):
    for n in range(value.shape[1] // LANE):
        lines_ref[n : n + 1, :] = value[:, n * LANE : (n + 1) * LANE]
    over = lax.rem(start, LANE)
    lines_ref[...] = pltpu.roll(lines_ref[...], lax.rem(LANE - over, LANE), 1)
    first = lines_ref[pl.ds(start // LANE, length // LANE), :]
    second = lines_ref[pl.ds(start // LANE + 1, length // LANE), :]
    lane = lax.broadcasted_iota(jnp.int32, first.shape, 1)
    return jnp.where(lane < LANE - over, first, second)


def spectra_kernel(plan, scale, start_ref, ridge_ref, order_ref, fields_ref, basis_ref, legendre_ref, sent_ref,
                   lam_ref, order_buf, index_ref, window_ref, column_ref, table_ref, fields_buf, basis_buf, weights_ref, lines_ref, even_ref, odd_ref, sums_ref, slab_ref,
                   order_sem, column_sem, fields_sem, basis_sem, weights_sem):
    times, lats, nlon = fields_ref.shape
    pieces = -(-lats // LANE)
    order_copy = pltpu.make_async_copy(order_ref, order_buf, order_sem)
    order_copy.start()
    fields_copy = pltpu.make_async_copy(fields_ref, fields_buf, fields_sem)
    fields_copy.start()
    basis_copy = pltpu.make_async_copy(basis_ref, basis_buf, basis_sem)
    basis_copy.start()
    for t in range(times):
        end = pieces * LANE * (t + 1)
        low = end - LANE
        lines_ref[low:end, :] = jnp.zeros((LANE, nlon), BF16)
    order_copy.wait()
    start = start_ref[0]
    column = SUB * (order_buf[1:2, :] + nlon // 2 * order_buf[2:3, :])
    window_ref[...] = window_of(column, start, plan.kcoef, index_ref)
    column_copy = pltpu.make_async_copy(window_ref, column_ref, column_sem)
    column_copy.start()
    degree = window_of(order_buf[0:1, :], start, plan.kcoef, index_ref)
    lam = ridge_ref[0] * (1.0 + (degree * (degree + 1)).astype(F32) / float(LMAX * (LMAX + 1)))
    for n in range(plan.kcoef // LANE):
        lam_ref[:, n * LANE : (n + 1) * LANE] = lam[n : n + 1, :]
    fields_copy.wait()
    for t in range(times):
        lines_ref[pieces * LANE * t : pieces * LANE * t + lats, :] = fields_buf[t]
    basis_copy.wait()
    weights_copy = plan.weights_copies(legendre_ref, weights_ref, weights_sem)
    tiles = times * pieces
    wide = 2 if tiles % 2 == 0 else 1
    for low in range(0, tiles, wide):
        spectra = scale * lax.dot_general(
            basis_buf[...], lines_ref[LANE * low : LANE * (low + wide), :], (((1,), (1,)), ((), ())),
            preferred_element_type=F32,
        )
        for s in range(wide):
            table_ref[pl.ds(low + s, nlon, stride=SUB), :] = spectra[:, LANE * s : LANE * (s + 1)]
    column_copy.wait()
    contract(plan, column_ref, table_ref, weights_ref, sums_ref, even_ref, odd_ref, weights_copy)
    plan.pack(sums_ref, slab_ref, sent_ref)


def in_hbm(value):
    return pltpu.with_memory_space_constraint(value, pltpu.HBM)


def spot_in(space):
    return pl.BlockSpec(memory_space=space)


def spectra_and_contract(plan, start, ridge, order, fields, basis, legendre):
    times, lats, nlon = fields.shape
    entries = order.shape[1] // LANE
    pieces = -(-lats // LANE)
    return pl.pallas_call(
        functools.partial(spectra_kernel, plan, 1.0 / math.sqrt(nlon)),
        in_specs=[spot_in(pltpu.SMEM)] * 2 + [spot_in(pltpu.HBM)] * 4,
        out_specs=[spot_in(pltpu.VMEM)] * 2,
        out_shape=[jax.ShapeDtypeStruct(plan.shape, BF16), jax.ShapeDtypeStruct((1, plan.kcoef), F32)],
        scratch_shapes=[
            pltpu.VMEM(order.shape, jnp.int32),
            pltpu.VMEM((entries + SUB, LANE), jnp.int32),
            pltpu.VMEM((plan.kcoef // LANE, LANE), jnp.int32),
            pltpu.SMEM((plan.kcoef // LANE, LANE), jnp.int32),
            pltpu.VMEM((nlon * SUB, LANE), F32),
            pltpu.VMEM(fields.shape, BF16),
            pltpu.VMEM(basis.shape, BF16),
            pltpu.VMEM((lats, plan.kcoef), BF16),
            pltpu.VMEM((times * pieces * LANE, nlon), BF16),
            pltpu.VMEM((GATHER * SUB, LANE), F32),
            pltpu.VMEM((GATHER * SUB, LANE), F32),
            pltpu.VMEM((times, plan.kcoef), F32),
            pltpu.VMEM(plan.slab, F32),
            pltpu.SemaphoreType.DMA(()),
            pltpu.SemaphoreType.DMA(()),
            pltpu.SemaphoreType.DMA(()),
            pltpu.SemaphoreType.DMA(()),
            pltpu.SemaphoreType.DMA((plan.parts // GROUP,)),
        ],
        compiler_params=pltpu.CompilerParams(vmem_limit_bytes=SPECTRA_VMEM),
        cost_estimate=pl.CostEstimate(flops=12 << 30, bytes_accessed=8 << 20, transcendentals=0),
        name="spectra_and_contract",
    )(start, ridge, in_hbm(order), in_hbm(fields), in_hbm(basis), in_hbm(legendre))


def split(value, pieces):
    out = []
    for _ in range(pieces):
        piece = value.astype(BF16)
        out.append(piece)
        value = value - piece.astype(F32)
    return out


def panel_kernel(plan, got_ref, lam_ref, w_ref, diag_ref, inverse_ref, slabs_ref, q_ref, g_ref, y_ref, x_ref, z_ref):
    nt = w_ref.shape[0]
    lanes = PANEL + LANE
    plan.gather_sums(got_ref, slabs_ref)
    coef = jnp.concatenate(
        [plan.tile(slabs_ref, plan.first_panel + n) for n in range(plan.panel_tiles)], axis=1
    )
    lam = lam_ref[...]
    scaled = coef / lam
    starts, total = [], 0
    for r in range(nt):
        low = r // 8 * 8
        z_ref[total : total + nt - low, :] = coef[low:, :] * scaled[r : r + 1, :]
        starts.append(total)
        total += nt - low
    ids = lax.broadcasted_iota(jnp.int32, (PANEL, PANEL), 0)
    upto = lax.broadcasted_iota(jnp.int32, (PANEL, PANEL), 1)
    tri = jnp.where(ids < upto, 1.0, 0.0).astype(BF16)
    prefix = 0.0
    for piece in split(z_ref[...], 3)[::-1]:
        prefix = prefix + jnp.dot(piece, tri, preferred_element_type=F32)
    q_ref[:, :PANEL] = prefix
    q_ref[:, PANEL:] = jnp.broadcast_to(prefix[:, PANEL - 1 :] + z_ref[:, PANEL - 1 :], (total, LANE))
    y_ref[:, :PANEL] = coef
    eye = lax.broadcasted_iota(jnp.int32, (nt, LANE), 0) == lax.broadcasted_iota(jnp.int32, (nt, LANE), 1)
    y_ref[:, PANEL:] = jnp.where(eye, 1.0, 0.0)
    inverses = []
    for r in range(nt):
        low = r // 8 * 8
        place = low + lax.broadcasted_iota(jnp.int32, (nt - low, lanes), 0)
        row = q_ref[starts[r] : starts[r] + nt - low, :] + jnp.where(place == r, float(nt), 0.0)
        for p in range(r):
            base = starts[p] + low - p // 8 * 8
            factor = g_ref[starts[p] + r - p // 8 * 8 : starts[p] + r - p // 8 * 8 + 1, :]
            row = row - factor * q_ref[base : base + nt - low, :]
        q_ref[starts[r] : starts[r] + nt - low, :] = row
        inv = 1.0 / row[r - low : r - low + 1, :]
        inverses.append(inv)
        ratio = jnp.where(place > r, row * inv, 0.0)
        g_ref[starts[r] : starts[r] + nt - low, :] = ratio
        y_ref[low:, :] = y_ref[low:, :] - ratio * y_ref[r : r + 1, :]
    x_ref[...] = jnp.zeros_like(x_ref)
    for r in range(nt - 1, -1, -1):
        low = r // 8 * 8
        ratio = g_ref[starts[r] : starts[r] + nt - low, :]
        tail = jnp.sum(ratio * x_ref[low:, :], axis=0, keepdims=True)
        x_ref[r : r + 1, :] = y_ref[r : r + 1, :] * inverses[r] - tail
    solved = x_ref[:, :PANEL]
    pivot = jnp.sqrt(lam + jnp.sum(coef * solved, axis=0, keepdims=True))
    w_ref[...] = solved / pivot
    diag_ref[...] = lam / pivot
    inverse_ref[...] = x_ref[:, PANEL:]


def panel_small(plan, got, lam):
    nt = plan.times * plan.tm_count
    rows = sum(nt - r // 8 * 8 for r in range(nt))
    lanes = PANEL + LANE
    return pl.pallas_call(
        functools.partial(panel_kernel, plan),
        grid=(1,),
        in_specs=[
            pl.BlockSpec(plan.shape, lambda i: (0, 0, 0)),
            pl.BlockSpec((1, PANEL), lambda i: (0, 0)),
        ],
        out_specs=[
            pl.BlockSpec((nt, PANEL), lambda i: (0, 0)),
            pl.BlockSpec((1, PANEL), lambda i: (0, 0)),
            pl.BlockSpec((nt, LANE), lambda i: (0, 0)),
        ],
        out_shape=[
            jax.ShapeDtypeStruct((nt, PANEL), F32),
            jax.ShapeDtypeStruct((1, PANEL), F32),
            jax.ShapeDtypeStruct((nt, LANE), F32),
        ],
        scratch_shapes=[
            pltpu.VMEM(plan.sums_shape, F32),
            pltpu.VMEM((rows, lanes), F32),
            pltpu.VMEM((rows, lanes), F32),
            pltpu.VMEM((nt, lanes), F32),
            pltpu.VMEM((nt, lanes), F32),
            pltpu.VMEM((rows, PANEL), F32),
        ],
        compiler_params=pltpu.CompilerParams(vmem_limit_bytes=SMALL_VMEM),
        cost_estimate=pl.CostEstimate(flops=4 << 30, bytes_accessed=1 << 18, transcendentals=0),
        name="panel_small",
    )(got, lam)


def panel_large(plan, got, lam):
    low = plan.first_panel * LANE
    coef, lam = plan.unpack(got)[:, low : low + PANEL], lam[:, :PANEL]
    nt = coef.shape[0]
    gram = jnp.dot(coef.T, coef, precision=lax.Precision.HIGHEST) / nt + jnp.diag(lam[0])
    factor = jnp.linalg.cholesky(gram)
    solved = jax.scipy.linalg.solve_triangular(factor, coef.T, lower=True)
    w = solved.T / nt
    rest = jnp.eye(nt, dtype=F32) / nt - jnp.dot(w, w.T, precision=lax.Precision.HIGHEST)
    pivot = jnp.diagonal(factor)[None, :]
    pad = -(-nt // LANE) * LANE - nt
    return w, pivot - jnp.sum(coef * w, axis=0, keepdims=True), jnp.pad(rest, ((0, 0), (0, pad)))


def stack_pieces(value):
    high, low = split(value, 2)
    return jnp.concatenate([high.astype(F32), low.astype(F32)], axis=0).astype(BF16)


def twice(value):
    return jnp.concatenate([value, value], axis=0).astype(BF16)


def contract_times(left, right):
    return lax.dot_general(left, right, (((0,), (0,)), ((), ())), preferred_element_type=F32)


def times_first(value):
    return value.astype(F32).T.astype(BF16)


def tile_kernel(plan, own_ref, other_ref, w_ref, diag_ref, lam_ref, inverse_ref, out_ref,
                own_slabs, other_slabs, rows_ref, cols_ref, left_ref, left_main_ref, right_ref, tiles_ref, out_sem):
    height = out_ref.shape[0]
    nt = rows_ref.shape[0]
    tm_index = lax.axis_index("tm")
    row_start = tm_index * height
    first_col = lax.axis_index("lat") * cols_ref.shape[1]
    in_panel_rows = row_start < PANEL

    for got_ref, slabs_ref, core in (
        (own_ref, own_slabs, lax.rem(tm_index, 2)),
        (other_ref, other_slabs, 1 - lax.rem(tm_index, 2)),
    ):
        plan.gather_sums(got_ref, slabs_ref)
        for n in range(plan.col_tiles):
            low = pl.multiple_of(core * plan.half + n * LANE, LANE)
            cols_ref[:, pl.ds(low, LANE)] = plan.tile(slabs_ref, n)
    for n in range(plan.row_tiles):
        rows_ref[:, n * LANE : (n + 1) * LANE] = plan.tile(own_slabs, plan.col_tiles + n)
    left_ref[...] = times_first(twice(rows_ref[...]))

    @pl.when(in_panel_rows)
    def _():
        low = pl.multiple_of(jnp.minimum(row_start, PANEL - height), LANE)
        left_main_ref[...] = times_first(stack_pieces(w_ref[:, pl.ds(low, height)]))
        right_ref[...] = twice(cols_ref[...])

    @pl.when(jnp.logical_not(in_panel_rows))
    def _():
        left_main_ref[...] = left_ref[...]
        turned = contract_times(stack_pieces(inverse_ref[:, :nt]), twice(cols_ref[...]))
        right_ref[...] = stack_pieces(turned)

    @pl.when(first_col < PANEL)
    def _():
        right_ref[:, :PANEL] = stack_pieces(w_ref[...])

    def copy(step):
        own = pl.ds(pl.multiple_of(step * WIDE, WIDE), WIDE)
        return pltpu.make_async_copy(tiles_ref.at[step], out_ref.at[:, own], out_sem.at[step])

    @pl.loop(0, cols_ref.shape[1] // WIDE)
    def _(step):
        col_start = first_col + step * WIDE
        in_panel_cols = col_start < PANEL
        on_diagonal = (row_start < col_start + WIDE) & (col_start < row_start + height)
        own = pl.ds(pl.multiple_of(step * WIDE, WIDE), WIDE)
        out = tiles_ref.at[step]

        def ids():
            rows = row_start + lax.broadcasted_iota(jnp.int32, (height, WIDE), 0)
            return rows, col_start + lax.broadcasted_iota(jnp.int32, (height, WIDE), 1)

        @pl.when(in_panel_cols)
        def _():
            out[...] = jnp.dot(left_ref[...], right_ref[:, own], preferred_element_type=F32)

        @pl.when(jnp.logical_not(in_panel_cols))
        def _():
            out[...] = jnp.dot(left_main_ref[...], right_ref[:, own], preferred_element_type=F32)

        @pl.when(in_panel_cols & in_panel_rows)
        def _():
            row_ids, col_ids = ids()
            diag = jnp.where(row_ids == col_ids, diag_ref[:, own_panel(step)], 0.0)
            out[...] = jnp.where(row_ids >= col_ids, out[...], 0.0) + diag

        @pl.when(on_diagonal & jnp.logical_not(in_panel_rows))
        def _():
            row_ids, col_ids = ids()
            lam = lam_ref[:, pl.ds(pl.multiple_of(col_start, LANE), WIDE)]
            out[...] += jnp.where(row_ids == col_ids, lam, 0.0)

        copy(step).start()

    @pl.loop(0, cols_ref.shape[1] // WIDE)
    def _(step):
        copy(step).wait()


def own_panel(step):
    return pl.ds(pl.multiple_of(jnp.minimum(step * WIDE, PANEL - WIDE), WIDE), WIDE)


def out_tile(plan, own, other, w, diag, lam, inverse):
    nt, height, width = plan.times * plan.tm_count, plan.rows_width, plan.part_width
    return pl.pallas_call(
        functools.partial(tile_kernel, plan),
        in_specs=[spot_in(pltpu.VMEM)] * 6,
        out_specs=spot_in(pltpu.HBM),
        out_shape=jax.ShapeDtypeStruct((height, width), F32),
        scratch_shapes=[
            pltpu.VMEM(plan.sums_shape, F32),
            pltpu.VMEM(plan.sums_shape, F32),
            pltpu.VMEM((nt, height), F32),
            pltpu.VMEM((nt, width), F32),
            pltpu.VMEM((height, 2 * nt), BF16),
            pltpu.VMEM((height, 2 * nt), BF16),
            pltpu.VMEM((2 * nt, width), BF16),
            pltpu.VMEM((width // WIDE, height, WIDE), F32),
            pltpu.SemaphoreType.DMA((width // WIDE,)),
        ],
        compiler_params=pltpu.CompilerParams(vmem_limit_bytes=SMALL_VMEM),
        cost_estimate=pl.CostEstimate(
            flops=4 * nt * height * width, bytes_accessed=4 * height * width, transcendentals=0
        ),
        name="out_tile",
    )(own, other, w, diag, lam, inverse)


def on_device(basis, fields, legendre, order_table, window_start, ridge):
    times = fields.shape[0]
    kcoef = legendre.shape[1]
    tm_count, lat_count = lax.axis_size("tm"), lax.axis_size("lat")
    plan = Plan(kcoef, tm_count, lat_count, times)
    sent, lam = spectra_and_contract(plan, window_start, ridge, order_table, fields, basis, legendre)
    own = lax.all_to_all(sent, ("tm", "lat"), 0, 0, tiled=True)
    other = lax.ppermute(own, "tm", [(i, i ^ 1) for i in range(tm_count)])
    small = times * tm_count <= LANE // 4
    w, diag, inverse = (panel_small if small else panel_large)(plan, own, lam)
    return out_tile(plan, own, other, w, diag, lam, inverse)


def solution(mesh):
    def run(fields, legendre, order_table, window_start, ridge):
        basis = jnp.asarray(basis_table(fields.shape[2]))
        placed = (P(), P("tm", "lat", None), P("lat", None), P(), P(), P())
        body = jax.shard_map(on_device, mesh=mesh, in_specs=placed, out_specs=P("tm", "lat"), check_vma=False)
        return body(basis, fields, legendre, order_table, window_start, ridge)

    return run
```

```python
import functools
import math

import jax
import jax.numpy as jnp
import ml_dtypes
import numpy as np
from jax import lax
from jax.experimental import pallas as pl
from jax.experimental.pallas import tpu as pltpu
from jax.sharding import PartitionSpec as P

LMAX = 720
PANEL = 512
LANE = 128
SUB = 8
GATHER = 256
GROUP = 4
WIDE = 512
SPECTRA_VMEM = 36 * 1024 * 1024
SMALL_VMEM = 20 * 1024 * 1024
F32 = jnp.float32
BF16 = jnp.bfloat16


def basis_table(nlon):
    half = nlon // 2
    order = np.concatenate([np.arange(0, half, 2), np.arange(0, half, 2), np.arange(1, half, 2), np.arange(1, half, 2)])
    sine = np.repeat([False, True, False, True], [half // 2] * 4)[:, None]
    longitude = np.arange(half, dtype=np.int64)[None, :]
    phase = (order[:, None] * longitude % nlon).astype(np.float32) * np.float32(2.0 * math.pi / nlon)
    return np.where(sine, np.sin(phase), np.cos(phase)).astype(ml_dtypes.bfloat16)


def basis_row(order, part, nlon):
    return nlon // 2 * (order & 1) + nlon // 4 * part + (order >> 1)


def pick_rows(column_ref, start, table_ref, picked_ref):
    row = start // LANE
    for j in range(GATHER):
        group = pl.multiple_of(column_ref[row + j // LANE, j % LANE], SUB)
        picked_ref[SUB * j : SUB * (j + 1), :] = table_ref[pl.ds(group, SUB), :]


def latitude_sums(picked_ref, weights, times):
    lats = weights.shape[0]
    pieces = -(-lats // LANE)
    picked = [picked_ref[pl.ds(s, GATHER, stride=SUB), :] for s in range(times * pieces)]
    value = jnp.concatenate(
        [jnp.concatenate(picked[pieces * t : pieces * (t + 1)], axis=1) for t in range(times)], axis=0
    )
    spare = jnp.zeros((pieces * LANE - lats, GATHER), BF16)
    every = jnp.dot(value.astype(BF16), jnp.concatenate([weights, spare], axis=0), preferred_element_type=F32)
    shape = (LANE, LANE)
    eye = lax.broadcasted_iota(jnp.int32, shape, 0) == lax.broadcasted_iota(jnp.int32, shape, 1)
    sums = []
    for t in range(times):
        own = []
        for low in range(0, GATHER, LANE):
            square = every[t * GATHER + low : t * GATHER + low + LANE, low : low + LANE]
            own.append(jnp.sum(jnp.where(eye, square, 0.0), axis=0, keepdims=True))
        sums.append(jnp.concatenate(own, axis=1))
    return jnp.concatenate(sums, axis=0)


def contract(plan, column_ref, table_ref, weights_ref, sums_ref, even_ref, odd_ref, weights_copy):
    picked = [even_ref, odd_ref]

    def place(part):
        return jnp.minimum(part, plan.parts - 1) * GATHER

    pick_rows(column_ref, 0, table_ref, even_ref)

    @pl.loop(0, plan.parts // GROUP)
    def _(group):
        weights_copy(group).wait()
        for n in range(GROUP):
            part = group * GROUP + n
            pick_rows(column_ref, place(part + 1), table_ref, picked[(n + 1) % 2])
            at = pl.ds(pl.multiple_of(part * GATHER, GATHER), GATHER)
            sums_ref[:, at] = latitude_sums(picked[n % 2], weights_ref[:, at], plan.times)


class Plan:
    def __init__(self, kcoef, tm_count, lat_count, times):
        self.tm_count, self.lat_count, self.times = tm_count, lat_count, times
        self.kcoef, self.part_width, self.rows_width = kcoef, kcoef // lat_count, kcoef // tm_count
        self.parts = kcoef // GATHER
        self.half = self.part_width // 2
        self.col_tiles, self.row_tiles, self.panel_tiles = self.half // LANE, self.rows_width // LANE, PANEL // LANE
        self.first_panel = self.col_tiles + self.row_tiles
        self.across = -(-(self.first_panel + self.panel_tiles) // SUB)
        self.slab = (times * SUB, self.across * LANE)
        self.shape = (tm_count * lat_count,) + self.slab
        self.sums_shape = (self.across, tm_count * self.slab[0], LANE)

    def weights_copies(self, legendre_ref, weights_ref, sems):
        width = GROUP * GATHER

        def copy(group):
            own = pl.ds(pl.multiple_of(group * width, width), width)
            return pltpu.make_async_copy(legendre_ref.at[:, own], weights_ref.at[:, own], sems.at[group])

        @pl.loop(0, self.parts // GROUP)
        def _(group):
            copy(group).start()

        return copy

    def spot(self, tile, time):
        low = tile % self.across * LANE
        return time * SUB + tile // self.across, slice(low, low + LANE)

    def pack(self, sums_ref, slab_ref, sent_ref):
        def fill(tile, source, count):
            for n in range(count):
                for t in range(self.times):
                    row, lanes = self.spot(tile + n, t)
                    low = source + n * LANE
                    slab_ref[row : row + 1, lanes] = sums_ref[t : t + 1, low : low + LANE]

        slab_ref[...] = jnp.zeros_like(slab_ref)
        fill(self.first_panel, 0, self.panel_tiles)
        for part in range(self.lat_count):
            for core in range(2):
                fill(0, part * self.part_width + core * self.half, self.col_tiles)
                for owner in range(core, self.tm_count, 2):
                    fill(self.col_tiles, owner * self.rows_width, self.row_tiles)
                    sent_ref[owner * self.lat_count + part] = slab_ref[...].astype(BF16)

    def gather_sums(self, got_ref, slabs_ref):
        rows = self.slab[0]
        for sender in range(self.tm_count):
            first = sender * self.lat_count
            total = got_ref[first].astype(F32)
            for part in range(1, self.lat_count):
                total = total + got_ref[first + part].astype(F32)
            for n in range(self.across):
                slabs_ref[n, sender * rows : (sender + 1) * rows, :] = total[:, n * LANE : (n + 1) * LANE]

    def tile(self, slabs_ref, tile):
        pieces = []
        for t in range(self.times):
            row = t * SUB + tile // self.across
            pieces.append(slabs_ref[tile % self.across, pl.ds(row, self.tm_count, stride=self.slab[0]), :])
        return jnp.concatenate(pieces, axis=0)

    def unpack(self, got):
        split_shape = (self.tm_count, self.lat_count, self.times, SUB * self.across * LANE)
        total = got.astype(F32).reshape(split_shape).sum(axis=1)
        return total.transpose(1, 0, 2).reshape(self.times * self.tm_count, -1)


def window_of(value, start, length, lines_ref):
    for n in range(value.shape[1] // LANE):
        lines_ref[n : n + 1, :] = value[:, n * LANE : (n + 1) * LANE]
    over = lax.rem(start, LANE)
    lines_ref[...] = pltpu.roll(lines_ref[...], lax.rem(LANE - over, LANE), 1)
    first = lines_ref[pl.ds(start // LANE, length // LANE), :]
    second = lines_ref[pl.ds(start // LANE + 1, length // LANE), :]
    lane = lax.broadcasted_iota(jnp.int32, first.shape, 1)
    return jnp.where(lane < LANE - over, first, second)


def spectra_kernel(plan, scale, start_ref, ridge_ref, order_ref, fields_ref, basis_ref, legendre_ref, sent_ref,
                   lam_ref, order_buf, index_ref, window_ref, column_ref, table_ref, fields_buf, basis_buf,
                   weights_ref, even_lines, odd_lines, even_ref, odd_ref, sums_ref, slab_ref, order_sem,
                   column_sem, fields_sem, basis_sem, weights_sem):
    times, lats, nlon = fields_ref.shape
    pieces = -(-lats // LANE)
    order_copy = pltpu.make_async_copy(order_ref, order_buf, order_sem)
    order_copy.start()
    fields_copy = pltpu.make_async_copy(fields_ref, fields_buf, fields_sem)
    fields_copy.start()
    basis_copy = pltpu.make_async_copy(basis_ref, basis_buf, basis_sem)
    basis_copy.start()
    for t in range(times):
        end = pieces * LANE * (t + 1)
        for folded in (even_lines, odd_lines):
            folded[end - LANE : end, :] = jnp.zeros((LANE, nlon // 2), BF16)
    order_copy.wait()
    start = start_ref[0]
    column = SUB * basis_row(order_buf[1:2, :], order_buf[2:3, :], nlon)
    window_ref[...] = window_of(column, start, plan.kcoef, index_ref)
    column_copy = pltpu.make_async_copy(window_ref, column_ref, column_sem)
    column_copy.start()
    degree = window_of(order_buf[0:1, :], start, plan.kcoef, index_ref)
    lam = ridge_ref[0] * (1.0 + (degree * (degree + 1)).astype(F32) / float(LMAX * (LMAX + 1)))
    for n in range(plan.kcoef // LANE):
        lam_ref[:, n * LANE : (n + 1) * LANE] = lam[n : n + 1, :]
    fields_copy.wait()
    for t in range(times):
        first = fields_buf[t, :, : nlon // 2].astype(F32)
        second = fields_buf[t, :, nlon // 2 :].astype(F32)
        own = slice(pieces * LANE * t, pieces * LANE * t + lats)
        even_lines[own, :] = (first + second).astype(BF16)
        odd_lines[own, :] = (first - second).astype(BF16)
    basis_copy.wait()
    weights_copy = plan.weights_copies(legendre_ref, weights_ref, weights_sem)
    tiles = times * pieces
    wide = 2 if tiles % 2 == 0 else 1
    for parity, folded in enumerate((even_lines, odd_lines)):
        half = slice(nlon // 2 * parity, nlon // 2 * (parity + 1))
        for low in range(0, tiles, wide):
            spectra = scale * lax.dot_general(
                basis_buf[half, :], folded[LANE * low : LANE * (low + wide), :], (((1,), (1,)), ((), ())),
                preferred_element_type=F32,
            )
            for s in range(wide):
                at = pl.ds(SUB * half.start + low + s, nlon // 2, stride=SUB)
                table_ref[at, :] = spectra[:, LANE * s : LANE * (s + 1)]
    column_copy.wait()
    contract(plan, column_ref, table_ref, weights_ref, sums_ref, even_ref, odd_ref, weights_copy)
    plan.pack(sums_ref, slab_ref, sent_ref)


def in_hbm(value):
    return pltpu.with_memory_space_constraint(value, pltpu.HBM)


def spot_in(space):
    return pl.BlockSpec(memory_space=space)


def spectra_and_contract(plan, start, ridge, order, fields, basis, legendre):
    times, lats, nlon = fields.shape
    entries = order.shape[1] // LANE
    pieces = -(-lats // LANE)
    return pl.pallas_call(
        functools.partial(spectra_kernel, plan, 1.0 / math.sqrt(nlon)),
        in_specs=[spot_in(pltpu.SMEM)] * 2 + [spot_in(pltpu.HBM)] * 4,
        out_specs=[spot_in(pltpu.VMEM)] * 2,
        out_shape=[jax.ShapeDtypeStruct(plan.shape, BF16), jax.ShapeDtypeStruct((1, plan.kcoef), F32)],
        scratch_shapes=[
            pltpu.VMEM(order.shape, jnp.int32),
            pltpu.VMEM((entries + SUB, LANE), jnp.int32),
            pltpu.VMEM((plan.kcoef // LANE, LANE), jnp.int32),
            pltpu.SMEM((plan.kcoef // LANE, LANE), jnp.int32),
            pltpu.VMEM((nlon * SUB, LANE), F32),
            pltpu.VMEM(fields.shape, BF16),
            pltpu.VMEM(basis.shape, BF16),
            pltpu.VMEM((lats, plan.kcoef), BF16),
            pltpu.VMEM((times * pieces * LANE, nlon // 2), BF16),
            pltpu.VMEM((times * pieces * LANE, nlon // 2), BF16),
            pltpu.VMEM((GATHER * SUB, LANE), F32),
            pltpu.VMEM((GATHER * SUB, LANE), F32),
            pltpu.VMEM((times, plan.kcoef), F32),
            pltpu.VMEM(plan.slab, F32),
            pltpu.SemaphoreType.DMA(()),
            pltpu.SemaphoreType.DMA(()),
            pltpu.SemaphoreType.DMA(()),
            pltpu.SemaphoreType.DMA(()),
            pltpu.SemaphoreType.DMA((plan.parts // GROUP,)),
        ],
        compiler_params=pltpu.CompilerParams(vmem_limit_bytes=SPECTRA_VMEM),
        cost_estimate=pl.CostEstimate(flops=12 << 30, bytes_accessed=8 << 20, transcendentals=0),
        name="spectra_and_contract",
    )(start, ridge, in_hbm(order), in_hbm(fields), in_hbm(basis), in_hbm(legendre))


def split(value, pieces):
    out = []
    for _ in range(pieces):
        piece = value.astype(BF16)
        out.append(piece)
        value = value - piece.astype(F32)
    return out


def panel_kernel(plan, got_ref, lam_ref, w_ref, diag_ref, inverse_ref, slabs_ref, q_ref, g_ref, y_ref, x_ref, z_ref):
    nt = w_ref.shape[0]
    lanes = PANEL + LANE
    plan.gather_sums(got_ref, slabs_ref)
    coef = jnp.concatenate(
        [plan.tile(slabs_ref, plan.first_panel + n) for n in range(plan.panel_tiles)], axis=1
    )
    lam = lam_ref[...]
    scaled = coef / lam
    starts, total = [], 0
    for r in range(nt):
        low = r // 8 * 8
        z_ref[total : total + nt - low, :] = coef[low:, :] * scaled[r : r + 1, :]
        starts.append(total)
        total += nt - low
    ids = lax.broadcasted_iota(jnp.int32, (PANEL, PANEL), 0)
    upto = lax.broadcasted_iota(jnp.int32, (PANEL, PANEL), 1)
    tri = jnp.where(ids < upto, 1.0, 0.0).astype(BF16)
    prefix = 0.0
    for piece in split(z_ref[...], 3)[::-1]:
        prefix = prefix + jnp.dot(piece, tri, preferred_element_type=F32)
    q_ref[:, :PANEL] = prefix
    q_ref[:, PANEL:] = jnp.broadcast_to(prefix[:, PANEL - 1 :] + z_ref[:, PANEL - 1 :], (total, LANE))
    y_ref[:, :PANEL] = coef
    eye = lax.broadcasted_iota(jnp.int32, (nt, LANE), 0) == lax.broadcasted_iota(jnp.int32, (nt, LANE), 1)
    y_ref[:, PANEL:] = jnp.where(eye, 1.0, 0.0)
    inverses = []
    for r in range(nt):
        low = r // 8 * 8
        place = low + lax.broadcasted_iota(jnp.int32, (nt - low, lanes), 0)
        row = q_ref[starts[r] : starts[r] + nt - low, :] + jnp.where(place == r, float(nt), 0.0)
        for p in range(r):
            base = starts[p] + low - p // 8 * 8
            factor = g_ref[starts[p] + r - p // 8 * 8 : starts[p] + r - p // 8 * 8 + 1, :]
            row = row - factor * q_ref[base : base + nt - low, :]
        q_ref[starts[r] : starts[r] + nt - low, :] = row
        inv = 1.0 / row[r - low : r - low + 1, :]
        inverses.append(inv)
        ratio = jnp.where(place > r, row * inv, 0.0)
        g_ref[starts[r] : starts[r] + nt - low, :] = ratio
        y_ref[low:, :] = y_ref[low:, :] - ratio * y_ref[r : r + 1, :]
    x_ref[...] = jnp.zeros_like(x_ref)
    for r in range(nt - 1, -1, -1):
        low = r // 8 * 8
        ratio = g_ref[starts[r] : starts[r] + nt - low, :]
        tail = jnp.sum(ratio * x_ref[low:, :], axis=0, keepdims=True)
        x_ref[r : r + 1, :] = y_ref[r : r + 1, :] * inverses[r] - tail
    solved = x_ref[:, :PANEL]
    pivot = jnp.sqrt(lam + jnp.sum(coef * solved, axis=0, keepdims=True))
    w_ref[...] = solved / pivot
    diag_ref[...] = lam / pivot
    inverse_ref[...] = x_ref[:, PANEL:]


def panel_small(plan, got, lam):
    nt = plan.times * plan.tm_count
    rows = sum(nt - r // 8 * 8 for r in range(nt))
    lanes = PANEL + LANE
    return pl.pallas_call(
        functools.partial(panel_kernel, plan),
        grid=(1,),
        in_specs=[
            pl.BlockSpec(plan.shape, lambda i: (0, 0, 0)),
            pl.BlockSpec((1, PANEL), lambda i: (0, 0)),
        ],
        out_specs=[
            pl.BlockSpec((nt, PANEL), lambda i: (0, 0)),
            pl.BlockSpec((1, PANEL), lambda i: (0, 0)),
            pl.BlockSpec((nt, LANE), lambda i: (0, 0)),
        ],
        out_shape=[
            jax.ShapeDtypeStruct((nt, PANEL), F32),
            jax.ShapeDtypeStruct((1, PANEL), F32),
            jax.ShapeDtypeStruct((nt, LANE), F32),
        ],
        scratch_shapes=[
            pltpu.VMEM(plan.sums_shape, F32),
            pltpu.VMEM((rows, lanes), F32),
            pltpu.VMEM((rows, lanes), F32),
            pltpu.VMEM((nt, lanes), F32),
            pltpu.VMEM((nt, lanes), F32),
            pltpu.VMEM((rows, PANEL), F32),
        ],
        compiler_params=pltpu.CompilerParams(vmem_limit_bytes=SMALL_VMEM),
        cost_estimate=pl.CostEstimate(flops=4 << 30, bytes_accessed=1 << 18, transcendentals=0),
        name="panel_small",
    )(got, lam)


def panel_large(plan, got, lam):
    low = plan.first_panel * LANE
    coef, lam = plan.unpack(got)[:, low : low + PANEL], lam[:, :PANEL]
    nt = coef.shape[0]
    gram = jnp.dot(coef.T, coef, precision=lax.Precision.HIGHEST) / nt + jnp.diag(lam[0])
    factor = jnp.linalg.cholesky(gram)
    solved = jax.scipy.linalg.solve_triangular(factor, coef.T, lower=True)
    w = solved.T / nt
    rest = jnp.eye(nt, dtype=F32) / nt - jnp.dot(w, w.T, precision=lax.Precision.HIGHEST)
    pivot = jnp.diagonal(factor)[None, :]
    pad = -(-nt // LANE) * LANE - nt
    return w, pivot - jnp.sum(coef * w, axis=0, keepdims=True), jnp.pad(rest, ((0, 0), (0, pad)))


def stack_left(value):
    high, low = (piece.astype(F32) for piece in split(value, 2))
    return jnp.concatenate([high, high, low], axis=0).astype(BF16)


def stack_right(value):
    high, low = (piece.astype(F32) for piece in split(value, 2))
    return jnp.concatenate([high, low, high], axis=0).astype(BF16)


def contract_times(left, right):
    return lax.dot_general(left, right, (((0,), (0,)), ((), ())), preferred_element_type=F32)


def times_first(value):
    return value.astype(F32).T.astype(BF16)


def tile_kernel(plan, own_ref, other_ref, w_ref, diag_ref, lam_ref, inverse_ref, out_ref,
                own_slabs, other_slabs, rows_ref, cols_ref, left_ref, left_main_ref, right_ref, tiles_ref, out_sem):
    height = out_ref.shape[0]
    nt = rows_ref.shape[0]
    tm_index = lax.axis_index("tm")
    row_start = tm_index * height
    first_col = lax.axis_index("lat") * cols_ref.shape[1]
    in_panel_rows = row_start < PANEL

    for got_ref, slabs_ref, core in (
        (own_ref, own_slabs, lax.rem(tm_index, 2)),
        (other_ref, other_slabs, 1 - lax.rem(tm_index, 2)),
    ):
        plan.gather_sums(got_ref, slabs_ref)
        for n in range(plan.col_tiles):
            low = pl.multiple_of(core * plan.half + n * LANE, LANE)
            cols_ref[:, pl.ds(low, LANE)] = plan.tile(slabs_ref, n)
    for n in range(plan.row_tiles):
        rows_ref[:, n * LANE : (n + 1) * LANE] = plan.tile(own_slabs, plan.col_tiles + n)
    left_ref[...] = times_first(stack_left(rows_ref[...]))

    @pl.when(in_panel_rows)
    def _():
        low = pl.multiple_of(jnp.minimum(row_start, PANEL - height), LANE)
        left_main_ref[...] = times_first(stack_left(w_ref[:, pl.ds(low, height)]))
        right_ref[...] = stack_right(cols_ref[...])

    @pl.when(jnp.logical_not(in_panel_rows))
    def _():
        left_main_ref[...] = left_ref[...]
        turned = contract_times(stack_left(inverse_ref[:, :nt]), stack_right(cols_ref[...]))
        right_ref[...] = stack_right(turned)

    @pl.when(first_col < PANEL)
    def _():
        right_ref[:, :PANEL] = stack_right(w_ref[...])

    def copy(step):
        own = pl.ds(pl.multiple_of(step * WIDE, WIDE), WIDE)
        return pltpu.make_async_copy(tiles_ref.at[step], out_ref.at[:, own], out_sem.at[step])

    @pl.loop(0, cols_ref.shape[1] // WIDE)
    def _(step):
        col_start = first_col + step * WIDE
        in_panel_cols = col_start < PANEL
        on_diagonal = (row_start < col_start + WIDE) & (col_start < row_start + height)
        own = pl.ds(pl.multiple_of(step * WIDE, WIDE), WIDE)
        out = tiles_ref.at[step]

        def ids():
            rows = row_start + lax.broadcasted_iota(jnp.int32, (height, WIDE), 0)
            return rows, col_start + lax.broadcasted_iota(jnp.int32, (height, WIDE), 1)

        @pl.when(in_panel_cols)
        def _():
            out[...] = jnp.dot(left_ref[...], right_ref[:, own], preferred_element_type=F32)

        @pl.when(jnp.logical_not(in_panel_cols))
        def _():
            out[...] = jnp.dot(left_main_ref[...], right_ref[:, own], preferred_element_type=F32)

        @pl.when(in_panel_cols & in_panel_rows)
        def _():
            row_ids, col_ids = ids()
            diag = jnp.where(row_ids == col_ids, diag_ref[:, own_panel(step)], 0.0)
            out[...] = jnp.where(row_ids >= col_ids, out[...], 0.0) + diag

        @pl.when(on_diagonal & jnp.logical_not(in_panel_rows))
        def _():
            row_ids, col_ids = ids()
            lam = lam_ref[:, pl.ds(pl.multiple_of(col_start, LANE), WIDE)]
            out[...] += jnp.where(row_ids == col_ids, lam, 0.0)

        copy(step).start()

    @pl.loop(0, cols_ref.shape[1] // WIDE)
    def _(step):
        copy(step).wait()


def own_panel(step):
    return pl.ds(pl.multiple_of(jnp.minimum(step * WIDE, PANEL - WIDE), WIDE), WIDE)


def out_tile(plan, own, other, w, diag, lam, inverse):
    nt, height, width = plan.times * plan.tm_count, plan.rows_width, plan.part_width
    return pl.pallas_call(
        functools.partial(tile_kernel, plan),
        in_specs=[spot_in(pltpu.VMEM)] * 6,
        out_specs=spot_in(pltpu.HBM),
        out_shape=jax.ShapeDtypeStruct((height, width), F32),
        scratch_shapes=[
            pltpu.VMEM(plan.sums_shape, F32),
            pltpu.VMEM(plan.sums_shape, F32),
            pltpu.VMEM((nt, height), F32),
            pltpu.VMEM((nt, width), F32),
            pltpu.VMEM((height, 3 * nt), BF16),
            pltpu.VMEM((height, 3 * nt), BF16),
            pltpu.VMEM((3 * nt, width), BF16),
            pltpu.VMEM((width // WIDE, height, WIDE), F32),
            pltpu.SemaphoreType.DMA((width // WIDE,)),
        ],
        compiler_params=pltpu.CompilerParams(vmem_limit_bytes=SMALL_VMEM),
        cost_estimate=pl.CostEstimate(
            flops=4 * nt * height * width, bytes_accessed=4 * height * width, transcendentals=0
        ),
        name="out_tile",
    )(own, other, w, diag, lam, inverse)


def on_device(basis, fields, legendre, order_table, window_start, ridge):
    times = fields.shape[0]
    kcoef = legendre.shape[1]
    tm_count, lat_count = lax.axis_size("tm"), lax.axis_size("lat")
    plan = Plan(kcoef, tm_count, lat_count, times)
    sent, lam = spectra_and_contract(plan, window_start, ridge, order_table, fields, basis, legendre)
    own = lax.all_to_all(sent, ("tm", "lat"), 0, 0, tiled=True)
    other = lax.ppermute(own, "tm", [(i, i ^ 1) for i in range(tm_count)])
    small = times * tm_count <= LANE // 4
    w, diag, inverse = (panel_small if small else panel_large)(plan, own, lam)
    return out_tile(plan, own, other, w, diag, lam, inverse)


def solution(mesh):
    def run(fields, legendre, order_table, window_start, ridge):
        basis = jnp.asarray(basis_table(fields.shape[2]))
        placed = (P(), P("tm", "lat", None), P("lat", None), P(), P(), P())
        body = jax.shard_map(on_device, mesh=mesh, in_specs=placed, out_specs=P("tm", "lat"), check_vma=False)
        return body(basis, fields, legendre, order_table, window_start, ridge)

    return run
```

```python
import functools
import math

import jax
import jax.numpy as jnp
import ml_dtypes
import numpy as np
from jax import lax
from jax.experimental import pallas as pl
from jax.experimental.pallas import tpu as pltpu
from jax.sharding import PartitionSpec as P

LMAX = 720
PANEL = 512
LANE = 128
SUB = 8
GATHER = 256
GROUP = 4
WIDE = 512
SPECTRA_VMEM = 36 * 1024 * 1024
SMALL_VMEM = 20 * 1024 * 1024
F32 = jnp.float32
BF16 = jnp.bfloat16


def basis_table(nlon):
    half = nlon // 2
    order = np.concatenate([np.arange(0, half, 2), np.arange(0, half, 2), np.arange(1, half, 2), np.arange(1, half, 2)])
    sine = np.repeat([False, True, False, True], [half // 2] * 4)[:, None]
    longitude = np.arange(half, dtype=np.int64)[None, :]
    phase = (order[:, None] * longitude % nlon).astype(np.float32) * np.float32(2.0 * math.pi / nlon)
    return np.where(sine, np.sin(phase), np.cos(phase)).astype(ml_dtypes.bfloat16)


def basis_row(order, part, nlon):
    return nlon // 2 * (order & 1) + nlon // 4 * part + (order >> 1)


def pick_rows(column_ref, start, table_ref, picked_ref):
    row = start // LANE
    for j in range(GATHER):
        group = pl.multiple_of(column_ref[row + j // LANE, j % LANE], SUB)
        picked_ref[SUB * j : SUB * (j + 1), :] = table_ref[pl.ds(group, SUB), :]


def latitude_sums(picked_ref, weights, times):
    lats = weights.shape[0]
    pieces = -(-lats // LANE)
    picked = [picked_ref[pl.ds(s, GATHER, stride=SUB), :] for s in range(times * pieces)]
    value = jnp.concatenate(
        [jnp.concatenate(picked[pieces * t : pieces * (t + 1)], axis=1) for t in range(times)], axis=0
    )
    spare = jnp.zeros((pieces * LANE - lats, GATHER), BF16)
    every = jnp.dot(value.astype(BF16), jnp.concatenate([weights, spare], axis=0), preferred_element_type=F32)
    shape = (LANE, LANE)
    eye = lax.broadcasted_iota(jnp.int32, shape, 0) == lax.broadcasted_iota(jnp.int32, shape, 1)
    sums = []
    for t in range(times):
        own = []
        for low in range(0, GATHER, LANE):
            square = every[t * GATHER + low : t * GATHER + low + LANE, low : low + LANE]
            own.append(jnp.sum(jnp.where(eye, square, 0.0), axis=0, keepdims=True))
        sums.append(jnp.concatenate(own, axis=1))
    return jnp.concatenate(sums, axis=0)


def contract(plan, column_ref, table_ref, weights_ref, sums_ref, even_ref, odd_ref, weights_copy):
    picked = [even_ref, odd_ref]

    def place(part):
        return jnp.minimum(part, plan.parts - 1) * GATHER

    pick_rows(column_ref, 0, table_ref, even_ref)

    @pl.loop(0, plan.parts // GROUP)
    def _(group):
        weights_copy(group).wait()
        for n in range(GROUP):
            part = group * GROUP + n
            pick_rows(column_ref, place(part + 1), table_ref, picked[(n + 1) % 2])
            at = pl.ds(pl.multiple_of(part * GATHER, GATHER), GATHER)
            sums_ref[:, at] = latitude_sums(picked[n % 2], weights_ref[:, at], plan.times)


class Plan:
    def __init__(self, kcoef, tm_count, lat_count, times):
        self.tm_count, self.lat_count, self.times = tm_count, lat_count, times
        self.kcoef, self.part_width, self.rows_width = kcoef, kcoef // lat_count, kcoef // tm_count
        self.parts = kcoef // GATHER
        self.half = self.part_width // 2
        self.col_tiles, self.row_tiles, self.panel_tiles = self.half // LANE, self.rows_width // LANE, PANEL // LANE
        self.first_panel = self.col_tiles + self.row_tiles
        self.across = -(-(self.first_panel + self.panel_tiles) // SUB)
        self.slab = (times * SUB, self.across * LANE)
        self.shape = (tm_count * lat_count,) + self.slab
        self.sums_shape = (self.across, tm_count * self.slab[0], LANE)

    def weights_copies(self, legendre_ref, weights_ref, sems):
        width = GROUP * GATHER

        def copy(group):
            own = pl.ds(pl.multiple_of(group * width, width), width)
            return pltpu.make_async_copy(legendre_ref.at[:, own], weights_ref.at[:, own], sems.at[group])

        @pl.loop(0, self.parts // GROUP)
        def _(group):
            copy(group).start()

        return copy

    def spot(self, tile, time):
        low = tile % self.across * LANE
        return time * SUB + tile // self.across, slice(low, low + LANE)

    def pack(self, sums_ref, slab_ref, sent_ref):
        def fill(tile, source, count):
            for n in range(count):
                for t in range(self.times):
                    row, lanes = self.spot(tile + n, t)
                    low = source + n * LANE
                    slab_ref[row : row + 1, lanes] = sums_ref[t : t + 1, low : low + LANE]

        slab_ref[...] = jnp.zeros_like(slab_ref)
        fill(self.first_panel, 0, self.panel_tiles)
        for part in range(self.lat_count):
            for core in range(2):
                fill(0, part * self.part_width + core * self.half, self.col_tiles)
                for owner in range(core, self.tm_count, 2):
                    fill(self.col_tiles, owner * self.rows_width, self.row_tiles)
                    sent_ref[owner * self.lat_count + part] = slab_ref[...].astype(BF16)

    def gather_sums(self, got_ref, slabs_ref):
        rows = self.slab[0]
        for sender in range(self.tm_count):
            first = sender * self.lat_count
            total = got_ref[first].astype(F32)
            for part in range(1, self.lat_count):
                total = total + got_ref[first + part].astype(F32)
            for n in range(self.across):
                slabs_ref[n, sender * rows : (sender + 1) * rows, :] = total[:, n * LANE : (n + 1) * LANE]

    def tile(self, slabs_ref, tile):
        pieces = []
        for t in range(self.times):
            row = t * SUB + tile // self.across
            pieces.append(slabs_ref[tile % self.across, pl.ds(row, self.tm_count, stride=self.slab[0]), :])
        return jnp.concatenate(pieces, axis=0)

    def unpack(self, got):
        split_shape = (self.tm_count, self.lat_count, self.times, SUB * self.across * LANE)
        total = got.astype(F32).reshape(split_shape).sum(axis=1)
        return total.transpose(1, 0, 2).reshape(self.times * self.tm_count, -1)


def window_of(value, start, length, lines_ref):
    for n in range(value.shape[1] // LANE):
        lines_ref[n : n + 1, :] = value[:, n * LANE : (n + 1) * LANE]
    over = lax.rem(start, LANE)
    lines_ref[...] = pltpu.roll(lines_ref[...], lax.rem(LANE - over, LANE), 1)
    first = lines_ref[pl.ds(start // LANE, length // LANE), :]
    second = lines_ref[pl.ds(start // LANE + 1, length // LANE), :]
    lane = lax.broadcasted_iota(jnp.int32, first.shape, 1)
    return jnp.where(lane < LANE - over, first, second)


def spectra_kernel(plan, scale, start_ref, ridge_ref, order_ref, fields_ref, basis_ref, legendre_ref, sent_ref,
                   lam_ref, order_buf, index_ref, window_ref, column_ref, table_ref, fields_buf, basis_buf,
                   weights_ref, even_lines, odd_lines, even_ref, odd_ref, sums_ref, slab_ref, order_sem,
                   column_sem, fields_sem, basis_sem, weights_sem):
    times, lats, nlon = fields_ref.shape
    pieces = -(-lats // LANE)
    order_copy = pltpu.make_async_copy(order_ref, order_buf, order_sem)
    order_copy.start()
    fields_copy = pltpu.make_async_copy(fields_ref, fields_buf, fields_sem)
    fields_copy.start()
    basis_copy = pltpu.make_async_copy(basis_ref, basis_buf, basis_sem)
    basis_copy.start()
    for t in range(times):
        end = pieces * LANE * (t + 1)
        for folded in (even_lines, odd_lines):
            folded[:, end - LANE : end, :] = jnp.zeros((2, LANE, nlon // 2), BF16)
    order_copy.wait()
    start = start_ref[0]
    column = SUB * basis_row(order_buf[1:2, :], order_buf[2:3, :], nlon)
    window_ref[...] = window_of(column, start, plan.kcoef, index_ref)
    column_copy = pltpu.make_async_copy(window_ref, column_ref, column_sem)
    column_copy.start()
    degree = window_of(order_buf[0:1, :], start, plan.kcoef, index_ref)
    lam = ridge_ref[0] * (1.0 + (degree * (degree + 1)).astype(F32) / float(LMAX * (LMAX + 1)))
    for n in range(plan.kcoef // LANE):
        lam_ref[:, n * LANE : (n + 1) * LANE] = lam[n : n + 1, :]
    fields_copy.wait()
    for t in range(times):
        first = fields_buf[t, :, : nlon // 2].astype(F32)
        second = fields_buf[t, :, nlon // 2 :].astype(F32)
        own = slice(pieces * LANE * t, pieces * LANE * t + lats)
        for folded, value in ((even_lines, first + second), (odd_lines, first - second)):
            for n, piece in enumerate(split(value, 2)):
                folded[n, own, :] = piece
    basis_copy.wait()
    weights_copy = plan.weights_copies(legendre_ref, weights_ref, weights_sem)
    tiles = times * pieces
    wide = 2 if tiles % 2 == 0 else 1
    for parity, folded in enumerate((even_lines, odd_lines)):
        half = slice(nlon // 2 * parity, nlon // 2 * (parity + 1))
        for low in range(0, tiles, wide):
            spectra = scale * sum(
                lax.dot_general(
                    basis_buf[half, :], folded[n, LANE * low : LANE * (low + wide), :], (((1,), (1,)), ((), ())),
                    preferred_element_type=F32,
                )
                for n in range(2)
            )
            for s in range(wide):
                at = pl.ds(SUB * half.start + low + s, nlon // 2, stride=SUB)
                table_ref[at, :] = spectra[:, LANE * s : LANE * (s + 1)]
    column_copy.wait()
    contract(plan, column_ref, table_ref, weights_ref, sums_ref, even_ref, odd_ref, weights_copy)
    plan.pack(sums_ref, slab_ref, sent_ref)


def in_hbm(value):
    return pltpu.with_memory_space_constraint(value, pltpu.HBM)


def spot_in(space):
    return pl.BlockSpec(memory_space=space)


def spectra_and_contract(plan, start, ridge, order, fields, basis, legendre):
    times, lats, nlon = fields.shape
    entries = order.shape[1] // LANE
    pieces = -(-lats // LANE)
    return pl.pallas_call(
        functools.partial(spectra_kernel, plan, 1.0 / math.sqrt(nlon)),
        in_specs=[spot_in(pltpu.SMEM)] * 2 + [spot_in(pltpu.HBM)] * 4,
        out_specs=[spot_in(pltpu.VMEM)] * 2,
        out_shape=[jax.ShapeDtypeStruct(plan.shape, BF16), jax.ShapeDtypeStruct((1, plan.kcoef), F32)],
        scratch_shapes=[
            pltpu.VMEM(order.shape, jnp.int32),
            pltpu.VMEM((entries + SUB, LANE), jnp.int32),
            pltpu.VMEM((plan.kcoef // LANE, LANE), jnp.int32),
            pltpu.SMEM((plan.kcoef // LANE, LANE), jnp.int32),
            pltpu.VMEM((nlon * SUB, LANE), F32),
            pltpu.VMEM(fields.shape, BF16),
            pltpu.VMEM(basis.shape, BF16),
            pltpu.VMEM((lats, plan.kcoef), BF16),
            pltpu.VMEM((2, times * pieces * LANE, nlon // 2), BF16),
            pltpu.VMEM((2, times * pieces * LANE, nlon // 2), BF16),
            pltpu.VMEM((GATHER * SUB, LANE), F32),
            pltpu.VMEM((GATHER * SUB, LANE), F32),
            pltpu.VMEM((times, plan.kcoef), F32),
            pltpu.VMEM(plan.slab, F32),
            pltpu.SemaphoreType.DMA(()),
            pltpu.SemaphoreType.DMA(()),
            pltpu.SemaphoreType.DMA(()),
            pltpu.SemaphoreType.DMA(()),
            pltpu.SemaphoreType.DMA((plan.parts // GROUP,)),
        ],
        compiler_params=pltpu.CompilerParams(vmem_limit_bytes=SPECTRA_VMEM),
        cost_estimate=pl.CostEstimate(flops=12 << 30, bytes_accessed=8 << 20, transcendentals=0),
        name="spectra_and_contract",
    )(start, ridge, in_hbm(order), in_hbm(fields), in_hbm(basis), in_hbm(legendre))


def split(value, pieces):
    out = []
    for _ in range(pieces):
        piece = value.astype(BF16)
        out.append(piece)
        value = value - piece.astype(F32)
    return out


def panel_kernel(plan, got_ref, lam_ref, w_ref, diag_ref, inverse_ref, slabs_ref, q_ref, g_ref, y_ref, x_ref, z_ref):
    nt = w_ref.shape[0]
    lanes = PANEL + LANE
    plan.gather_sums(got_ref, slabs_ref)
    coef = jnp.concatenate(
        [plan.tile(slabs_ref, plan.first_panel + n) for n in range(plan.panel_tiles)], axis=1
    )
    lam = lam_ref[...]
    scaled = coef / lam
    starts, total = [], 0
    for r in range(nt):
        low = r // 8 * 8
        z_ref[total : total + nt - low, :] = coef[low:, :] * scaled[r : r + 1, :]
        starts.append(total)
        total += nt - low
    ids = lax.broadcasted_iota(jnp.int32, (PANEL, PANEL), 0)
    upto = lax.broadcasted_iota(jnp.int32, (PANEL, PANEL), 1)
    tri = jnp.where(ids < upto, 1.0, 0.0).astype(BF16)
    prefix = 0.0
    for piece in split(z_ref[...], 3)[::-1]:
        prefix = prefix + jnp.dot(piece, tri, preferred_element_type=F32)
    q_ref[:, :PANEL] = prefix
    q_ref[:, PANEL:] = jnp.broadcast_to(prefix[:, PANEL - 1 :] + z_ref[:, PANEL - 1 :], (total, LANE))
    y_ref[:, :PANEL] = coef
    eye = lax.broadcasted_iota(jnp.int32, (nt, LANE), 0) == lax.broadcasted_iota(jnp.int32, (nt, LANE), 1)
    y_ref[:, PANEL:] = jnp.where(eye, 1.0, 0.0)
    inverses = []
    for r in range(nt):
        low = r // 8 * 8
        place = low + lax.broadcasted_iota(jnp.int32, (nt - low, lanes), 0)
        row = q_ref[starts[r] : starts[r] + nt - low, :] + jnp.where(place == r, float(nt), 0.0)
        for p in range(r):
            base = starts[p] + low - p // 8 * 8
            factor = g_ref[starts[p] + r - p // 8 * 8 : starts[p] + r - p // 8 * 8 + 1, :]
            row = row - factor * q_ref[base : base + nt - low, :]
        q_ref[starts[r] : starts[r] + nt - low, :] = row
        inv = 1.0 / row[r - low : r - low + 1, :]
        inverses.append(inv)
        ratio = jnp.where(place > r, row * inv, 0.0)
        g_ref[starts[r] : starts[r] + nt - low, :] = ratio
        y_ref[low:, :] = y_ref[low:, :] - ratio * y_ref[r : r + 1, :]
    x_ref[...] = jnp.zeros_like(x_ref)
    for r in range(nt - 1, -1, -1):
        low = r // 8 * 8
        ratio = g_ref[starts[r] : starts[r] + nt - low, :]
        tail = jnp.sum(ratio * x_ref[low:, :], axis=0, keepdims=True)
        x_ref[r : r + 1, :] = y_ref[r : r + 1, :] * inverses[r] - tail
    solved = x_ref[:, :PANEL]
    pivot = jnp.sqrt(lam + jnp.sum(coef * solved, axis=0, keepdims=True))
    w_ref[...] = solved / pivot
    diag_ref[...] = lam / pivot
    inverse_ref[...] = x_ref[:, PANEL:]


def panel_small(plan, got, lam):
    nt = plan.times * plan.tm_count
    rows = sum(nt - r // 8 * 8 for r in range(nt))
    lanes = PANEL + LANE
    return pl.pallas_call(
        functools.partial(panel_kernel, plan),
        grid=(1,),
        in_specs=[
            pl.BlockSpec(plan.shape, lambda i: (0, 0, 0)),
            pl.BlockSpec((1, PANEL), lambda i: (0, 0)),
        ],
        out_specs=[
            pl.BlockSpec((nt, PANEL), lambda i: (0, 0)),
            pl.BlockSpec((1, PANEL), lambda i: (0, 0)),
            pl.BlockSpec((nt, LANE), lambda i: (0, 0)),
        ],
        out_shape=[
            jax.ShapeDtypeStruct((nt, PANEL), F32),
            jax.ShapeDtypeStruct((1, PANEL), F32),
            jax.ShapeDtypeStruct((nt, LANE), F32),
        ],
        scratch_shapes=[
            pltpu.VMEM(plan.sums_shape, F32),
            pltpu.VMEM((rows, lanes), F32),
            pltpu.VMEM((rows, lanes), F32),
            pltpu.VMEM((nt, lanes), F32),
            pltpu.VMEM((nt, lanes), F32),
            pltpu.VMEM((rows, PANEL), F32),
        ],
        compiler_params=pltpu.CompilerParams(vmem_limit_bytes=SMALL_VMEM),
        cost_estimate=pl.CostEstimate(flops=4 << 30, bytes_accessed=1 << 18, transcendentals=0),
        name="panel_small",
    )(got, lam)


def panel_large(plan, got, lam):
    low = plan.first_panel * LANE
    coef, lam = plan.unpack(got)[:, low : low + PANEL], lam[:, :PANEL]
    nt = coef.shape[0]
    gram = jnp.dot(coef.T, coef, precision=lax.Precision.HIGHEST) / nt + jnp.diag(lam[0])
    factor = jnp.linalg.cholesky(gram)
    solved = jax.scipy.linalg.solve_triangular(factor, coef.T, lower=True)
    w = solved.T / nt
    rest = jnp.eye(nt, dtype=F32) / nt - jnp.dot(w, w.T, precision=lax.Precision.HIGHEST)
    pivot = jnp.diagonal(factor)[None, :]
    pad = -(-nt // LANE) * LANE - nt
    return w, pivot - jnp.sum(coef * w, axis=0, keepdims=True), jnp.pad(rest, ((0, 0), (0, pad)))


def stack_left(value):
    high, low = (piece.astype(F32) for piece in split(value, 2))
    return jnp.concatenate([high, high, low], axis=0).astype(BF16)


def stack_right(value):
    high, low = (piece.astype(F32) for piece in split(value, 2))
    return jnp.concatenate([high, low, high], axis=0).astype(BF16)


def contract_times(left, right):
    return lax.dot_general(left, right, (((0,), (0,)), ((), ())), preferred_element_type=F32)


def times_first(value):
    return value.astype(F32).T.astype(BF16)


def tile_kernel(plan, own_ref, other_ref, w_ref, diag_ref, lam_ref, inverse_ref, out_ref,
                own_slabs, other_slabs, rows_ref, cols_ref, left_ref, left_main_ref, right_ref, tiles_ref, out_sem):
    height = out_ref.shape[0]
    nt = rows_ref.shape[0]
    tm_index = lax.axis_index("tm")
    row_start = tm_index * height
    first_col = lax.axis_index("lat") * cols_ref.shape[1]
    in_panel_rows = row_start < PANEL

    for got_ref, slabs_ref, core in (
        (own_ref, own_slabs, lax.rem(tm_index, 2)),
        (other_ref, other_slabs, 1 - lax.rem(tm_index, 2)),
    ):
        plan.gather_sums(got_ref, slabs_ref)
        for n in range(plan.col_tiles):
            low = pl.multiple_of(core * plan.half + n * LANE, LANE)
            cols_ref[:, pl.ds(low, LANE)] = plan.tile(slabs_ref, n)
    for n in range(plan.row_tiles):
        rows_ref[:, n * LANE : (n + 1) * LANE] = plan.tile(own_slabs, plan.col_tiles + n)
    left_ref[...] = times_first(stack_left(rows_ref[...]))

    @pl.when(in_panel_rows)
    def _():
        low = pl.multiple_of(jnp.minimum(row_start, PANEL - height), LANE)
        left_main_ref[...] = times_first(stack_left(w_ref[:, pl.ds(low, height)]))
        right_ref[...] = stack_right(cols_ref[...])

    @pl.when(jnp.logical_not(in_panel_rows))
    def _():
        left_main_ref[...] = left_ref[...]
        turned = contract_times(stack_left(inverse_ref[:, :nt]), stack_right(cols_ref[...]))
        right_ref[...] = stack_right(turned)

    @pl.when(first_col < PANEL)
    def _():
        right_ref[:, :PANEL] = stack_right(w_ref[...])

    def copy(step):
        own = pl.ds(pl.multiple_of(step * WIDE, WIDE), WIDE)
        return pltpu.make_async_copy(tiles_ref.at[step], out_ref.at[:, own], out_sem.at[step])

    @pl.loop(0, cols_ref.shape[1] // WIDE)
    def _(step):
        col_start = first_col + step * WIDE
        in_panel_cols = col_start < PANEL
        on_diagonal = (row_start < col_start + WIDE) & (col_start < row_start + height)
        own = pl.ds(pl.multiple_of(step * WIDE, WIDE), WIDE)
        out = tiles_ref.at[step]

        def ids():
            rows = row_start + lax.broadcasted_iota(jnp.int32, (height, WIDE), 0)
            return rows, col_start + lax.broadcasted_iota(jnp.int32, (height, WIDE), 1)

        @pl.when(in_panel_cols)
        def _():
            out[...] = jnp.dot(left_ref[...], right_ref[:, own], preferred_element_type=F32)

        @pl.when(jnp.logical_not(in_panel_cols))
        def _():
            out[...] = jnp.dot(left_main_ref[...], right_ref[:, own], preferred_element_type=F32)

        @pl.when(in_panel_cols & in_panel_rows)
        def _():
            row_ids, col_ids = ids()
            diag = jnp.where(row_ids == col_ids, diag_ref[:, own_panel(step)], 0.0)
            out[...] = jnp.where(row_ids >= col_ids, out[...], 0.0) + diag

        @pl.when(on_diagonal & jnp.logical_not(in_panel_rows))
        def _():
            row_ids, col_ids = ids()
            lam = lam_ref[:, pl.ds(pl.multiple_of(col_start, LANE), WIDE)]
            out[...] += jnp.where(row_ids == col_ids, lam, 0.0)

        copy(step).start()

    @pl.loop(0, cols_ref.shape[1] // WIDE)
    def _(step):
        copy(step).wait()


def own_panel(step):
    return pl.ds(pl.multiple_of(jnp.minimum(step * WIDE, PANEL - WIDE), WIDE), WIDE)


def out_tile(plan, own, other, w, diag, lam, inverse):
    nt, height, width = plan.times * plan.tm_count, plan.rows_width, plan.part_width
    return pl.pallas_call(
        functools.partial(tile_kernel, plan),
        in_specs=[spot_in(pltpu.VMEM)] * 6,
        out_specs=spot_in(pltpu.HBM),
        out_shape=jax.ShapeDtypeStruct((height, width), F32),
        scratch_shapes=[
            pltpu.VMEM(plan.sums_shape, F32),
            pltpu.VMEM(plan.sums_shape, F32),
            pltpu.VMEM((nt, height), F32),
            pltpu.VMEM((nt, width), F32),
            pltpu.VMEM((height, 3 * nt), BF16),
            pltpu.VMEM((height, 3 * nt), BF16),
            pltpu.VMEM((3 * nt, width), BF16),
            pltpu.VMEM((width // WIDE, height, WIDE), F32),
            pltpu.SemaphoreType.DMA((width // WIDE,)),
        ],
        compiler_params=pltpu.CompilerParams(vmem_limit_bytes=SMALL_VMEM),
        cost_estimate=pl.CostEstimate(
            flops=4 * nt * height * width, bytes_accessed=4 * height * width, transcendentals=0
        ),
        name="out_tile",
    )(own, other, w, diag, lam, inverse)


def on_device(basis, fields, legendre, order_table, window_start, ridge):
    times = fields.shape[0]
    kcoef = legendre.shape[1]
    tm_count, lat_count = lax.axis_size("tm"), lax.axis_size("lat")
    plan = Plan(kcoef, tm_count, lat_count, times)
    sent, lam = spectra_and_contract(plan, window_start, ridge, order_table, fields, basis, legendre)
    own = lax.all_to_all(sent, ("tm", "lat"), 0, 0, tiled=True)
    other = lax.ppermute(own, "tm", [(i, i ^ 1) for i in range(tm_count)])
    small = times * tm_count <= LANE // 4
    w, diag, inverse = (panel_small if small else panel_large)(plan, own, lam)
    return out_tile(plan, own, other, w, diag, lam, inverse)


def solution(mesh):
    def run(fields, legendre, order_table, window_start, ridge):
        basis = jnp.asarray(basis_table(fields.shape[2]))
        placed = (P(), P("tm", "lat", None), P("lat", None), P(), P(), P())
        body = jax.shard_map(on_device, mesh=mesh, in_specs=placed, out_specs=P("tm", "lat"), check_vma=False)
        return body(basis, fields, legendre, order_table, window_start, ridge)

    return run
```

```python
import functools
import math

import jax
import jax.numpy as jnp
import ml_dtypes
import numpy as np
from jax import lax
from jax.experimental import pallas as pl
from jax.experimental.pallas import tpu as pltpu
from jax.sharding import PartitionSpec as P

LMAX = 720
PANEL = 512
LANE = 128
SUB = 8
GATHER = 256
GROUP = 4
WIDE = 512
SPECTRA_VMEM = 36 * 1024 * 1024
SMALL_VMEM = 20 * 1024 * 1024
F32 = jnp.float32
BF16 = jnp.bfloat16


def basis_table(nlon):
    half = nlon // 2
    order = np.concatenate([np.arange(0, half, 2), np.arange(0, half, 2), np.arange(1, half, 2), np.arange(1, half, 2)])
    sine = np.repeat([False, True, False, True], [half // 2] * 4)[:, None]
    longitude = np.arange(half, dtype=np.int64)[None, :]
    phase = (order[:, None] * longitude % nlon).astype(np.float32) * np.float32(2.0 * math.pi / nlon)
    return np.where(sine, np.sin(phase), np.cos(phase)).astype(ml_dtypes.bfloat16)


def basis_row(order, part, nlon):
    return nlon // 2 * (order & 1) + nlon // 4 * part + (order >> 1)


def pick_rows(column_ref, start, table_ref, picked_ref):
    row = start // LANE
    for j in range(GATHER):
        group = pl.multiple_of(column_ref[row + j // LANE, j % LANE], SUB)
        picked_ref[SUB * j : SUB * (j + 1), :] = table_ref[pl.ds(group, SUB), :]


def latitude_sums(picked_ref, weights, times):
    lats = weights.shape[0]
    pieces = -(-lats // LANE)
    picked = [picked_ref[pl.ds(s, GATHER, stride=SUB), :] for s in range(times * pieces)]
    value = jnp.concatenate(
        [jnp.concatenate(picked[pieces * t : pieces * (t + 1)], axis=1) for t in range(times)], axis=0
    )
    spare = jnp.zeros((pieces * LANE - lats, GATHER), BF16)
    every = jnp.dot(value.astype(BF16), jnp.concatenate([weights, spare], axis=0), preferred_element_type=F32)
    shape = (LANE, LANE)
    eye = lax.broadcasted_iota(jnp.int32, shape, 0) == lax.broadcasted_iota(jnp.int32, shape, 1)
    sums = []
    for t in range(times):
        own = []
        for low in range(0, GATHER, LANE):
            square = every[t * GATHER + low : t * GATHER + low + LANE, low : low + LANE]
            own.append(jnp.sum(jnp.where(eye, square, 0.0), axis=0, keepdims=True))
        sums.append(jnp.concatenate(own, axis=1))
    return jnp.concatenate(sums, axis=0)


def contract(plan, column_ref, table_ref, weights_ref, sums_ref, even_ref, odd_ref, weights_copy):
    picked = [even_ref, odd_ref]

    def place(part):
        return jnp.minimum(part, plan.parts - 1) * GATHER

    pick_rows(column_ref, 0, table_ref, even_ref)

    @pl.loop(0, plan.parts // GROUP)
    def _(group):
        weights_copy(group).wait()
        for n in range(GROUP):
            part = group * GROUP + n
            pick_rows(column_ref, place(part + 1), table_ref, picked[(n + 1) % 2])
            at = pl.ds(pl.multiple_of(part * GATHER, GATHER), GATHER)
            sums_ref[:, at] = latitude_sums(picked[n % 2], weights_ref[:, at], plan.times)


class Plan:
    def __init__(self, kcoef, tm_count, lat_count, times):
        self.tm_count, self.lat_count, self.times = tm_count, lat_count, times
        self.kcoef, self.part_width, self.rows_width = kcoef, kcoef // lat_count, kcoef // tm_count
        self.parts = kcoef // GATHER
        self.half = self.part_width // 2
        self.col_tiles, self.row_tiles, self.panel_tiles = self.half // LANE, self.rows_width // LANE, PANEL // LANE
        self.first_panel = self.col_tiles + self.row_tiles
        self.across = -(-(self.first_panel + self.panel_tiles) // SUB)
        self.slab = (times * SUB, self.across * LANE)
        self.shape = (tm_count * lat_count,) + self.slab
        self.sums_shape = (self.across, tm_count * self.slab[0], LANE)

    def weights_copies(self, legendre_ref, weights_ref, sems):
        width = GROUP * GATHER

        def copy(group):
            own = pl.ds(pl.multiple_of(group * width, width), width)
            return pltpu.make_async_copy(legendre_ref.at[:, own], weights_ref.at[:, own], sems.at[group])

        @pl.loop(0, self.parts // GROUP)
        def _(group):
            copy(group).start()

        return copy

    def spot(self, tile, time):
        low = tile % self.across * LANE
        return time * SUB + tile // self.across, slice(low, low + LANE)

    def pack(self, sums_ref, slab_ref, sent_ref):
        def fill(tile, source, count):
            for n in range(count):
                for t in range(self.times):
                    row, lanes = self.spot(tile + n, t)
                    low = source + n * LANE
                    slab_ref[row : row + 1, lanes] = sums_ref[t : t + 1, low : low + LANE]

        if self.first_panel + self.panel_tiles < self.across * SUB:
            slab_ref[...] = jnp.zeros_like(slab_ref)
        fill(self.first_panel, 0, self.panel_tiles)
        for part in range(self.lat_count):
            for core in range(2):
                fill(0, part * self.part_width + core * self.half, self.col_tiles)
                for owner in range(core, self.tm_count, 2):
                    fill(self.col_tiles, owner * self.rows_width, self.row_tiles)
                    sent_ref[owner * self.lat_count + part] = slab_ref[...].astype(BF16)

    def gather_sums(self, got_ref, slabs_ref):
        rows = self.slab[0]
        for sender in range(self.tm_count):
            first = sender * self.lat_count
            total = got_ref[first].astype(F32)
            for part in range(1, self.lat_count):
                total = total + got_ref[first + part].astype(F32)
            for n in range(self.across):
                slabs_ref[n, sender * rows : (sender + 1) * rows, :] = total[:, n * LANE : (n + 1) * LANE]

    def tile(self, slabs_ref, tile):
        pieces = []
        for t in range(self.times):
            row = t * SUB + tile // self.across
            pieces.append(slabs_ref[tile % self.across, pl.ds(row, self.tm_count, stride=self.slab[0]), :])
        return jnp.concatenate(pieces, axis=0)

    def unpack(self, got):
        split_shape = (self.tm_count, self.lat_count, self.times, SUB * self.across * LANE)
        total = got.astype(F32).reshape(split_shape).sum(axis=1)
        return total.transpose(1, 0, 2).reshape(self.times * self.tm_count, -1)


def window_of(value, start, length, lines_ref):
    for n in range(value.shape[1] // LANE):
        lines_ref[n : n + 1, :] = value[:, n * LANE : (n + 1) * LANE]
    over = lax.rem(start, LANE)
    lines_ref[...] = pltpu.roll(lines_ref[...], lax.rem(LANE - over, LANE), 1)
    first = lines_ref[pl.ds(start // LANE, length // LANE), :]
    second = lines_ref[pl.ds(start // LANE + 1, length // LANE), :]
    lane = lax.broadcasted_iota(jnp.int32, first.shape, 1)
    return jnp.where(lane < LANE - over, first, second)


def spectra_kernel(plan, scale, start_ref, ridge_ref, order_ref, fields_ref, basis_ref, legendre_ref, sent_ref,
                   lam_ref, order_buf, index_ref, window_ref, column_ref, table_ref, fields_buf, basis_buf,
                   weights_ref, even_lines, odd_lines, even_ref, odd_ref, sums_ref, slab_ref, order_sem,
                   column_sem, fields_sem, basis_sem, weights_sem):
    times, lats, nlon = fields_ref.shape
    pieces = -(-lats // LANE)
    order_copy = pltpu.make_async_copy(order_ref, order_buf, order_sem)
    order_copy.start()
    fields_copy = pltpu.make_async_copy(fields_ref, fields_buf, fields_sem)
    fields_copy.start()
    basis_copy = pltpu.make_async_copy(basis_ref, basis_buf, basis_sem)
    basis_copy.start()
    for t in range(times):
        end = pieces * LANE * (t + 1)
        for folded in (even_lines, odd_lines):
            folded[end - LANE : end, :] = jnp.zeros((LANE, nlon // 2), BF16)
    order_copy.wait()
    start = start_ref[0]
    column = SUB * basis_row(order_buf[1:2, :], order_buf[2:3, :], nlon)
    window_ref[...] = window_of(column, start, plan.kcoef, index_ref)
    column_copy = pltpu.make_async_copy(window_ref, column_ref, column_sem)
    column_copy.start()
    degree = window_of(order_buf[0:1, :], start, plan.kcoef, index_ref)
    lam = ridge_ref[0] * (1.0 + (degree * (degree + 1)).astype(F32) / float(LMAX * (LMAX + 1)))
    for n in range(plan.kcoef // LANE):
        lam_ref[:, n * LANE : (n + 1) * LANE] = lam[n : n + 1, :]
    fields_copy.wait()
    for t in range(times):
        first = fields_buf[t, :, : nlon // 2].astype(F32)
        second = fields_buf[t, :, nlon // 2 :].astype(F32)
        own = slice(pieces * LANE * t, pieces * LANE * t + lats)
        even_lines[own, :] = (first + second).astype(BF16)
        odd_lines[own, :] = (first - second).astype(BF16)
    basis_copy.wait()
    weights_copy = plan.weights_copies(legendre_ref, weights_ref, weights_sem)
    tiles = times * pieces
    wide = 2 if tiles % 2 == 0 else 1
    for parity, folded in enumerate((even_lines, odd_lines)):
        half = slice(nlon // 2 * parity, nlon // 2 * (parity + 1))
        for low in range(0, tiles, wide):
            spectra = scale * lax.dot_general(
                basis_buf[half, :], folded[LANE * low : LANE * (low + wide), :], (((1,), (1,)), ((), ())),
                preferred_element_type=F32,
            )
            for s in range(wide):
                at = pl.ds(SUB * half.start + low + s, nlon // 2, stride=SUB)
                table_ref[at, :] = spectra[:, LANE * s : LANE * (s + 1)]
    column_copy.wait()
    contract(plan, column_ref, table_ref, weights_ref, sums_ref, even_ref, odd_ref, weights_copy)
    plan.pack(sums_ref, slab_ref, sent_ref)


def in_hbm(value):
    return pltpu.with_memory_space_constraint(value, pltpu.HBM)


def spot_in(space):
    return pl.BlockSpec(memory_space=space)


def spectra_and_contract(plan, start, ridge, order, fields, basis, legendre):
    times, lats, nlon = fields.shape
    entries = order.shape[1] // LANE
    pieces = -(-lats // LANE)
    return pl.pallas_call(
        functools.partial(spectra_kernel, plan, 1.0 / math.sqrt(nlon)),
        in_specs=[spot_in(pltpu.SMEM)] * 2 + [spot_in(pltpu.HBM)] * 4,
        out_specs=[spot_in(pltpu.VMEM)] * 2,
        out_shape=[pltpu.VMEM(plan.shape, BF16), jax.ShapeDtypeStruct((1, plan.kcoef), F32)],
        scratch_shapes=[
            pltpu.VMEM(order.shape, jnp.int32),
            pltpu.VMEM((entries + SUB, LANE), jnp.int32),
            pltpu.VMEM((plan.kcoef // LANE, LANE), jnp.int32),
            pltpu.SMEM((plan.kcoef // LANE, LANE), jnp.int32),
            pltpu.VMEM((nlon * SUB, LANE), F32),
            pltpu.VMEM(fields.shape, BF16),
            pltpu.VMEM(basis.shape, BF16),
            pltpu.VMEM((lats, plan.kcoef), BF16),
            pltpu.VMEM((times * pieces * LANE, nlon // 2), BF16),
            pltpu.VMEM((times * pieces * LANE, nlon // 2), BF16),
            pltpu.VMEM((GATHER * SUB, LANE), F32),
            pltpu.VMEM((GATHER * SUB, LANE), F32),
            pltpu.VMEM((times, plan.kcoef), F32),
            pltpu.VMEM(plan.slab, F32),
            pltpu.SemaphoreType.DMA(()),
            pltpu.SemaphoreType.DMA(()),
            pltpu.SemaphoreType.DMA(()),
            pltpu.SemaphoreType.DMA(()),
            pltpu.SemaphoreType.DMA((plan.parts // GROUP,)),
        ],
        compiler_params=pltpu.CompilerParams(vmem_limit_bytes=SPECTRA_VMEM),
        cost_estimate=pl.CostEstimate(flops=12 << 30, bytes_accessed=8 << 20, transcendentals=0),
        name="spectra_and_contract",
    )(start, ridge, in_hbm(order), in_hbm(fields), in_hbm(basis), in_hbm(legendre))


def split(value, pieces):
    out = []
    for _ in range(pieces):
        piece = value.astype(BF16)
        out.append(piece)
        value = value - piece.astype(F32)
    return out


def panel_kernel(plan, got_ref, lam_ref, w_ref, diag_ref, inverse_ref, slabs_ref, q_ref, g_ref, y_ref, x_ref, z_ref):
    nt = w_ref.shape[0]
    lanes = PANEL + LANE
    plan.gather_sums(got_ref, slabs_ref)
    coef = jnp.concatenate(
        [plan.tile(slabs_ref, plan.first_panel + n) for n in range(plan.panel_tiles)], axis=1
    )
    lam = lam_ref[...]
    scaled = coef / lam
    starts, total = [], 0
    for r in range(nt):
        low = r // 8 * 8
        z_ref[total : total + nt - low, :] = coef[low:, :] * scaled[r : r + 1, :]
        starts.append(total)
        total += nt - low
    ids = lax.broadcasted_iota(jnp.int32, (PANEL, PANEL), 0)
    upto = lax.broadcasted_iota(jnp.int32, (PANEL, PANEL), 1)
    tri = jnp.where(ids < upto, 1.0, 0.0).astype(BF16)
    prefix = 0.0
    for piece in split(z_ref[...], 3)[::-1]:
        prefix = prefix + jnp.dot(piece, tri, preferred_element_type=F32)
    q_ref[:, :PANEL] = prefix
    q_ref[:, PANEL:] = jnp.broadcast_to(prefix[:, PANEL - 1 :] + z_ref[:, PANEL - 1 :], (total, LANE))
    y_ref[:, :PANEL] = coef
    eye = lax.broadcasted_iota(jnp.int32, (nt, LANE), 0) == lax.broadcasted_iota(jnp.int32, (nt, LANE), 1)
    y_ref[:, PANEL:] = jnp.where(eye, 1.0, 0.0)
    inverses = []
    for r in range(nt):
        low = r // 8 * 8
        place = low + lax.broadcasted_iota(jnp.int32, (nt - low, lanes), 0)
        row = q_ref[starts[r] : starts[r] + nt - low, :] + jnp.where(place == r, float(nt), 0.0)
        for p in range(r):
            base = starts[p] + low - p // 8 * 8
            factor = g_ref[starts[p] + r - p // 8 * 8 : starts[p] + r - p // 8 * 8 + 1, :]
            row = row - factor * q_ref[base : base + nt - low, :]
        q_ref[starts[r] : starts[r] + nt - low, :] = row
        inv = 1.0 / row[r - low : r - low + 1, :]
        inverses.append(inv)
        ratio = jnp.where(place > r, row * inv, 0.0)
        g_ref[starts[r] : starts[r] + nt - low, :] = ratio
        y_ref[low:, :] = y_ref[low:, :] - ratio * y_ref[r : r + 1, :]
    x_ref[...] = jnp.zeros_like(x_ref)
    for r in range(nt - 1, -1, -1):
        low = r // 8 * 8
        ratio = g_ref[starts[r] : starts[r] + nt - low, :]
        tail = jnp.sum(ratio * x_ref[low:, :], axis=0, keepdims=True)
        x_ref[r : r + 1, :] = y_ref[r : r + 1, :] * inverses[r] - tail
    solved = x_ref[:, :PANEL]
    pivot = jnp.sqrt(lam + jnp.sum(coef * solved, axis=0, keepdims=True))
    w_ref[...] = solved / pivot
    diag_ref[...] = lam / pivot
    inverse_ref[...] = x_ref[:, PANEL:]


def panel_small(plan, got, lam):
    nt = plan.times * plan.tm_count
    rows = sum(nt - r // 8 * 8 for r in range(nt))
    lanes = PANEL + LANE
    return pl.pallas_call(
        functools.partial(panel_kernel, plan),
        grid=(1,),
        in_specs=[
            pl.BlockSpec(plan.shape, lambda i: (0, 0, 0)),
            pl.BlockSpec((1, PANEL), lambda i: (0, 0)),
        ],
        out_specs=[
            pl.BlockSpec((nt, PANEL), lambda i: (0, 0)),
            pl.BlockSpec((1, PANEL), lambda i: (0, 0)),
            pl.BlockSpec((nt, LANE), lambda i: (0, 0)),
        ],
        out_shape=[
            jax.ShapeDtypeStruct((nt, PANEL), F32),
            jax.ShapeDtypeStruct((1, PANEL), F32),
            jax.ShapeDtypeStruct((nt, LANE), F32),
        ],
        scratch_shapes=[
            pltpu.VMEM(plan.sums_shape, F32),
            pltpu.VMEM((rows, lanes), F32),
            pltpu.VMEM((rows, lanes), F32),
            pltpu.VMEM((nt, lanes), F32),
            pltpu.VMEM((nt, lanes), F32),
            pltpu.VMEM((rows, PANEL), F32),
        ],
        compiler_params=pltpu.CompilerParams(vmem_limit_bytes=SMALL_VMEM),
        cost_estimate=pl.CostEstimate(flops=4 << 30, bytes_accessed=1 << 18, transcendentals=0),
        name="panel_small",
    )(got, lam)


def panel_large(plan, got, lam):
    low = plan.first_panel * LANE
    coef, lam = plan.unpack(got)[:, low : low + PANEL], lam[:, :PANEL]
    nt = coef.shape[0]
    gram = jnp.dot(coef.T, coef, precision=lax.Precision.HIGHEST) / nt + jnp.diag(lam[0])
    factor = jnp.linalg.cholesky(gram)
    solved = jax.scipy.linalg.solve_triangular(factor, coef.T, lower=True)
    w = solved.T / nt
    rest = jnp.eye(nt, dtype=F32) / nt - jnp.dot(w, w.T, precision=lax.Precision.HIGHEST)
    pivot = jnp.diagonal(factor)[None, :]
    pad = -(-nt // LANE) * LANE - nt
    return w, pivot - jnp.sum(coef * w, axis=0, keepdims=True), jnp.pad(rest, ((0, 0), (0, pad)))


def stack_left(value):
    high, low = (piece.astype(F32) for piece in split(value, 2))
    return jnp.concatenate([high, high, low], axis=0).astype(BF16)


def stack_right(value):
    high, low = (piece.astype(F32) for piece in split(value, 2))
    return jnp.concatenate([high, low, high], axis=0).astype(BF16)


def contract_times(left, right):
    return lax.dot_general(left, right, (((0,), (0,)), ((), ())), preferred_element_type=F32)


def times_first(value):
    return value.astype(F32).T.astype(BF16)


def tile_kernel(plan, own_ref, other_ref, w_ref, diag_ref, lam_ref, inverse_ref, out_ref,
                own_slabs, other_slabs, rows_ref, cols_ref, left_ref, left_main_ref, right_ref, tiles_ref, out_sem):
    height = out_ref.shape[0]
    nt = rows_ref.shape[0]
    tm_index = lax.axis_index("tm")
    row_start = tm_index * height
    first_col = lax.axis_index("lat") * cols_ref.shape[1]
    in_panel_rows = row_start < PANEL

    for got_ref, slabs_ref, core in (
        (own_ref, own_slabs, lax.rem(tm_index, 2)),
        (other_ref, other_slabs, 1 - lax.rem(tm_index, 2)),
    ):
        plan.gather_sums(got_ref, slabs_ref)
        for n in range(plan.col_tiles):
            low = pl.multiple_of(core * plan.half + n * LANE, LANE)
            cols_ref[:, pl.ds(low, LANE)] = plan.tile(slabs_ref, n)
    for n in range(plan.row_tiles):
        rows_ref[:, n * LANE : (n + 1) * LANE] = plan.tile(own_slabs, plan.col_tiles + n)
    left_ref[...] = times_first(stack_left(rows_ref[...]))

    @pl.when(in_panel_rows)
    def _():
        low = pl.multiple_of(jnp.minimum(row_start, PANEL - height), LANE)
        left_main_ref[...] = times_first(stack_left(w_ref[:, pl.ds(low, height)]))
        right_ref[...] = stack_right(cols_ref[...])

    @pl.when(jnp.logical_not(in_panel_rows))
    def _():
        left_main_ref[...] = left_ref[...]
        turned = contract_times(stack_left(inverse_ref[:, :nt]), stack_right(cols_ref[...]))
        right_ref[...] = stack_right(turned)

    @pl.when(first_col < PANEL)
    def _():
        right_ref[:, :PANEL] = stack_right(w_ref[...])

    def copy(step):
        own = pl.ds(pl.multiple_of(step * WIDE, WIDE), WIDE)
        return pltpu.make_async_copy(tiles_ref.at[step], out_ref.at[:, own], out_sem.at[step])

    @pl.loop(0, cols_ref.shape[1] // WIDE)
    def _(step):
        col_start = first_col + step * WIDE
        in_panel_cols = col_start < PANEL
        on_diagonal = (row_start < col_start + WIDE) & (col_start < row_start + height)
        own = pl.ds(pl.multiple_of(step * WIDE, WIDE), WIDE)
        out = tiles_ref.at[step]

        def ids():
            rows = row_start + lax.broadcasted_iota(jnp.int32, (height, WIDE), 0)
            return rows, col_start + lax.broadcasted_iota(jnp.int32, (height, WIDE), 1)

        @pl.when(in_panel_cols)
        def _():
            out[...] = jnp.dot(left_ref[...], right_ref[:, own], preferred_element_type=F32)

        @pl.when(jnp.logical_not(in_panel_cols))
        def _():
            out[...] = jnp.dot(left_main_ref[...], right_ref[:, own], preferred_element_type=F32)

        @pl.when(in_panel_cols & in_panel_rows)
        def _():
            row_ids, col_ids = ids()
            diag = jnp.where(row_ids == col_ids, diag_ref[:, own_panel(step)], 0.0)
            out[...] = jnp.where(row_ids >= col_ids, out[...], 0.0) + diag

        @pl.when(on_diagonal & jnp.logical_not(in_panel_rows))
        def _():
            row_ids, col_ids = ids()
            lam = lam_ref[:, pl.ds(pl.multiple_of(col_start, LANE), WIDE)]
            out[...] += jnp.where(row_ids == col_ids, lam, 0.0)

        copy(step).start()

    @pl.loop(0, cols_ref.shape[1] // WIDE)
    def _(step):
        copy(step).wait()


def own_panel(step):
    return pl.ds(pl.multiple_of(jnp.minimum(step * WIDE, PANEL - WIDE), WIDE), WIDE)


def out_tile(plan, own, other, w, diag, lam, inverse):
    nt, height, width = plan.times * plan.tm_count, plan.rows_width, plan.part_width
    return pl.pallas_call(
        functools.partial(tile_kernel, plan),
        in_specs=[spot_in(pltpu.VMEM)] * 6,
        out_specs=spot_in(pltpu.HBM),
        out_shape=jax.ShapeDtypeStruct((height, width), F32),
        scratch_shapes=[
            pltpu.VMEM(plan.sums_shape, F32),
            pltpu.VMEM(plan.sums_shape, F32),
            pltpu.VMEM((nt, height), F32),
            pltpu.VMEM((nt, width), F32),
            pltpu.VMEM((height, 3 * nt), BF16),
            pltpu.VMEM((height, 3 * nt), BF16),
            pltpu.VMEM((3 * nt, width), BF16),
            pltpu.VMEM((width // WIDE, height, WIDE), F32),
            pltpu.SemaphoreType.DMA((width // WIDE,)),
        ],
        compiler_params=pltpu.CompilerParams(vmem_limit_bytes=SMALL_VMEM),
        cost_estimate=pl.CostEstimate(
            flops=4 * nt * height * width, bytes_accessed=4 * height * width, transcendentals=0
        ),
        name="out_tile",
    )(own, other, w, diag, lam, inverse)


def on_device(basis, fields, legendre, order_table, window_start, ridge):
    times = fields.shape[0]
    kcoef = legendre.shape[1]
    tm_count, lat_count = lax.axis_size("tm"), lax.axis_size("lat")
    plan = Plan(kcoef, tm_count, lat_count, times)
    sent, lam = spectra_and_contract(plan, window_start, ridge, order_table, fields, basis, legendre)
    own = lax.all_to_all(sent, ("tm", "lat"), 0, 0, tiled=True)
    other = lax.ppermute(own, "tm", [(i, i ^ 1) for i in range(tm_count)])
    small = times * tm_count <= LANE // 4
    w, diag, inverse = (panel_small if small else panel_large)(plan, own, lam)
    return out_tile(plan, own, other, w, diag, lam, inverse)


def solution(mesh):
    def run(fields, legendre, order_table, window_start, ridge):
        basis = jnp.asarray(basis_table(fields.shape[2]))
        placed = (P(), P("tm", "lat", None), P("lat", None), P(), P(), P())
        body = jax.shard_map(on_device, mesh=mesh, in_specs=placed, out_specs=P("tm", "lat"), check_vma=False)
        return body(basis, fields, legendre, order_table, window_start, ridge)

    return run
```

```python
import functools
import math

import jax
import jax.numpy as jnp
import ml_dtypes
import numpy as np
from jax import lax
from jax.experimental import pallas as pl
from jax.experimental.pallas import tpu as pltpu
from jax.sharding import PartitionSpec as P

LMAX = 720
PANEL = 512
LANE = 128
SUB = 8
GATHER = 256
GROUP = 4
WIDE = 512
SPECTRA_VMEM = 36 * 1024 * 1024
SMALL_VMEM = 20 * 1024 * 1024
F32 = jnp.float32
BF16 = jnp.bfloat16


def basis_table(nlon):
    half = nlon // 2
    order = np.concatenate([np.arange(0, half, 2), np.arange(0, half, 2), np.arange(1, half, 2), np.arange(1, half, 2)])
    sine = np.repeat([False, True, False, True], [half // 2] * 4)[:, None]
    longitude = np.arange(half, dtype=np.int64)[None, :]
    phase = (order[:, None] * longitude % nlon).astype(np.float32) * np.float32(2.0 * math.pi / nlon)
    return np.where(sine, np.sin(phase), np.cos(phase)).astype(ml_dtypes.bfloat16)


def basis_row(order, part, nlon):
    return nlon // 2 * (order & 1) + nlon // 4 * part + (order >> 1)


def pick_rows(column_ref, start, table_ref, picked_ref):
    row = start // LANE
    for j in range(GATHER):
        group = pl.multiple_of(column_ref[row + j // LANE, j % LANE], SUB)
        picked_ref[SUB * j : SUB * (j + 1), :] = table_ref[pl.ds(group, SUB), :]


def latitude_sums(picked_ref, weights, times):
    lats = weights.shape[0]
    pieces = -(-lats // LANE)
    picked = [picked_ref[pl.ds(s, GATHER, stride=SUB), :] for s in range(times * pieces)]
    value = jnp.concatenate(
        [jnp.concatenate(picked[pieces * t : pieces * (t + 1)], axis=1) for t in range(times)], axis=0
    )
    spare = jnp.zeros((pieces * LANE - lats, GATHER), BF16)
    every = jnp.dot(value.astype(BF16), jnp.concatenate([weights, spare], axis=0), preferred_element_type=F32)
    shape = (LANE, LANE)
    eye = lax.broadcasted_iota(jnp.int32, shape, 0) == lax.broadcasted_iota(jnp.int32, shape, 1)
    sums = []
    for t in range(times):
        own = []
        for low in range(0, GATHER, LANE):
            square = every[t * GATHER + low : t * GATHER + low + LANE, low : low + LANE]
            own.append(jnp.sum(jnp.where(eye, square, 0.0), axis=0, keepdims=True))
        sums.append(jnp.concatenate(own, axis=1))
    return jnp.concatenate(sums, axis=0)


def contract(plan, column_ref, table_ref, weights_ref, sums_ref, even_ref, odd_ref, weights_copy):
    picked = [even_ref, odd_ref]

    def place(part):
        return jnp.minimum(part, plan.parts - 1) * GATHER

    pick_rows(column_ref, 0, table_ref, even_ref)

    @pl.loop(0, plan.parts // GROUP)
    def _(group):
        weights_copy(group).wait()
        for n in range(GROUP):
            part = group * GROUP + n
            pick_rows(column_ref, place(part + 1), table_ref, picked[(n + 1) % 2])
            at = pl.ds(pl.multiple_of(part * GATHER, GATHER), GATHER)
            sums_ref[:, at] = latitude_sums(picked[n % 2], weights_ref[:, at], plan.times)


class Plan:
    def __init__(self, kcoef, tm_count, lat_count, times):
        self.tm_count, self.lat_count, self.times = tm_count, lat_count, times
        self.kcoef, self.part_width, self.rows_width = kcoef, kcoef // lat_count, kcoef // tm_count
        self.parts = kcoef // GATHER
        self.half = self.part_width // 2
        self.col_tiles, self.row_tiles, self.panel_tiles = self.half // LANE, self.rows_width // LANE, PANEL // LANE
        self.first_panel = self.col_tiles + self.row_tiles
        self.across = -(-(self.first_panel + self.panel_tiles) // SUB)
        self.slab = (times * SUB, self.across * LANE)
        self.shape = (tm_count * lat_count,) + self.slab
        self.sums_shape = (self.across, tm_count * self.slab[0], LANE)

    def weights_copies(self, legendre_ref, weights_ref, sems):
        width = GROUP * GATHER

        def copy(group):
            own = pl.ds(pl.multiple_of(group * width, width), width)
            return pltpu.make_async_copy(legendre_ref.at[:, own], weights_ref.at[:, own], sems.at[group])

        @pl.loop(0, self.parts // GROUP)
        def _(group):
            copy(group).start()

        return copy

    def spot(self, tile, time):
        low = tile % self.across * LANE
        return time * SUB + tile // self.across, slice(low, low + LANE)

    def pack(self, sums_ref, slab_ref, sent_ref):
        def fill(tile, source, count):
            for n in range(count):
                for t in range(self.times):
                    row, lanes = self.spot(tile + n, t)
                    low = source + n * LANE
                    slab_ref[row : row + 1, lanes] = sums_ref[t : t + 1, low : low + LANE]

        if self.first_panel + self.panel_tiles < self.across * SUB:
            slab_ref[...] = jnp.zeros_like(slab_ref)
        fill(self.first_panel, 0, self.panel_tiles)
        for part in range(self.lat_count):
            for core in range(2):
                fill(0, part * self.part_width + core * self.half, self.col_tiles)
                for owner in range(core, self.tm_count, 2):
                    fill(self.col_tiles, owner * self.rows_width, self.row_tiles)
                    sent_ref[owner * self.lat_count + part] = slab_ref[...].astype(BF16)

    def gather_sums(self, got_ref, slabs_ref):
        rows = self.slab[0]
        for sender in range(self.tm_count):
            first = sender * self.lat_count
            total = got_ref[first].astype(F32)
            for part in range(1, self.lat_count):
                total = total + got_ref[first + part].astype(F32)
            for n in range(self.across):
                slabs_ref[n, sender * rows : (sender + 1) * rows, :] = total[:, n * LANE : (n + 1) * LANE]

    def tile(self, slabs_ref, tile):
        pieces = []
        for t in range(self.times):
            row = t * SUB + tile // self.across
            pieces.append(slabs_ref[tile % self.across, pl.ds(row, self.tm_count, stride=self.slab[0]), :])
        return jnp.concatenate(pieces, axis=0)

    def unpack(self, got):
        split_shape = (self.tm_count, self.lat_count, self.times, SUB * self.across * LANE)
        total = got.astype(F32).reshape(split_shape).sum(axis=1)
        return total.transpose(1, 0, 2).reshape(self.times * self.tm_count, -1)


def window_of(value, start, length, lines_ref):
    for n in range(value.shape[1] // LANE):
        lines_ref[n : n + 1, :] = value[:, n * LANE : (n + 1) * LANE]
    over = lax.rem(start, LANE)
    lines_ref[...] = pltpu.roll(lines_ref[...], lax.rem(LANE - over, LANE), 1)
    first = lines_ref[pl.ds(start // LANE, length // LANE), :]
    second = lines_ref[pl.ds(start // LANE + 1, length // LANE), :]
    lane = lax.broadcasted_iota(jnp.int32, first.shape, 1)
    return jnp.where(lane < LANE - over, first, second)


def spectra_kernel(plan, scale, start_ref, ridge_ref, order_ref, fields_ref, basis_ref, legendre_ref, sent_ref,
                   lam_ref, order_buf, index_ref, window_ref, column_ref, table_ref, fields_buf, basis_buf,
                   weights_ref, even_lines, odd_lines, even_ref, odd_ref, sums_ref, slab_ref, order_sem,
                   column_sem, fields_sem, basis_sem, weights_sem):
    times, lats, nlon = fields_ref.shape
    pieces = -(-lats // LANE)
    order_copy = pltpu.make_async_copy(order_ref, order_buf, order_sem)
    order_copy.start()
    fields_copy = pltpu.make_async_copy(fields_ref, fields_buf, fields_sem)
    fields_copy.start()
    basis_copy = pltpu.make_async_copy(basis_ref, basis_buf, basis_sem)
    basis_copy.start()
    for t in range(times):
        end = pieces * LANE * (t + 1)
        for folded in (even_lines, odd_lines):
            folded[end - LANE : end, :] = jnp.zeros((LANE, nlon // 2), BF16)
    order_copy.wait()
    start = start_ref[0]
    column = SUB * basis_row(order_buf[1:2, :], order_buf[2:3, :], nlon)
    window_ref[...] = window_of(column, start, plan.kcoef, index_ref)
    column_copy = pltpu.make_async_copy(window_ref, column_ref, column_sem)
    column_copy.start()
    degree = window_of(order_buf[0:1, :], start, plan.kcoef, index_ref)
    lam = ridge_ref[0] * (1.0 + (degree * (degree + 1)).astype(F32) / float(LMAX * (LMAX + 1)))
    for n in range(plan.kcoef // LANE):
        lam_ref[:, n * LANE : (n + 1) * LANE] = lam[n : n + 1, :]
    fields_copy.wait()
    for t in range(times):
        first = fields_buf[t, :, : nlon // 2].astype(F32)
        second = fields_buf[t, :, nlon // 2 :].astype(F32)
        own = slice(pieces * LANE * t, pieces * LANE * t + lats)
        even_lines[own, :] = (first + second).astype(BF16)
        odd_lines[own, :] = (first - second).astype(BF16)
    basis_copy.wait()
    weights_copy = plan.weights_copies(legendre_ref, weights_ref, weights_sem)
    tiles = times * pieces
    wide = 2 if tiles % 2 == 0 else 1
    for parity, folded in enumerate((even_lines, odd_lines)):
        half = slice(nlon // 2 * parity, nlon // 2 * (parity + 1))
        for low in range(0, tiles, wide):
            spectra = scale * lax.dot_general(
                basis_buf[half, :], folded[LANE * low : LANE * (low + wide), :], (((1,), (1,)), ((), ())),
                preferred_element_type=F32,
            )
            for s in range(wide):
                at = pl.ds(SUB * half.start + low + s, nlon // 2, stride=SUB)
                table_ref[at, :] = spectra[:, LANE * s : LANE * (s + 1)]
    column_copy.wait()
    contract(plan, column_ref, table_ref, weights_ref, sums_ref, even_ref, odd_ref, weights_copy)
    plan.pack(sums_ref, slab_ref, sent_ref)


def in_hbm(value):
    return pltpu.with_memory_space_constraint(value, pltpu.HBM)


def spot_in(space):
    return pl.BlockSpec(memory_space=space)


def spectra_and_contract(plan, start, ridge, order, fields, basis, legendre):
    times, lats, nlon = fields.shape
    entries = order.shape[1] // LANE
    pieces = -(-lats // LANE)
    return pl.pallas_call(
        functools.partial(spectra_kernel, plan, 1.0 / math.sqrt(nlon)),
        in_specs=[spot_in(pltpu.SMEM)] * 2 + [spot_in(pltpu.HBM)] * 4,
        out_specs=[spot_in(pltpu.VMEM)] * 2,
        out_shape=[pltpu.VMEM(plan.shape, BF16), jax.ShapeDtypeStruct((1, plan.kcoef), F32)],
        scratch_shapes=[
            pltpu.VMEM(order.shape, jnp.int32),
            pltpu.VMEM((entries + SUB, LANE), jnp.int32),
            pltpu.VMEM((plan.kcoef // LANE, LANE), jnp.int32),
            pltpu.SMEM((plan.kcoef // LANE, LANE), jnp.int32),
            pltpu.VMEM((nlon * SUB, LANE), F32),
            pltpu.VMEM(fields.shape, BF16),
            pltpu.VMEM(basis.shape, BF16),
            pltpu.VMEM((lats, plan.kcoef), BF16),
            pltpu.VMEM((times * pieces * LANE, nlon // 2), BF16),
            pltpu.VMEM((times * pieces * LANE, nlon // 2), BF16),
            pltpu.VMEM((GATHER * SUB, LANE), F32),
            pltpu.VMEM((GATHER * SUB, LANE), F32),
            pltpu.VMEM((times, plan.kcoef), F32),
            pltpu.VMEM(plan.slab, F32),
            pltpu.SemaphoreType.DMA(()),
            pltpu.SemaphoreType.DMA(()),
            pltpu.SemaphoreType.DMA(()),
            pltpu.SemaphoreType.DMA(()),
            pltpu.SemaphoreType.DMA((plan.parts // GROUP,)),
        ],
        compiler_params=pltpu.CompilerParams(vmem_limit_bytes=SPECTRA_VMEM),
        cost_estimate=pl.CostEstimate(flops=12 << 30, bytes_accessed=8 << 20, transcendentals=0),
        name="spectra_and_contract",
    )(start, ridge, in_hbm(order), in_hbm(fields), in_hbm(basis), in_hbm(legendre))


def split(value, pieces):
    out = []
    for _ in range(pieces):
        piece = value.astype(BF16)
        out.append(piece)
        value = value - piece.astype(F32)
    return out


def panel_kernel(plan, got_ref, lam_ref, w_ref, diag_ref, inverse_ref, slabs_ref, q_ref, g_ref, y_ref, x_ref, z_ref):
    nt = w_ref.shape[0]
    lanes = PANEL + LANE
    plan.gather_sums(got_ref, slabs_ref)
    coef = jnp.concatenate(
        [plan.tile(slabs_ref, plan.first_panel + n) for n in range(plan.panel_tiles)], axis=1
    )
    lam = lam_ref[...]
    scaled = coef / lam
    starts, total = [], 0
    for r in range(nt):
        low = r // 8 * 8
        z_ref[total : total + nt - low, :] = coef[low:, :] * scaled[r : r + 1, :]
        starts.append(total)
        total += nt - low
    ids = lax.broadcasted_iota(jnp.int32, (PANEL, PANEL), 0)
    upto = lax.broadcasted_iota(jnp.int32, (PANEL, PANEL), 1)
    tri = jnp.where(ids < upto, 1.0, 0.0).astype(BF16)
    pieces = jnp.concatenate(split(z_ref[...], 3)[::-1], axis=1)
    prefix = jnp.dot(pieces, jnp.concatenate([tri] * 3, axis=0), preferred_element_type=F32)
    q_ref[:, :PANEL] = prefix
    q_ref[:, PANEL:] = jnp.broadcast_to(prefix[:, PANEL - 1 :] + z_ref[:, PANEL - 1 :], (total, LANE))
    y_ref[:, :PANEL] = coef
    eye = lax.broadcasted_iota(jnp.int32, (nt, LANE), 0) == lax.broadcasted_iota(jnp.int32, (nt, LANE), 1)
    y_ref[:, PANEL:] = jnp.where(eye, 1.0, 0.0)
    inverses = []
    for r in range(nt):
        low = r // 8 * 8
        place = low + lax.broadcasted_iota(jnp.int32, (nt - low, lanes), 0)
        row = q_ref[starts[r] : starts[r] + nt - low, :] + jnp.where(place == r, float(nt), 0.0)
        for p in range(r):
            base = starts[p] + low - p // 8 * 8
            factor = g_ref[starts[p] + r - p // 8 * 8 : starts[p] + r - p // 8 * 8 + 1, :]
            row = row - factor * q_ref[base : base + nt - low, :]
        q_ref[starts[r] : starts[r] + nt - low, :] = row
        inv = 1.0 / row[r - low : r - low + 1, :]
        inverses.append(inv)
        ratio = jnp.where(place > r, row * inv, 0.0)
        g_ref[starts[r] : starts[r] + nt - low, :] = ratio
        y_ref[low:, :] = y_ref[low:, :] - ratio * y_ref[r : r + 1, :]
    x_ref[...] = jnp.zeros_like(x_ref)
    for r in range(nt - 1, -1, -1):
        low = r // 8 * 8
        ratio = g_ref[starts[r] : starts[r] + nt - low, :]
        tail = jnp.sum(ratio * x_ref[low:, :], axis=0, keepdims=True)
        x_ref[r : r + 1, :] = y_ref[r : r + 1, :] * inverses[r] - tail
    solved = x_ref[:, :PANEL]
    pivot = jnp.sqrt(lam + jnp.sum(coef * solved, axis=0, keepdims=True))
    w_ref[...] = solved / pivot
    diag_ref[...] = lam / pivot
    inverse_ref[...] = x_ref[:, PANEL:]


def panel_small(plan, got, lam):
    nt = plan.times * plan.tm_count
    rows = sum(nt - r // 8 * 8 for r in range(nt))
    lanes = PANEL + LANE
    return pl.pallas_call(
        functools.partial(panel_kernel, plan),
        grid=(1,),
        in_specs=[
            pl.BlockSpec(plan.shape, lambda i: (0, 0, 0)),
            pl.BlockSpec((1, PANEL), lambda i: (0, 0)),
        ],
        out_specs=[
            pl.BlockSpec((nt, PANEL), lambda i: (0, 0)),
            pl.BlockSpec((1, PANEL), lambda i: (0, 0)),
            pl.BlockSpec((nt, LANE), lambda i: (0, 0)),
        ],
        out_shape=[
            jax.ShapeDtypeStruct((nt, PANEL), F32),
            jax.ShapeDtypeStruct((1, PANEL), F32),
            jax.ShapeDtypeStruct((nt, LANE), F32),
        ],
        scratch_shapes=[
            pltpu.VMEM(plan.sums_shape, F32),
            pltpu.VMEM((rows, lanes), F32),
            pltpu.VMEM((rows, lanes), F32),
            pltpu.VMEM((nt, lanes), F32),
            pltpu.VMEM((nt, lanes), F32),
            pltpu.VMEM((rows, PANEL), F32),
        ],
        compiler_params=pltpu.CompilerParams(vmem_limit_bytes=SMALL_VMEM),
        cost_estimate=pl.CostEstimate(flops=4 << 30, bytes_accessed=1 << 18, transcendentals=0),
        name="panel_small",
    )(got, lam)


def panel_large(plan, got, lam):
    low = plan.first_panel * LANE
    coef, lam = plan.unpack(got)[:, low : low + PANEL], lam[:, :PANEL]
    nt = coef.shape[0]
    gram = jnp.dot(coef.T, coef, precision=lax.Precision.HIGHEST) / nt + jnp.diag(lam[0])
    factor = jnp.linalg.cholesky(gram)
    solved = jax.scipy.linalg.solve_triangular(factor, coef.T, lower=True)
    w = solved.T / nt
    rest = jnp.eye(nt, dtype=F32) / nt - jnp.dot(w, w.T, precision=lax.Precision.HIGHEST)
    pivot = jnp.diagonal(factor)[None, :]
    pad = -(-nt // LANE) * LANE - nt
    return w, pivot - jnp.sum(coef * w, axis=0, keepdims=True), jnp.pad(rest, ((0, 0), (0, pad)))


def stack_left(value):
    high, low = (piece.astype(F32) for piece in split(value, 2))
    return jnp.concatenate([high, high, low], axis=0).astype(BF16)


def stack_right(value):
    high, low = (piece.astype(F32) for piece in split(value, 2))
    return jnp.concatenate([high, low, high], axis=0).astype(BF16)


def contract_times(left, right):
    return lax.dot_general(left, right, (((0,), (0,)), ((), ())), preferred_element_type=F32)


def times_first(value):
    return value.astype(F32).T.astype(BF16)


def tile_kernel(plan, own_ref, other_ref, w_ref, diag_ref, lam_ref, inverse_ref, out_ref,
                own_slabs, other_slabs, rows_ref, cols_ref, left_ref, left_main_ref, right_ref, tiles_ref, out_sem):
    height = out_ref.shape[0]
    nt = rows_ref.shape[0]
    tm_index = lax.axis_index("tm")
    row_start = tm_index * height
    first_col = lax.axis_index("lat") * cols_ref.shape[1]
    in_panel_rows = row_start < PANEL

    for got_ref, slabs_ref, core in (
        (own_ref, own_slabs, lax.rem(tm_index, 2)),
        (other_ref, other_slabs, 1 - lax.rem(tm_index, 2)),
    ):
        plan.gather_sums(got_ref, slabs_ref)
        for n in range(plan.col_tiles):
            low = pl.multiple_of(core * plan.half + n * LANE, LANE)
            cols_ref[:, pl.ds(low, LANE)] = plan.tile(slabs_ref, n)
    for n in range(plan.row_tiles):
        rows_ref[:, n * LANE : (n + 1) * LANE] = plan.tile(own_slabs, plan.col_tiles + n)
    left_ref[...] = times_first(stack_left(rows_ref[...]))

    @pl.when(in_panel_rows)
    def _():
        low = pl.multiple_of(jnp.minimum(row_start, PANEL - height), LANE)
        left_main_ref[...] = times_first(stack_left(w_ref[:, pl.ds(low, height)]))
        right_ref[...] = stack_right(cols_ref[...])

    @pl.when(jnp.logical_not(in_panel_rows))
    def _():
        left_main_ref[...] = left_ref[...]
        turned = contract_times(stack_left(inverse_ref[:, :nt]), stack_right(cols_ref[...]))
        right_ref[...] = stack_right(turned)

    @pl.when(first_col < PANEL)
    def _():
        right_ref[:, :PANEL] = stack_right(w_ref[...])

    def copy(step):
        own = pl.ds(pl.multiple_of(step * WIDE, WIDE), WIDE)
        return pltpu.make_async_copy(tiles_ref.at[step], out_ref.at[:, own], out_sem.at[step])

    @pl.loop(0, cols_ref.shape[1] // WIDE)
    def _(step):
        col_start = first_col + step * WIDE
        in_panel_cols = col_start < PANEL
        on_diagonal = (row_start < col_start + WIDE) & (col_start < row_start + height)
        own = pl.ds(pl.multiple_of(step * WIDE, WIDE), WIDE)
        out = tiles_ref.at[step]

        def ids():
            rows = row_start + lax.broadcasted_iota(jnp.int32, (height, WIDE), 0)
            return rows, col_start + lax.broadcasted_iota(jnp.int32, (height, WIDE), 1)

        @pl.when(in_panel_cols)
        def _():
            out[...] = jnp.dot(left_ref[...], right_ref[:, own], preferred_element_type=F32)

        @pl.when(jnp.logical_not(in_panel_cols))
        def _():
            out[...] = jnp.dot(left_main_ref[...], right_ref[:, own], preferred_element_type=F32)

        @pl.when(in_panel_cols & in_panel_rows)
        def _():
            row_ids, col_ids = ids()
            diag = jnp.where(row_ids == col_ids, diag_ref[:, own_panel(step)], 0.0)
            out[...] = jnp.where(row_ids >= col_ids, out[...], 0.0) + diag

        @pl.when(on_diagonal & jnp.logical_not(in_panel_rows))
        def _():
            row_ids, col_ids = ids()
            lam = lam_ref[:, pl.ds(pl.multiple_of(col_start, LANE), WIDE)]
            out[...] += jnp.where(row_ids == col_ids, lam, 0.0)

        copy(step).start()

    @pl.loop(0, cols_ref.shape[1] // WIDE)
    def _(step):
        copy(step).wait()


def own_panel(step):
    return pl.ds(pl.multiple_of(jnp.minimum(step * WIDE, PANEL - WIDE), WIDE), WIDE)


def out_tile(plan, own, other, w, diag, lam, inverse):
    nt, height, width = plan.times * plan.tm_count, plan.rows_width, plan.part_width
    return pl.pallas_call(
        functools.partial(tile_kernel, plan),
        in_specs=[spot_in(pltpu.VMEM)] * 6,
        out_specs=spot_in(pltpu.HBM),
        out_shape=jax.ShapeDtypeStruct((height, width), F32),
        scratch_shapes=[
            pltpu.VMEM(plan.sums_shape, F32),
            pltpu.VMEM(plan.sums_shape, F32),
            pltpu.VMEM((nt, height), F32),
            pltpu.VMEM((nt, width), F32),
            pltpu.VMEM((height, 3 * nt), BF16),
            pltpu.VMEM((height, 3 * nt), BF16),
            pltpu.VMEM((3 * nt, width), BF16),
            pltpu.VMEM((width // WIDE, height, WIDE), F32),
            pltpu.SemaphoreType.DMA((width // WIDE,)),
        ],
        compiler_params=pltpu.CompilerParams(vmem_limit_bytes=SMALL_VMEM),
        cost_estimate=pl.CostEstimate(
            flops=4 * nt * height * width, bytes_accessed=4 * height * width, transcendentals=0
        ),
        name="out_tile",
    )(own, other, w, diag, lam, inverse)


def on_device(basis, fields, legendre, order_table, window_start, ridge):
    times = fields.shape[0]
    kcoef = legendre.shape[1]
    tm_count, lat_count = lax.axis_size("tm"), lax.axis_size("lat")
    plan = Plan(kcoef, tm_count, lat_count, times)
    sent, lam = spectra_and_contract(plan, window_start, ridge, order_table, fields, basis, legendre)
    own = lax.all_to_all(sent, ("tm", "lat"), 0, 0, tiled=True)
    other = lax.ppermute(own, "tm", [(i, i ^ 1) for i in range(tm_count)])
    small = times * tm_count <= LANE // 4
    w, diag, inverse = (panel_small if small else panel_large)(plan, own, lam)
    return out_tile(plan, own, other, w, diag, lam, inverse)


def solution(mesh):
    def run(fields, legendre, order_table, window_start, ridge):
        basis = jnp.asarray(basis_table(fields.shape[2]))
        placed = (P(), P("tm", "lat", None), P("lat", None), P(), P(), P())
        body = jax.shard_map(on_device, mesh=mesh, in_specs=placed, out_specs=P("tm", "lat"), check_vma=False)
        return body(basis, fields, legendre, order_table, window_start, ridge)

    return run
```
